32 devices in a mesh: dp: 4 (over x, core), fsdp: 8 (over z, y).
Axes of the slice: x: 2, y: 2, z: 4, core: 2. Of those that a mesh axis runs over, the one named last changes fastest.
Arguments:
- tokens: bfloat16 [16384, 1024], P(('dp', 'fsdp')), may hold values from -6 to 6
- segments: int32 [32, 512], P(('dp', 'fsdp')), may hold values from 0 to 3, never falling along the last dimension, each value on 1 to 256 neighbouring positions
- mixer_gain: bfloat16 [1024], P('fsdp'), may hold values from 0.099609375 to 1.8984375
- in_weight: bfloat16 [1024, 3072], P('fsdp', 'dp'), may hold values from -0.1875 to 0.1875
- conv_kernel: bfloat16 [1024, 3], P('fsdp'), may hold values from -3.5 to 3.5
- out_weight: bfloat16 [1024, 1024], P('fsdp', 'dp'), may hold values from -0.1875 to 0.1875
- ffn_gain: bfloat16 [1024], P('fsdp'), may hold values from 0.099609375 to 1.8984375
- gate_weight: bfloat16 [1024, 4608], P('fsdp', 'dp'), may hold values from -0.1875 to 0.1875
- up_weight: bfloat16 [1024, 4608], P('fsdp', 'dp'), may hold values from -0.1875 to 0.1875
- down_weight: bfloat16 [1024, 4608], P('fsdp', 'dp'), may hold values from -0.09375 to 0.09375
- cotangent: bfloat16 [16384, 1024], P(('dp', 'fsdp')), may hold values from -6 to 6
Outputs:
- output: bfloat16 [16384, 1024], P(('dp', 'fsdp'))
- input_grad: float32 [16384, 1024], P(('dp', 'fsdp'))
- mixer_gain_grad: float32 [1024], P('fsdp')
- in_weight_grad: float32 [1024, 3072], P('fsdp', 'dp')
- conv_kernel_grad: float32 [1024, 3], P('fsdp')
- out_weight_grad: float32 [1024, 1024], P('fsdp', 'dp')
- ffn_gain_grad: float32 [1024], P('fsdp')
- gate_weight_grad: float32 [1024, 4608], P('fsdp', 'dp')
- up_weight_grad: float32 [1024, 4608], P('fsdp', 'dp')
- down_weight_grad: float32 [1024, 4608], P('fsdp', 'dp')
The draws below stay inside these ranges and needn't reach their ends.
Inputs may be any that keep to these rules, and one draw needn't show every extreme that they name: `segments`: in each sequence the document numbers never fall, start at 0, and each document has 1 to 256 tokens, one exactly 256.
All inputs are finite; a program needn't handle non-finite values.
Results may differ from the reference program's by a relative error of at most 0.0091.
Values may be sent and summed in bfloat16 or wider, within the bound.
No kernel may reach another device: no remote copies, remote signals or barrier semaphores. Data moves between devices by JAX's collectives and lax.ppermute only.
A program may use at most 256 MiB of HBM per device.

```python
import math
import jax
import jax.numpy as jnp
import numpy as np
from jax import lax

D = 1024
FF = 4608
TOK_DEV = 512
NSEQ = 32
TOKENS = 16384
DOCS = 4
DOC_MOST = 256


def strengthened(entries, rng, source, target, shards_of, factor):
    owner, partner = [(jnp.arange(entries.shape[dim]) // (entries.shape[dim] // shards_of)).reshape([-1 if axis == dim else 1 for axis in range(entries.ndim)]) for dim in (source, target)]
    chosen = jax.random.permutation(rng, shards_of)[partner]
    strong = (owner == chosen) | (owner == (partner + shards_of // 2) % shards_of)
    return jnp.where(strong, factor * entries, entries)


def steps_of(rng, shape, cuts, least, top_value):
    def one(axis_at, parts):
        heights = jax.random.uniform(jax.random.fold_in(jax.random.fold_in(rng, 6), axis_at), (parts,), jnp.float32, least / len(cuts), top_value / len(cuts))
        return jnp.repeat(jnp.exp(heights), shape[axis_at] // parts).reshape((-1,) + (1,) * (len(shape) - axis_at - 1))

    level = one(*cuts[0])
    for cut in cuts[1:]:
        level = level * one(*cut)
    return level


def profile(count, total, most, slope):
    weights = [(1 << 20) // math.isqrt(standing ** slope) + 1 for standing in range(2, count + 1)]
    surplus, counts = total - most - (count - 1), [1] * (count - 1)
    while surplus > 0:
        movable = [i for i in range(count - 1) if counts[i] < most]
        whole, remaining = sum([weights[i] for i in movable]), surplus
        for i in movable:
            extra = min(most - counts[i], max(1, remaining * weights[i] // whole), surplus)
            counts[i] = counts[i] + extra
            surplus = surplus - extra
    return np.array([most] + counts)


def ragged_sizes(key, amount, total, bound, lean):
    if amount == 2:
        one = jax.random.randint(key, (), max(1, total - bound), min(bound, total - 1) + 1)
        return jnp.stack([one, total - one])
    lengths = jnp.asarray(profile(amount, total, bound, lean), jnp.int32)
    pairs = (amount - 1) // 2
    source_of, receiver = lengths[1:1 + 2 * pairs:2], lengths[2:2 + 2 * pairs:2]
    room = jnp.minimum(source_of - 1, bound - receiver)
    shifted = jax.random.randint(jax.random.fold_in(key, 1), (pairs,), 0, 1 << 20) % (room + 1)
    lengths = lengths.at[1:1 + 2 * pairs:2].set(source_of - shifted).at[2:2 + 2 * pairs:2].set(receiver + shifted)
    return lengths[jax.random.permutation(jax.random.fold_in(key, 2), amount)]


def gaussian(rng, shape, spread, limit, cuts=(), dtype=jnp.bfloat16):
    loudness = steps_of(rng, shape, cuts, -0.22, 0.18) if cuts else 1.0
    values = jax.random.normal(rng, shape, jnp.float32) * spread * loudness
    return jnp.minimum(jnp.maximum(values, -limit), limit).astype(dtype)


def heavy_noise(rng, extent, scale, reach, cuts, heavy, dtype=jnp.bfloat16):
    array = scale * jax.random.normal(rng, extent, jnp.float32)
    if cuts:
        array = array * steps_of(rng, extent, cuts, -0.22, 0.18)
    return jnp.clip(strengthened(array, jax.random.fold_in(rng, 3), *heavy), -reach, reach).astype(dtype)


def setup_inputs(seed: int = 0) -> dict:
    streams_of = jax.random.split(jax.random.key(seed), 12)
    tokens = gaussian(streams_of[0], (TOKENS, D), 1.0, 6.0, ((0, 32),))
    segments = jax.vmap(lambda own: jnp.searchsorted(jnp.cumsum(ragged_sizes(own, DOCS, TOK_DEV, DOC_MOST, 0)), jnp.arange(TOK_DEV), side="right"))(jax.random.split(streams_of[1], NSEQ)).reshape((NSEQ, TOK_DEV)).astype(jnp.int32)
    mixer_gain = jnp.clip(1.0 + 0.18 * jax.random.normal(streams_of[2], (D,), jnp.float32), 0.099609375, 1.8984375).astype(jnp.bfloat16)
    in_weight = gaussian(streams_of[3], (D, 3 * D), D ** -0.5, 0.1875, ((0, 8), (1, 4)))
    conv_kernel = gaussian(streams_of[4], (D, 3), 3 ** -0.5, 3.5, ((0, 8),))
    out_weight = gaussian(streams_of[5], (D, D), D ** -0.5, 0.1875, ((0, 8), (1, 4)))
    ffn_gain = jnp.clip(1.0 + 0.18 * jax.random.normal(streams_of[6], (D,), jnp.float32), 0.099609375, 1.8984375).astype(jnp.bfloat16)
    gate_weight = gaussian(streams_of[7], (D, FF), D ** -0.5, 0.1875, ((0, 8), (1, 4)))
    up_weight = gaussian(streams_of[8], (D, FF), D ** -0.5, 0.1875, ((0, 8), (1, 4)))
    down_weight = gaussian(streams_of[9], (D, FF), FF ** -0.5, 0.09375, ((0, 8), (1, 4)))
    cotangent = heavy_noise(streams_of[10], (TOKENS, D), 1.0, 6.0, ((0, 32),), (0, 1, 32, 2.75))
    return {"tokens": tokens, "segments": segments, "mixer_gain": mixer_gain, "in_weight": in_weight, "conv_kernel": conv_kernel, "out_weight": out_weight, "ffn_gain": ffn_gain, "gate_weight": gate_weight, "up_weight": up_weight, "down_weight": down_weight, "cotangent": cotangent}


@jax.custom_vjp
def low(v):
    return lax.optimization_barrier(v.astype(jnp.bfloat16)).astype(jnp.float32)

@jax.custom_vjp
def low_back(v):
    return v

def low_keep(v):
    return (low(v), None)

def low_pass(kept, grad):
    return (grad,)

def back_keep(v):
    return (v, None)

def back_low(kept, grad):
    return (low(grad),)
low.defvjp(low_keep, low_pass)
low_back.defvjp(back_keep, back_low)
EPSILON = 1e-05

def matmul(left, right):
    return jnp.dot(left, right, precision=lax.Precision.HIGHEST, preferred_element_type=jnp.float32)

def rms_scale(values, gain):
    return values * lax.rsqrt(lax.optimization_barrier(jnp.mean(values * values, axis=-1, keepdims=True)) + EPSILON) * gain

def forward(weights, inputs, seg_ids):
    mixer_gain, in_weight, conv_kernel, out_weight, ffn_gain, gate_weight, up_weight, down_weight = weights
    several = seg_ids.shape[0]
    length = seg_ids.shape[1]
    normed = low(rms_scale(inputs, mixer_gain))
    projected = low_back(matmul(normed, in_weight))
    b_part = projected[:, :D]
    c_part = projected[:, D:2 * D]
    x_part = projected[:, 2 * D:]
    gated = (b_part * x_part).reshape(several, length, D)
    same_one = jnp.concatenate([jnp.zeros((several, 1), jnp.float32), (seg_ids[:, 1:] == seg_ids[:, :-1]).astype(jnp.float32)], axis=1)
    same_two = jnp.concatenate([jnp.zeros((several, 2), jnp.float32), (seg_ids[:, 2:] == seg_ids[:, :-2]).astype(jnp.float32)], axis=1)
    back_one = jnp.concatenate([jnp.zeros((several, 1, D), jnp.float32), gated[:, :-1]], axis=1) * same_one[:, :, None]
    back_two = jnp.concatenate([jnp.zeros((several, 2, D), jnp.float32), gated[:, :-2]], axis=1) * same_two[:, :, None]
    mixed = conv_kernel[:, 0] * gated + conv_kernel[:, 1] * back_one + conv_kernel[:, 2] * back_two
    mixed = mixed.reshape(several * length, D)
    scaled = low(c_part * mixed)
    branch = low_back(matmul(scaled, out_weight.T))
    hidden = inputs + branch
    normed_two = low(rms_scale(hidden, ffn_gain))
    gate_value = low_back(matmul(normed_two, gate_weight))
    up_value = low_back(matmul(normed_two, up_weight))
    activated = low(jax.nn.silu(gate_value) * up_value)
    return hidden + matmul(activated, down_weight.T)

def reference(tokens, segments, mixer_gain, in_weight, conv_kernel, out_weight, ffn_gain, gate_weight, up_weight, down_weight, cotangent):
    weights = (mixer_gain.astype(jnp.float32), in_weight.astype(jnp.float32), conv_kernel.astype(jnp.float32), out_weight.astype(jnp.float32), ffn_gain.astype(jnp.float32), gate_weight.astype(jnp.float32), up_weight.astype(jnp.float32), down_weight.astype(jnp.float32))
    group = min(NSEQ, max(1, 4096 // TOK_DEV))
    blocks = NSEQ // group
    inputs = tokens.astype(jnp.float32).reshape(blocks, group * TOK_DEV, D)
    seg_blocks = segments.reshape(blocks, group, TOK_DEV)
    cot_blocks = cotangent.astype(jnp.float32).reshape(blocks, group * TOK_DEV, D)

    def advance(totals, item):
        block_in, block_seg, block_cot = item
        result, pull = jax.vjp(lambda weights_in, values_in: forward(weights_in, values_in, block_seg), weights, block_in)
        weight_grads, input_grad = pull(block_cot)
        return (jax.tree.map(jnp.add, totals, weight_grads), (result, input_grad))
    starting = jax.tree.map(jnp.zeros_like, weights)
    totals, (results, input_grads) = lax.scan(advance, starting, (inputs, seg_blocks, cot_blocks))
    return (results.reshape(TOKENS, D).astype(jnp.bfloat16), input_grads.reshape(TOKENS, D), totals[0], totals[1], totals[2], totals[3], totals[4], totals[5], totals[6], totals[7])
```

```python
import jax
import jax.numpy as jnp
from jax import lax
from jax.sharding import PartitionSpec as P

EPSILON = 1e-05
LINK = jnp.bfloat16
PAD = 128


def dot_plain(left, right):
    return jnp.dot(left, right, preferred_element_type=jnp.float32)


def dot_rows(left, right):
    return lax.dot_general(
        left, right, (((0,), (0,)), ((), ())), preferred_element_type=jnp.float32
    )


def dot_last(left, right):
    return lax.dot_general(
        left, right, (((1,), (1,)), ((), ())), preferred_element_type=jnp.float32
    )


def norm_back(grad_normed, values, inverse, gain):
    weighted = grad_normed * gain
    return inverse * (
        weighted - values * inverse * inverse * jnp.mean(weighted * values, axis=1, keepdims=True)
    )


def shifted(values, steps):
    return jnp.concatenate(
        [jnp.zeros((steps, values.shape[1]), jnp.float32), values[:-steps]], axis=0
    )


def lifted(values, steps):
    return jnp.concatenate(
        [values[steps:], jnp.zeros((steps, values.shape[1]), jnp.float32)], axis=0
    )


def body(
    tokens,
    segments,
    mixer_gain,
    in_weight,
    conv_kernel,
    out_weight,
    ffn_gain,
    gate_weight,
    up_weight,
    down_weight,
    cotangent,
):
    count, width = tokens.shape
    rows = in_weight.shape[0]
    in_cols, out_cols = in_weight.shape[1], out_weight.shape[1]
    ways = width // rows
    half = ways // 2
    place = lax.axis_index("dp")
    low_bit = lax.rem(lax.axis_index("fsdp"), 2)
    low_is_zero = low_bit == 0
    columns = lax.axis_size("dp")
    strides = [[2 * high + low for high in range(half)] for low in range(2)]

    def swap_row(v):
        return lax.ppermute(v, "fsdp", [(i, i ^ 1) for i in range(ways)])

    def swap_far(v):
        return lax.ppermute(v, "dp", [(i, i ^ 2) for i in range(columns)])

    def swap_core(v):
        return lax.ppermute(v, "dp", [(i, i ^ 1) for i in range(columns)])

    def gather_high(v):
        return lax.all_gather(v, "fsdp", axis=0, tiled=True, axis_index_groups=strides)

    def scatter_high(v):
        return lax.psum_scatter(
            v, "fsdp", scatter_dimension=0, tiled=True, axis_index_groups=strides
        )

    def to_own(v):
        parts = v.reshape(v.shape[0], half, 2, rows)
        near = jnp.where(low_is_zero, parts[:, :, 0], parts[:, :, 1])
        away = jnp.where(low_is_zero, parts[:, :, 1], parts[:, :, 0])
        return jnp.concatenate(
            [near.reshape(v.shape[0], -1), away.reshape(v.shape[0], -1)], axis=1
        )

    def from_own(v):
        near = v[:, : width // 2].reshape(v.shape[0], half, rows)
        away = v[:, width // 2 :].reshape(v.shape[0], half, rows)
        zero = jnp.where(low_is_zero, near, away)
        one = jnp.where(low_is_zero, away, near)
        return jnp.stack([zero, one], axis=2).reshape(v.shape[0], width)

    def rows_to_own(v):
        parts = v.reshape(half, 2, rows, v.shape[1])
        near = jnp.where(low_is_zero, parts[:, 0], parts[:, 1])
        away = jnp.where(low_is_zero, parts[:, 1], parts[:, 0])
        return near.reshape(-1, v.shape[1]), away.reshape(-1, v.shape[1])

    def rows_from_own(near, away):
        near = near.reshape(half, rows, -1)
        away = away.reshape(half, rows, -1)
        zero = jnp.where(low_is_zero, near, away)
        one = jnp.where(low_is_zero, away, near)
        return jnp.stack([zero, one], axis=1).reshape(width, -1)

    small = jnp.concatenate(
        [mixer_gain[:, None], ffn_gain[:, None], conv_kernel, jnp.zeros((rows, PAD - 5), LINK)],
        axis=1,
    )
    in_half, out_half = in_cols // 2, out_cols // 2
    packed = jnp.concatenate(
        [
            in_weight[:, :in_half],
            out_weight[:, :out_half],
            small,
            in_weight[:, in_half:],
            out_weight[:, out_half:],
        ],
        axis=1,
    )
    tall = gather_high(packed)
    cut = in_half + out_half
    first = tall[:, : cut + PAD]
    second = tall[:, cut + PAD :]
    first_row = swap_row(first)
    second_far = swap_far(second)
    first_all = jnp.concatenate([first[:, :cut], first_row[:, :cut]], axis=0)
    small_near, small_away = first[:, cut:], first_row[:, cut:]
    second_all = jnp.concatenate([second, second_far], axis=1)
    first_far = swap_far(first_all)
    second_row = swap_row(second_all)
    chip = jnp.concatenate(
        [
            first_all,
            first_far,
            jnp.concatenate([second_all, second_row], axis=0),
        ],
        axis=1,
    )
    chip_core = swap_core(chip)

    def blocks(v):
        ins = [
            jnp.concatenate(
                [v[:, k * cut : k * cut + in_half], v[:, (2 + k) * cut : (2 + k) * cut + in_half]],
                axis=1,
            )
            for k in range(2)
        ]
        outs = [
            jnp.concatenate(
                [
                    v[:, k * cut + in_half : (k + 1) * cut],
                    v[:, (2 + k) * cut + in_half : (3 + k) * cut],
                ],
                axis=1,
            )
            for k in range(2)
        ]
        return ins, outs

    ins_a, outs_a = blocks(chip)
    ins_b, outs_b = blocks(chip_core)
    in_blocks = [ins_a[0], ins_b[0], ins_a[1], ins_b[1]]
    out_rel = jnp.concatenate([outs_a[0], outs_b[0], outs_a[1], outs_b[1]], axis=1)

    def collect(w):
        near = gather_high(w)
        return jnp.concatenate([near, swap_row(near)], axis=0)

    gate_all = collect(gate_weight)
    up_all = collect(up_weight)
    down_all = collect(down_weight)

    def gather_tokens(v):
        far = swap_far(v)
        return jnp.concatenate([v, swap_core(v), far, swap_core(far)], axis=0)

    def sum_tokens(v):
        parts = v.reshape(4, count, width)
        got = swap_core(jnp.concatenate([parts[1], parts[3]], axis=0).astype(LINK))
        far = parts[2] + got[count:].astype(jnp.float32)
        got_far = swap_far(far.astype(LINK))
        return parts[0] + got[:count].astype(jnp.float32) + got_far.astype(jnp.float32)

    def relative(v, size):
        parts = [
            lax.dynamic_slice_in_dim(v, lax.bitwise_xor(place, r) * size, size, 1)
            for r in range(4)
        ]
        return parts

    inputs = to_own(tokens).astype(jnp.float32)
    cot = to_own(cotangent)
    cot_all = gather_tokens(cot)
    small_full = jnp.concatenate([small_near[:, :2], small_away[:, :2]], axis=0).astype(
        jnp.float32
    )
    gain_one = small_full[:, 0]
    gain_two = small_full[:, 1]
    taps = rows_from_own(small_near[:, 2:5], small_away[:, 2:5]).astype(jnp.float32)
    inverse_one = lax.rsqrt(jnp.mean(inputs * inputs, axis=1, keepdims=True) + EPSILON)
    normed = (inputs * inverse_one * gain_one).astype(jnp.bfloat16)
    projected_rel = jnp.stack([dot_plain(normed, w) for w in in_blocks])
    projected = jnp.concatenate(
        [
            lax.dynamic_index_in_dim(projected_rel, lax.bitwise_xor(place, j), 0, False)
            for j in range(4)
        ],
        axis=1,
    )
    b_part = projected[:, :width]
    c_part = projected[:, width : 2 * width]
    x_part = projected[:, 2 * width :]
    gated = b_part * x_part
    seg_ids = segments[0]
    same_one = jnp.concatenate(
        [jnp.zeros((1,), jnp.float32), (seg_ids[1:] == seg_ids[:-1]).astype(jnp.float32)]
    )[:, None]
    same_two = jnp.concatenate(
        [jnp.zeros((2,), jnp.float32), (seg_ids[2:] == seg_ids[:-2]).astype(jnp.float32)]
    )[:, None]
    back_one = shifted(gated, 1) * same_one
    back_two = shifted(gated, 2) * same_two
    mixed = taps[:, 0] * gated + taps[:, 1] * back_one + taps[:, 2] * back_two
    scaled = (c_part * mixed).astype(jnp.bfloat16)
    scaled_rel = jnp.concatenate(relative(scaled, out_cols), axis=1)
    hidden = inputs + dot_last(scaled_rel, out_rel)

    inverse_two = lax.rsqrt(jnp.mean(hidden * hidden, axis=1, keepdims=True) + EPSILON)
    normed_two = gather_tokens((hidden * inverse_two * gain_two).astype(jnp.bfloat16))
    gate_value = dot_plain(normed_two, gate_all)
    up_value = dot_plain(normed_two, up_all)
    sigmoid_gate = jax.nn.sigmoid(gate_value)
    silu_gate = gate_value * sigmoid_gate
    activated = (silu_gate * up_value).astype(jnp.bfloat16)

    def spread(left, right):
        away = dot_rows(left[:, width // 2 :], right).astype(LINK)
        near = dot_rows(left[:, : width // 2], right)
        total = near + swap_row(away).astype(jnp.float32)
        return scatter_high(total.astype(LINK)).astype(jnp.float32)

    grad_down = spread(cot_all, activated)
    grad_act = dot_plain(cot_all, down_all)
    grad_gate_value = (
        grad_act * up_value * sigmoid_gate * (1.0 + gate_value * (1.0 - sigmoid_gate))
    ).astype(jnp.bfloat16)
    grad_up_value = (grad_act * silu_gate).astype(jnp.bfloat16)
    grad_normed_two = sum_tokens(
        dot_last(grad_gate_value, gate_all) + dot_last(grad_up_value, up_all)
    )
    grad_gate = spread(normed_two, grad_gate_value)
    grad_up = spread(normed_two, grad_up_value)
    result = from_own(hidden + sum_tokens(dot_last(activated, down_all))).astype(jnp.bfloat16)

    grad_gain_two = jnp.sum(grad_normed_two * hidden * inverse_two, axis=0)
    grad_hidden = cot.astype(jnp.float32) + norm_back(
        grad_normed_two, hidden, inverse_two, gain_two
    )
    grad_branch = grad_hidden.astype(jnp.bfloat16)
    grad_outw_rel = dot_rows(grad_branch, scaled_rel)
    grad_scaled_rel = dot_plain(grad_branch, out_rel)
    grad_scaled = jnp.concatenate(relative(grad_scaled_rel, out_cols), axis=1)
    grad_c = grad_scaled * mixed
    grad_mixed = grad_scaled * c_part
    grad_gated = (
        taps[:, 0] * grad_mixed
        + taps[:, 1] * lifted(grad_mixed * same_one, 1)
        + taps[:, 2] * lifted(grad_mixed * same_two, 2)
    )
    grad_taps = jnp.stack(
        [
            jnp.sum(grad_mixed * gated, axis=0),
            jnp.sum(grad_mixed * back_one, axis=0),
            jnp.sum(grad_mixed * back_two, axis=0),
        ],
        axis=1,
    )
    grad_projected = jnp.concatenate(
        [grad_gated * x_part, grad_c, grad_gated * b_part], axis=1
    ).astype(jnp.bfloat16)
    grad_proj_rel = relative(grad_projected, in_cols)
    grad_normed = (
        dot_last(grad_proj_rel[0], in_blocks[0])
        + dot_last(grad_proj_rel[1], in_blocks[1])
        + dot_last(grad_proj_rel[2], in_blocks[2])
        + dot_last(grad_proj_rel[3], in_blocks[3])
    )
    grad_gain_one = jnp.sum(grad_normed * inputs * inverse_one, axis=0)
    grad_inputs = from_own(
        grad_hidden + norm_back(grad_normed, inputs, inverse_one, gain_one)
    )

    grad_in_rel = [dot_rows(normed, g) for g in grad_proj_rel]
    taps_near, taps_away = rows_to_own(grad_taps)
    small_grad = jnp.concatenate(
        [
            grad_gain_one[:, None],
            grad_gain_two[:, None],
            jnp.concatenate([taps_near, taps_away], axis=0),
            jnp.zeros((width, PAD - 5), jnp.float32),
        ],
        axis=1,
    )

    def pack(ins, outs):
        return jnp.concatenate(
            [
                piece
                for lo, hi, lo2, hi2 in ((0, in_half, 0, out_half), (in_half, in_cols, out_half, out_cols))
                for k in range(2)
                for piece in (ins[k][:, lo:hi], outs[k][:, lo2:hi2])
            ],
            axis=1,
        )

    def out_block(r):
        return grad_outw_rel[:, r * out_cols : (r + 1) * out_cols]

    mine = pack([grad_in_rel[0], grad_in_rel[2]], [out_block(0), out_block(2)])
    other = pack([grad_in_rel[1], grad_in_rel[3]], [out_block(1), out_block(3)])
    got = swap_core(jnp.concatenate([other, small_grad], axis=1).astype(LINK)).astype(jnp.float32)
    mine = mine + got[:, : 4 * cut]
    small_sum = small_grad + got[:, 4 * cut :]
    first_own = jnp.concatenate([mine[:, :cut], small_sum], axis=1)
    got_first = swap_far(jnp.concatenate([mine[:, cut : 2 * cut], small_sum], axis=1).astype(LINK))
    first_own = first_own + got_first.astype(jnp.float32)
    got_first = swap_row(first_own[width // 2 :].astype(LINK))
    first_done = first_own[: width // 2] + got_first.astype(jnp.float32)
    got_second = swap_row(mine[width // 2 :, 2 * cut :].astype(LINK))
    second_own = mine[: width // 2, 2 * cut :] + got_second.astype(jnp.float32)
    got_second = swap_far(second_own[:, cut:].astype(LINK))
    second_done = second_own[:, :cut] + got_second.astype(jnp.float32)
    owned = scatter_high(
        jnp.concatenate([first_done, second_done], axis=1).astype(LINK)
    ).astype(jnp.float32)
    grad_in = jnp.concatenate(
        [owned[:, :in_half], owned[:, cut + PAD : cut + PAD + in_half]], axis=1
    )
    grad_outw = jnp.concatenate(
        [owned[:, in_half:cut], owned[:, cut + PAD + in_half :]], axis=1
    )
    return (
        result,
        grad_inputs,
        owned[:, cut],
        grad_in,
        owned[:, cut + 2 : cut + 5],
        grad_outw,
        owned[:, cut + 1],
        grad_gate,
        grad_up,
        grad_down,
    )


def solution(mesh):
    return jax.shard_map(
        body,
        mesh=mesh,
        in_specs=(
            P(("dp", "fsdp"), None),
            P(("dp", "fsdp"), None),
            P("fsdp"),
            P("fsdp", "dp"),
            P("fsdp", None),
            P("fsdp", "dp"),
            P("fsdp"),
            P("fsdp", "dp"),
            P("fsdp", "dp"),
            P("fsdp", "dp"),
            P(("dp", "fsdp"), None),
        ),
        out_specs=(
            P(("dp", "fsdp"), None),
            P(("dp", "fsdp"), None),
            P("fsdp"),
            P("fsdp", "dp"),
            P("fsdp", None),
            P("fsdp", "dp"),
            P("fsdp"),
            P("fsdp", "dp"),
            P("fsdp", "dp"),
            P("fsdp", "dp"),
        ),
        check_vma=False,
    )
```

```python
import functools

import jax
import jax.numpy as jnp
from jax import lax
from jax.experimental import pallas as pl
from jax.experimental.pallas import tpu as pltpu
from jax.sharding import PartitionSpec as P

EPSILON = 1e-05
LINK = jnp.bfloat16
F32 = jnp.float32
PAD = 128
MIB = 1 << 20


def dot_plain(left, right):
    return jnp.dot(left, right, preferred_element_type=F32)


def dot_rows(left, right):
    return lax.dot_general(left, right, (((0,), (0,)), ((), ())), preferred_element_type=F32)


def dot_last(left, right):
    return lax.dot_general(left, right, (((1,), (1,)), ((), ())), preferred_element_type=F32)


def after(v, *others):
    return lax.optimization_barrier((v, *others))[0]


def shape(dims, dtype):
    return jax.ShapeDtypeStruct(dims, dtype)


SCALARS = pl.BlockSpec(memory_space=pltpu.SMEM)
WHOLE = pl.BlockSpec(memory_space=pltpu.VMEM)


def call(kernel, scalars, args, outs, flops=0, limit=40, scratch=(), name=None):
    moved = sum(a.size * a.dtype.itemsize for a in args) + sum(
        o.size * jnp.dtype(o.dtype).itemsize for o in outs
    )
    return pl.pallas_call(
        kernel,
        out_shape=outs,
        in_specs=[SCALARS] + [WHOLE] * len(args),
        out_specs=[WHOLE] * len(outs),
        scratch_shapes=list(scratch),
        compiler_params=pltpu.CompilerParams(vmem_limit_bytes=limit * MIB),
        cost_estimate=pl.CostEstimate(flops=flops, bytes_accessed=moved, transcendentals=0),
        name=name,
    )(scalars, *args)


def pack_kernel(where_ref, in_ref, out_ref, one_ref, two_ref, taps_ref, packed_ref):
    rows = in_ref.shape[0]
    in_half, out_half = in_ref.shape[1] // 2, out_ref.shape[1] // 2
    cut = in_half + out_half
    packed_ref[:, :in_half] = in_ref[:, :in_half]
    packed_ref[:, in_half:cut] = out_ref[:, :out_half]
    packed_ref[:, cut : cut + in_half] = in_ref[:, in_half:]
    packed_ref[:, cut + in_half : 2 * cut] = out_ref[:, out_half:]
    eye = lax.broadcasted_iota(jnp.int32, (rows, rows), 0) == lax.broadcasted_iota(
        jnp.int32, (rows, rows), 1
    )
    lane = lax.broadcasted_iota(jnp.int32, (rows, PAD), 1)
    small = jnp.zeros((rows, PAD), F32)
    for k, ref in enumerate((one_ref, two_ref)):
        column = jnp.sum(jnp.where(eye, ref[...].astype(F32), 0.0), axis=1, keepdims=True)
        small = jnp.where(lane == k, column, small)
    for k in range(3):
        small = jnp.where(lane == 2 + k, taps_ref[:, k : k + 1].astype(F32), small)
    packed_ref[:, 2 * cut :] = small.astype(LINK)


def merge_kernel(where_ref, *refs):
    pieces, (first_ref, second_ref, small_ref) = refs[:-3], refs[-3:]
    rows = pieces[0].shape[0]
    high = where_ref[2]
    cut = first_ref.shape[1]
    for s, piece in enumerate(pieces):
        spot = high - s
        spot = jnp.where(spot < 0, spot + len(pieces), spot)
        at = pl.ds(pl.multiple_of(spot * rows, rows), rows)
        first_ref[at, :] = piece[:, :cut]
        second_ref[at, :] = piece[:, cut : 2 * cut]
        small_ref[at, :] = piece[:, 2 * cut :]


def natural(low, near, away, put, rows, blocks):
    def one(h, carry):
        at = pl.ds(pl.multiple_of(h * rows, rows), rows)
        put(pl.ds(pl.multiple_of((2 * h + low) * rows, rows), rows), at, near)
        put(pl.ds(pl.multiple_of((2 * h + 1 - low) * rows, rows), rows), at, away)
        return carry

    lax.fori_loop(0, blocks, one, 0)


def mixer_weights_kernel(rows, where_ref, *refs):
    pieces, (in_ref, out_ref) = refs[:16], refs[16:18]
    low, place = where_ref[0], where_ref[1]
    in_half, out_half = in_ref.shape[1] // 8, out_ref.shape[1] // 8
    for k in range(8):
        half, r = k // 4, k % 4
        block = lax.bitwise_xor(place, r)
        in_at = pl.ds(pl.multiple_of((2 * block + half) * in_half, PAD), in_half)
        out_at = pl.ds(pl.multiple_of((2 * block + half) * out_half, PAD), out_half)

        def put(to, at, ref):
            in_ref[to, in_at] = ref[at, :in_half]
            out_ref[to, out_at] = ref[at, in_half:]

        natural(low, pieces[2 * k], pieces[2 * k + 1], put, rows, pieces[0].shape[0] // rows)


def back_rows(v, steps):
    return pltpu.roll(v, steps, 0)


def ahead_rows(v, steps):
    return pltpu.roll(v, v.shape[0] - steps, 0)


def small_rows(rows, low, near_ref, away_ref, small_ref):
    def put(to, at, ref):
        small_ref[to, :] = ref[at, :].astype(F32)

    natural(low, near_ref, away_ref, put, rows, near_ref.shape[0] // rows)
    return small_ref[...].T[:8]


def mixer_kernel(
    rows,
    where_ref,
    tokens_ref,
    same_ref,
    near_ref,
    away_ref,
    *refs,
):
    pieces = refs[:16]
    normed_ref, parts_ref, scaled_ref, hidden_ref, next_ref, gains_ref = refs[16:22]
    small_ref, in_ref, outw_ref = refs[22:]
    mixer_weights_kernel(rows, where_ref, *pieces, in_ref, outw_ref)
    width = tokens_ref.shape[1]
    step = 256
    gains_ref[...] = small_rows(rows, where_ref[0], near_ref, away_ref, small_ref)
    inputs = tokens_ref[...].astype(F32)
    inverse = lax.rsqrt(jnp.mean(inputs * inputs, axis=1, keepdims=True) + EPSILON)
    normed_ref[...] = (inputs * inverse * gains_ref[0:1, :]).astype(LINK)

    def chunk(q, carry):
        at = pl.ds(pl.multiple_of(q * step, step), step)

        def part(k):
            w = in_ref[:, pl.ds(pl.multiple_of(k * width + q * step, step), step)]
            v = dot_plain(normed_ref[...], w)
            parts_ref[k, :, at] = v
            return v

        b_part = part(0)
        x_part = part(2)
        gated = b_part * x_part
        mixed = (
            gains_ref[2:3, at] * gated
            + gains_ref[3:4, at] * (back_rows(gated, 1) * same_ref[:, 0:1])
            + gains_ref[4:5, at] * (back_rows(gated, 2) * same_ref[:, 1:2])
        )
        scaled_ref[:, at] = (part(1) * mixed).astype(LINK)
        return carry

    lax.fori_loop(0, width // step, chunk, 0)

    def final(q, total):
        at = pl.ds(pl.multiple_of(q * step, step), step)
        v = tokens_ref[:, at].astype(F32) + dot_last(scaled_ref[...], outw_ref[at, :])
        hidden_ref[:, at] = v
        return total + jnp.sum(v * v, axis=1, keepdims=True)

    total = lax.fori_loop(
        0, width // step, final, jnp.zeros((tokens_ref.shape[0], 1), F32)
    )
    inverse_two = lax.rsqrt(total / width + EPSILON)
    next_ref[...] = (hidden_ref[...] * inverse_two * gains_ref[1:2, :]).astype(LINK)


def mixer_back_kernel(
    where_ref,
    own_ref,
    got_ref,
    got_far_ref,
    hidden_ref,
    cot_ref,
    same_ref,
    gains_ref,
    parts_ref,
    outw_ref,
    hidden_grad_ref,
    branch_ref,
    proj_ref,
    sums_ref,
):
    width = hidden_ref.shape[1]
    step = 256
    hidden = hidden_ref[...]
    inverse = lax.rsqrt(jnp.mean(hidden * hidden, axis=1, keepdims=True) + EPSILON)
    grad = own_ref[...].astype(F32) + got_ref[...].astype(F32) + got_far_ref[...].astype(F32)
    sums_ref[0:1, :] = jnp.zeros((1, width), F32)
    sums_ref[1:2, :] = jnp.sum(grad * (hidden * inverse), axis=0, keepdims=True)
    weighted = grad * gains_ref[1:2, :]
    mean = jnp.mean(weighted * hidden, axis=1, keepdims=True)
    total = cot_ref[...].astype(F32) + inverse * (weighted - hidden * (inverse * inverse * mean))
    hidden_grad_ref[...] = total
    branch_ref[...] = total.astype(LINK)

    def chunk(q, carry):
        at = pl.ds(pl.multiple_of(q * step, step), step)
        grad_scaled = dot_plain(branch_ref[...], outw_ref[:, at])
        b_part, c_part, x_part = (parts_ref[k, :, at] for k in range(3))
        same_one, same_two = same_ref[:, 0:1], same_ref[:, 1:2]
        gated = b_part * x_part
        back_one = back_rows(gated, 1) * same_one
        back_two = back_rows(gated, 2) * same_two
        taps = [gains_ref[2 + k : 3 + k, at] for k in range(3)]
        mixed = taps[0] * gated + taps[1] * back_one + taps[2] * back_two
        grad_mixed = grad_scaled * c_part
        sums_ref[2:3, at] = jnp.sum(grad_mixed * gated, axis=0, keepdims=True)
        sums_ref[3:4, at] = jnp.sum(grad_mixed * back_one, axis=0, keepdims=True)
        sums_ref[4:5, at] = jnp.sum(grad_mixed * back_two, axis=0, keepdims=True)
        grad_gated = (
            taps[0] * grad_mixed
            + taps[1] * ahead_rows(grad_mixed * same_one, 1)
            + taps[2] * ahead_rows(grad_mixed * same_two, 2)
        )
        for k, v in enumerate((grad_gated * x_part, grad_scaled * mixed, grad_gated * b_part)):
            proj_ref[:, pl.ds(pl.multiple_of(k * width + q * step, step), step)] = v.astype(LINK)
        return carry

    lax.fori_loop(0, width // step, chunk, 0)
    sums_ref[5:8, :] = jnp.zeros((3, width), F32)


def mixer_grads_kernel(
    rows, order, where_ref, normed_ref, proj_ref, branch_ref, scaled_ref, *refs
):
    low, place = where_ref[0], where_ref[1]
    total_ref = refs[-1]
    in_half = proj_ref.shape[1] // 8
    out_half = scaled_ref.shape[1] // 8
    for n in range(4):
        i, half = n // 2, n % 2
        block = 2 * lax.bitwise_xor(place, order[i]) + half
        in_at = pl.ds(pl.multiple_of(block * in_half, PAD), in_half)
        out_at = pl.ds(pl.multiple_of(block * out_half, PAD), out_half)
        total_ref[:, :in_half] = dot_rows(normed_ref[...], proj_ref[:, in_at])
        total_ref[:, in_half:] = dot_rows(branch_ref[...], scaled_ref[:, out_at])

        def copy(h, carry, n=n):
            to = pl.ds(pl.multiple_of(h * rows, rows), rows)
            for k, bit in enumerate((low, 1 - low)):
                at = pl.ds(pl.multiple_of((2 * h + bit) * rows, rows), rows)
                refs[2 * n + k][to, :] = total_ref[at, :].astype(LINK)
            return carry

        lax.fori_loop(0, refs[0].shape[0] // rows, copy, 0)


def add_kernel(where_ref, *refs):
    n = len(refs) // 3
    for a, b, c in zip(refs[:n], refs[n : 2 * n], refs[2 * n :]):
        c[...] = (a[...].astype(F32) + b[...].astype(F32)).astype(c.dtype)


def last_kernel(
    rows, where_ref, a_ref, a_got_ref, a_far_ref, a_row_ref, b_ref, b_got_ref, b_row_ref, b_far_ref, small_ref, *refs
):
    low, high = where_ref[0], where_ref[2]
    cut = a_ref.shape[1]
    own_ref, sends, turned_ref = refs[0], refs[1:-1], refs[-1]
    width = turned_ref.shape[0]
    turned_ref[...] = jnp.concatenate(
        [small_ref[...], jnp.zeros((PAD - 8, width), F32)], axis=0
    ).T

    def total(at, *parts):
        v = parts[0][at, :].astype(F32)
        for p in parts[1:]:
            v = v + p[at, :].astype(F32)
        return v

    for s, ref in enumerate((own_ref, *sends)):
        spot = high + s
        spot = jnp.where(spot >= len(sends) + 1, spot - len(sends) - 1, spot)
        at = pl.ds(pl.multiple_of(spot * rows, rows), rows)
        ref[:, :cut] = total(at, a_ref, a_got_ref, a_far_ref, a_row_ref).astype(ref.dtype)
        ref[:, cut : 2 * cut] = total(at, b_ref, b_got_ref, b_row_ref, b_far_ref).astype(ref.dtype)
        at = pl.ds(pl.multiple_of((2 * spot + low) * rows, rows), rows)
        ref[:, 2 * cut :] = turned_ref[at, :].astype(ref.dtype)


def mixer_input_kernel(
    rows,
    where_ref,
    tokens_ref,
    hidden_grad_ref,
    gains_ref,
    sums_ref,
    proj_ref,
    in_ref,
    input_ref,
    small_ref,
    grad_ref,
):
    width = tokens_ref.shape[1]
    step = 256
    inputs = tokens_ref[...].astype(F32)
    inverse = lax.rsqrt(jnp.mean(inputs * inputs, axis=1, keepdims=True) + EPSILON)

    def chunk(q, carry):
        at = pl.ds(pl.multiple_of(q * step, step), step)
        grad_ref[:, at] = dot_last(proj_ref[...], in_ref[at, :])
        return carry

    lax.fori_loop(0, width // step, chunk, 0)
    grad = grad_ref[...]
    row = lax.broadcasted_iota(jnp.int32, (8, width), 0)
    gain_grad = jnp.sum(grad * (inputs * inverse), axis=0, keepdims=True)
    small_ref[...] = jnp.where(row == 0, gain_grad, sums_ref[...])
    weighted = grad * gains_ref[0:1, :]
    mean = jnp.mean(weighted * inputs, axis=1, keepdims=True)
    input_ref[...] = hidden_grad_ref[...] + inverse * (
        weighted - inputs * (inverse * inverse * mean)
    )


TILE = 256


def piece_specs(pieces, count, width):
    tiles = count // TILE
    return [
        pl.BlockSpec(
            (TILE, width), lambda t, k=k: (jnp.clip(t - k * tiles, 0, tiles - 1), 0)
        )
        for k in range(pieces)
    ]


def pick(refs, tiles):
    v = refs[0][...]
    for k in range(1, len(refs)):
        v = jnp.where(pl.program_id(0) >= k * tiles, refs[k][...], v)
    return v


def put_piece(refs, tiles, v):
    for k, ref in enumerate(refs):

        @pl.when((pl.program_id(0) >= k * tiles) & (pl.program_id(0) < (k + 1) * tiles))
        def _(ref=ref):
            ref[...] = v.astype(ref.dtype)


def whole_spec(v):
    return pl.BlockSpec(v.shape, lambda t: (0, 0))


def tiled(kernel, grid, in_specs, args, out_specs, outs, flops, limit=56, scratch=()):
    moved = sum(a.size * a.dtype.itemsize for a in args) + sum(
        o.size * jnp.dtype(o.dtype).itemsize for o in outs
    )
    return pl.pallas_call(
        kernel,
        grid=(grid,),
        in_specs=in_specs,
        out_specs=out_specs,
        out_shape=outs,
        scratch_shapes=list(scratch),
        compiler_params=pltpu.CompilerParams(vmem_limit_bytes=limit * MIB),
        cost_estimate=pl.CostEstimate(flops=flops, bytes_accessed=moved, transcendentals=0),
    )(*args)


def act_kernel(tiles, rows, where_ref, *refs):
    pieces, woven, (act_ref, silu_ref, slope_ref, gate_ref, up_ref) = refs[:4], refs[4:8], refs[8:]

    @pl.when(pl.program_id(0) == 0)
    def _():
        for k, whole_ref in enumerate((gate_ref, up_ref)):

            def put(to, at, ref, whole_ref=whole_ref):
                whole_ref[to, :] = ref[at, :]

            natural(where_ref[0], *woven[2 * k : 2 * k + 2], put, rows, woven[0].shape[0] // rows)

    normed = pick(pieces, tiles)
    gate = dot_plain(normed, gate_ref[...])
    up = dot_plain(normed, up_ref[...])
    sigmoid = 1.0 / (1.0 + jnp.exp(-gate))
    silu = gate * sigmoid
    act_ref[...] = (silu * up).astype(LINK)
    silu_ref[...] = silu.astype(LINK)
    slope_ref[...] = (up * (sigmoid + silu * (1.0 - sigmoid))).astype(LINK)


def act_call(rows, scalars, pieces, woven):
    count, width = pieces[0].shape
    inner = woven[0].shape[1]
    tiles = count // TILE
    wide = pl.BlockSpec((TILE, inner), lambda t: (t, 0))
    weight = shape((width, inner), LINK)
    return tiled(
        functools.partial(act_kernel, tiles, rows),
        4 * tiles,
        [SCALARS] + piece_specs(4, count, width) + [whole_spec(v) for v in woven],
        [scalars, *pieces, *woven],
        [wide] * 3 + [whole_spec(weight)] * 2,
        [shape((4 * count, inner), LINK)] * 3 + [weight] * 2,
        16 * count * width * inner,
    )


def back_kernel(pieces, tiles, with_got, *refs):
    cots, refs = refs[:pieces], refs[pieces:]
    silu_ref, slope_ref, gate_ref, up_ref, down_ref = refs[:5]
    refs = refs[5:]
    if with_got:
        got_ref, refs = refs[0], refs[1:]
    grad_gate_ref, grad_up_ref = refs[:2]
    grad_act = dot_plain(pick(cots, tiles), down_ref[...])
    grad_up_ref[...] = (grad_act * silu_ref[...].astype(F32)).astype(LINK)
    grad_gate_ref[...] = (grad_act * slope_ref[...].astype(F32)).astype(LINK)
    back = dot_last(grad_gate_ref[...], gate_ref[...]) + dot_last(grad_up_ref[...], up_ref[...])
    if with_got:
        back = back + got_ref[...].astype(F32)
    put_piece(refs[2:], tiles, back)


def back_call(start, cots, silu, slope, gate, up, down, got=None):
    count, width = cots[0].shape
    inner = gate.shape[1]
    tiles, pieces = count // TILE, len(cots)
    wide_in = pl.BlockSpec((TILE, inner), lambda t: (t + start * tiles, 0))
    wide = pl.BlockSpec((TILE, inner), lambda t: (t, 0))
    thin = piece_specs(pieces, count, width)
    extra = [] if got is None else [got]
    return tiled(
        functools.partial(back_kernel, pieces, tiles, got is not None),
        pieces * tiles,
        thin + [wide_in] * 2 + [whole_spec(gate)] * 3 + thin[: len(extra)],
        [*cots, silu, slope, gate, up, down, *extra],
        [wide] * 2 + thin,
        [shape((pieces * count, inner), LINK)] * 2 + [shape((count, width), LINK)] * pieces,
        6 * pieces * count * width * inner,
    )


def out_kernel(tiles, act_ref, down_ref, *refs):
    put_piece(refs, tiles, dot_last(act_ref[...], down_ref[...]))


def out_call(act, down, count):
    width, inner = down.shape
    tiles = count // TILE
    return tiled(
        functools.partial(out_kernel, tiles),
        4 * tiles,
        [pl.BlockSpec((TILE, inner), lambda t: (t, 0)), whole_spec(down)],
        [act, down],
        piece_specs(4, count, width),
        [shape((count, width), LINK)] * 4,
        8 * count * width * inner,
    )


def weight_grad_kernel(rows, spots, whole, where_ref, *refs):
    lefts, refs = refs[:4], refs[4:]
    low = where_ref[0]
    count = lefts[0].shape[0]
    at = pl.ds(pl.multiple_of(pl.program_id(0) * TILE, TILE), TILE)
    total = None
    for left, (k, start) in zip(lefts, spots):
        v = dot_rows(left[:, at], refs[k][start * count : (start + 1) * count, :])
        total = v if total is None else total + v
    if whole:
        refs[-1][...] = total.astype(LINK)
        return
    near_ref, away_ref, total_ref = refs[-3:]
    total_ref[...] = total
    for h in range(near_ref.shape[0] // rows):
        to = pl.ds(h * rows, rows)
        for ref, bit in ((near_ref, low), (away_ref, 1 - low)):
            at = pl.ds(pl.multiple_of((2 * h + bit) * rows, rows), rows)
            ref[to, :] = total_ref[at, :].astype(ref.dtype)


def weight_grad(rows, scalars, lefts, rights, spots, whole=False):
    count, width = lefts[0].shape
    inner = rights[0].shape[1]
    half = pl.BlockSpec((TILE // 2, inner), lambda t: (t, 0))
    return tiled(
        functools.partial(weight_grad_kernel, rows, spots, whole),
        width // TILE,
        [SCALARS] + [whole_spec(v) for v in (*lefts, *rights)],
        [scalars, *lefts, *rights],
        [pl.BlockSpec((TILE, inner), lambda t: (t, 0))] if whole else [half, half],
        [shape((width, inner), LINK)]
        if whole
        else [shape((width // 2, inner), F32), shape((width // 2, inner), LINK)],
        8 * count * width * inner,
        scratch=[] if whole else [pltpu.VMEM((TILE, inner), F32)],
    )


def body(
    tokens,
    segments,
    mixer_gain,
    in_weight,
    conv_kernel,
    out_weight,
    ffn_gain,
    gate_weight,
    up_weight,
    down_weight,
    cotangent,
):
    count, width = tokens.shape
    rows = in_weight.shape[0]
    in_cols, out_cols = in_weight.shape[1], out_weight.shape[1]
    cut = (in_cols + out_cols) // 2
    ways = width // rows
    half = ways // 2
    columns = lax.axis_size("dp")
    place = lax.axis_index("dp")
    low = lax.rem(lax.axis_index("fsdp"), 2)
    high = lax.axis_index("fsdp") // 2
    scalars = jnp.stack([low, place, high]).astype(jnp.int32)
    strides = [[2 * h + bit for h in range(half)] for bit in range(2)]

    def swap_row(v):
        return lax.ppermute(v, "fsdp", [(i, i ^ 1) for i in range(ways)])

    def swap_far(v):
        return lax.ppermute(v, "dp", [(i, i ^ 2) for i in range(columns)])

    def swap_core(v):
        return lax.ppermute(v, "dp", [(i, i ^ 1) for i in range(columns)])

    def shift_high(v, s):
        return lax.ppermute(v, "fsdp", [(i, (i + 2 * s) % ways) for i in range(ways)])

    def gather_high(v):
        return lax.all_gather(v, "fsdp", axis=0, tiled=True, axis_index_groups=strides)

    def scatter_high(v):
        return lax.psum_scatter(
            v, "fsdp", scatter_dimension=0, tiled=True, axis_index_groups=strides
        )

    (packed,) = call(
        pack_kernel,
        scalars,
        [in_weight, out_weight, mixer_gain[None, :], ffn_gain[None, :], conv_kernel],
        [shape((rows, 2 * cut + PAD), LINK)],
    )
    shifts = [packed] + [shift_high(packed, s) for s in range(1, half)]
    tall = half * rows
    cot_far = swap_far(after(cotangent, packed))
    down_other = swap_row(after(down_weight, packed))
    down_pair = jnp.where(
        low == 0,
        jnp.concatenate([down_weight, down_other], axis=0),
        jnp.concatenate([down_other, down_weight], axis=0),
    )
    shifts[0] = after(shifts[0], cot_far, down_pair)
    first, second, small_near = call(
        merge_kernel,
        scalars,
        shifts,
        [shape((tall, cut), LINK), shape((tall, cut), LINK), shape((tall, PAD), LINK)],
    )
    gate_near = gather_high(after(gate_weight, first))
    up_near = gather_high(after(up_weight, first))
    down_all = gather_high(after(down_pair, first))
    first_row = swap_row(first)
    second_far = swap_far(second)
    small_away = swap_row(small_near)
    second_row = swap_row(second)
    first_far = swap_far(first)
    second_far_row = swap_row(second_far)
    first_row_far = swap_far(first_row)
    chip = [[[first, first_row], [first_far, first_row_far]], [[second, second_row], [second_far, second_far_row]]]
    pieces = []
    for k in range(2):
        other = [[swap_core(v) for v in pair] for pair in chip[k]]
        for pair in (chip[k][0], other[0], chip[k][1], other[1]):
            pieces += pair
    pieces[0] = after(pieces[0], gate_near, small_away)
    gate_row = swap_row(gate_near)
    up_row = swap_row(up_near)

    def gather_tokens(v, far):
        return [v, swap_core(v), far, swap_core(far)]

    cots = gather_tokens(cotangent, cot_far)

    seg_ids = segments[0]
    zero = jnp.zeros((2,), F32)
    same = jnp.stack(
        [
            jnp.concatenate([zero[:1], (seg_ids[1:] == seg_ids[:-1]).astype(F32)]),
            jnp.concatenate([zero, (seg_ids[2:] == seg_ids[:-2]).astype(F32)]),
        ],
        axis=1,
    )
    normed, parts, scaled, hidden, normed_two, gains = call(
        functools.partial(mixer_kernel, rows),
        scalars,
        [tokens, same, small_near, small_away, *pieces],
        [
            shape((count, width), LINK),
            shape((3, count, width), F32),
            shape((count, width), LINK),
            shape((count, width), F32),
            shape((count, width), LINK),
            shape((8, width), F32),
        ],
        flops=8 * count * width * width,
        scratch=[
            pltpu.VMEM((width, PAD), F32),
            pltpu.VMEM((width, columns * in_cols), LINK),
            pltpu.VMEM((width, columns * out_cols), LINK),
        ],
        limit=56,
    )
    in_all, outw_all = call(
        functools.partial(mixer_weights_kernel, rows),
        scalars,
        [after(pieces[0], normed_two), *pieces[1:]],
        [shape((width, columns * in_cols), LINK), shape((width, columns * out_cols), LINK)],
    )

    normed_two = after(normed_two, up_near, gate_row)
    normeds = gather_tokens(normed_two, swap_far(normed_two))
    act, silu, slope, gate_all, up_all = act_call(
        rows, scalars, [after(normeds[0], outw_all), *normeds[1:]], [gate_near, gate_row, up_near, up_row]
    )

    def add(*pairs):
        return call(
            add_kernel,
            scalars,
            [p[0] for p in pairs] + [p[1] for p in pairs],
            [shape(p[0].shape, LINK) for p in pairs],
        )

    def spread(near, away_got):
        total = near + away_got.astype(F32)
        return scatter_high(total.astype(LINK)).astype(F32)

    weights = (silu, slope, gate_all, up_all, down_all)
    gate_xc, up_xc, back_xc = back_call(3, [cots[3]], *weights)
    down_near, down_away = weight_grad(
        rows,
        scalars,
        [after(cots[0], back_xc), *cots[1:]],
        [act],
        [(0, 0), (0, 1), (0, 2), (0, 3)],
    )
    gate_x, up_x, back_far = back_call(
        2, [after(cots[2], down_away)], *weights, got=swap_core(back_xc)
    )
    gate_o, up_o, back_own, back_c = back_call(
        0, [after(cots[0], back_far), cots[1]], *weights
    )
    down_got = swap_row(down_away)
    back = [back_own, swap_core(back_c), swap_far(back_far)]
    spots = [(0, 0), (0, 1), (1, 0), (2, 0)]
    (up_whole,) = weight_grad(
        rows,
        scalars,
        [after(normeds[0], down_got, back[2]), *normeds[1:]],
        [up_o, up_x, up_xc],
        spots,
        whole=True,
    )
    up_pair = scatter_high(up_whole).reshape(2, rows, -1)
    up_mine = jnp.where(low == 0, up_pair[0], up_pair[1])
    up_other = jnp.where(low == 0, up_pair[1], up_pair[0])
    grad_down = spread(down_near, down_got)
    gate_near_grad, gate_away = weight_grad(
        rows,
        scalars,
        [after(normeds[0], up_whole), *normeds[1:]],
        [gate_o, gate_x, gate_xc],
        spots,
    )
    gate_got = swap_row(gate_away)

    hidden_grad, branch, proj, sums = call(
        mixer_back_kernel,
        scalars,
        [after(back[0], gate_away), *back[1:], hidden, cotangent, same, gains, parts, outw_all],
        [
            shape((count, width), F32),
            shape((count, width), LINK),
            shape((count, 3 * width), LINK),
            shape((8, width), F32),
        ],
        flops=2 * count * width * width,
        limit=48,
    )

    def mixer_grads(order, first_arg):
        return call(
            functools.partial(mixer_grads_kernel, rows, order),
            scalars,
            [first_arg, proj, branch, scaled],
            [shape((tall, cut), LINK)] * 8,
            flops=4 * count * width * width,
            scratch=[pltpu.VMEM((width, cut), F32)],
        )

    send = mixer_grads((1, 3), normed)
    got = [swap_core(v) for v in send]
    mine = mixer_grads((0, 2), after(normed, send[0], gate_got))
    a_away_far, b_away_far, a_near_far, b_away_own = add(
        *((after(mine[k], up_pair), got[k]) for k in (5, 7, 4, 3))
    )
    a_away_got = swap_far(a_away_far)
    b_away_got = swap_row(b_away_far)
    a_near_got = swap_far(a_near_far)
    b_own_got = swap_row(b_away_own)
    input_grad, sums = call(
        functools.partial(mixer_input_kernel, rows),
        scalars,
        [tokens, after(hidden_grad, a_near_far), gains, sums, proj, in_all],
        [shape((count, width), F32), shape((8, width), F32)],
        flops=6 * count * width * width,
        scratch=[pltpu.VMEM((count, width), F32)],
    )
    grad_gate = spread(after(gate_near_grad, mine[0]), gate_got)

    a_away_got = after(a_away_got, input_grad)
    sums_core = sums + swap_core(sums)
    sums_far = sums_core + swap_far(sums_core)
    a_away = (mine[1].astype(F32) + got[1].astype(F32) + a_away_got.astype(F32)).astype(LINK)
    b_far = (mine[6].astype(F32) + got[6].astype(F32) + b_away_got.astype(F32)).astype(LINK)
    a_row_got = swap_row(a_away)
    b_far_got = swap_far(b_far)
    out_own, out_c, out_x, out_xc = out_call(after(act, a_away, b_far), down_all, count)
    (out_far,) = add((after(out_x, a_row_got), swap_core(out_xc)))
    out_got, out_got_far = swap_core(out_c), swap_far(after(out_far, b_far_got, sums_far))
    up_got = swap_row(up_other)
    sums = sums_far + swap_row(sums_far)
    own, *sends = call(
        functools.partial(last_kernel, rows),
        scalars,
        [
            mine[0],
            got[0],
            a_near_got,
            a_row_got,
            mine[2],
            got[2],
            b_own_got,
            b_far_got,
            after(sums, up_got),
        ],
        [shape((rows, 2 * cut + PAD), F32)] + [shape((rows, 2 * cut + PAD), LINK)] * (half - 1),
        scratch=[pltpu.VMEM((width, PAD), F32)],
    )
    owned = own
    for s in range(1, half):
        owned = owned + shift_high(sends[s - 1], s).astype(F32)
    grad_up = up_mine.astype(F32) + up_got.astype(F32)
    result = (
        hidden + (out_own.astype(F32) + out_got.astype(F32) + out_got_far.astype(F32))
    ).astype(LINK)
    in_half = in_cols // 2
    grad_in = jnp.concatenate([owned[:, :in_half], owned[:, cut : cut + in_half]], axis=1)
    grad_outw = jnp.concatenate([owned[:, in_half:cut], owned[:, cut + in_half : 2 * cut]], axis=1)
    return (
        result,
        input_grad,
        owned[:, 2 * cut],
        grad_in,
        owned[:, 2 * cut + 2 : 2 * cut + 5],
        grad_outw,
        owned[:, 2 * cut + 1],
        grad_gate,
        grad_up,
        grad_down,
    )


def solution(mesh):
    rows_spec, cols_spec = P(("dp", "fsdp"), None), P("fsdp", "dp")
    gain_spec, taps_spec = P("fsdp"), P("fsdp", None)
    return jax.shard_map(
        body,
        mesh=mesh,
        in_specs=(
            rows_spec,
            rows_spec,
            gain_spec,
            cols_spec,
            taps_spec,
            cols_spec,
            gain_spec,
            cols_spec,
            cols_spec,
            cols_spec,
            rows_spec,
        ),
        out_specs=(
            rows_spec,
            rows_spec,
            gain_spec,
            cols_spec,
            taps_spec,
            cols_spec,
            gain_spec,
            cols_spec,
            cols_spec,
            cols_spec,
        ),
        check_vma=False,
    )
```

```python
import functools

import jax
import jax.numpy as jnp
from jax import lax
from jax.experimental import pallas as pl
from jax.experimental.pallas import tpu as pltpu
from jax.sharding import PartitionSpec as P

EPSILON = 1e-05
LINK = jnp.bfloat16
F32 = jnp.float32
PAD = 128
MIB = 1 << 20


def dot_plain(left, right):
    return jnp.dot(left, right, preferred_element_type=F32)


def dot_rows(left, right):
    return lax.dot_general(left, right, (((0,), (0,)), ((), ())), preferred_element_type=F32)


def dot_last(left, right):
    return lax.dot_general(left, right, (((1,), (1,)), ((), ())), preferred_element_type=F32)


def after(v, *others):
    return lax.optimization_barrier((v, *others))[0]


def shape(dims, dtype):
    return jax.ShapeDtypeStruct(dims, dtype)


SCALARS = pl.BlockSpec(memory_space=pltpu.SMEM)
WHOLE = pl.BlockSpec(memory_space=pltpu.VMEM)
APART = pl.BlockSpec(memory_space=pl.ANY)


def call(kernel, scalars, args, outs, flops=0, limit=40, scratch=(), apart=0, deps=()):
    moved = sum(a.size * a.dtype.itemsize for a in args) + sum(
        o.size * jnp.dtype(o.dtype).itemsize for o in outs
    )
    first, last = 1 + len(args), 1 + len(args) + len(deps)

    def run(*refs):
        kernel(*refs[:first], *refs[last:])

    return pl.pallas_call(
        run,
        out_shape=outs,
        in_specs=[SCALARS] + [WHOLE] * len(args) + [APART] * len(deps),
        out_specs=[WHOLE] * (len(outs) - apart) + [APART] * apart,
        scratch_shapes=list(scratch),
        compiler_params=pltpu.CompilerParams(vmem_limit_bytes=limit * MIB),
        cost_estimate=pl.CostEstimate(flops=flops, bytes_accessed=moved, transcendentals=0),
    )(scalars, *args, *deps)


def pack_kernel(where_ref, in_ref, out_ref, one_ref, two_ref, taps_ref, packed_ref):
    rows = in_ref.shape[0]
    in_half, out_half = in_ref.shape[1] // 2, out_ref.shape[1] // 2
    cut = in_half + out_half
    packed_ref[:, :in_half] = in_ref[:, :in_half]
    packed_ref[:, in_half:cut] = out_ref[:, :out_half]
    packed_ref[:, cut : cut + in_half] = in_ref[:, in_half:]
    packed_ref[:, cut + in_half : 2 * cut] = out_ref[:, out_half:]
    eye = lax.broadcasted_iota(jnp.int32, (rows, rows), 0) == lax.broadcasted_iota(
        jnp.int32, (rows, rows), 1
    )
    lane = lax.broadcasted_iota(jnp.int32, (rows, PAD), 1)
    small = jnp.zeros((rows, PAD), F32)
    for k, ref in enumerate((one_ref, two_ref)):
        column = jnp.sum(jnp.where(eye, ref[...].astype(F32), 0.0), axis=1, keepdims=True)
        small = jnp.where(lane == k, column, small)
    for k in range(3):
        small = jnp.where(lane == 2 + k, taps_ref[:, k : k + 1].astype(F32), small)
    packed_ref[:, 2 * cut :] = small.astype(LINK)


def merge_kernel(where_ref, *refs):
    pieces, (first_ref, second_ref, small_ref) = refs[:-3], refs[-3:]
    rows = pieces[0].shape[0]
    high = where_ref[2]
    cut = first_ref.shape[1]
    for s, piece in enumerate(pieces):
        spot = high - s
        spot = jnp.where(spot < 0, spot + len(pieces), spot)
        at = pl.ds(pl.multiple_of(spot * rows, rows), rows)
        first_ref[at, :] = piece[:, :cut]
        second_ref[at, :] = piece[:, cut : 2 * cut]
        small_ref[at, :] = piece[:, 2 * cut :]


def natural(low, near, away, put, rows, blocks):
    def one(h, carry):
        at = pl.ds(pl.multiple_of(h * rows, rows), rows)
        put(pl.ds(pl.multiple_of((2 * h + low) * rows, rows), rows), at, near)
        put(pl.ds(pl.multiple_of((2 * h + 1 - low) * rows, rows), rows), at, away)
        return carry

    lax.fori_loop(0, blocks, one, 0)


def mixer_weights_kernel(rows, where_ref, *refs):
    pieces, (in_ref, out_ref) = refs[:16], refs[16:18]
    low, place = where_ref[0], where_ref[1]
    in_half, out_half = in_ref.shape[1] // 8, out_ref.shape[1] // 8
    for k in range(8):
        half, r = k // 4, k % 4
        block = lax.bitwise_xor(place, r)
        in_at = pl.ds(pl.multiple_of((2 * block + half) * in_half, PAD), in_half)
        out_at = pl.ds(pl.multiple_of((2 * block + half) * out_half, PAD), out_half)

        def put(to, at, ref):
            in_ref[to, in_at] = ref[at, :in_half]
            out_ref[to, out_at] = ref[at, in_half:]

        natural(low, pieces[2 * k], pieces[2 * k + 1], put, rows, pieces[0].shape[0] // rows)


def back_rows(v, steps):
    return pltpu.roll(v, steps, 0)


def ahead_rows(v, steps):
    return pltpu.roll(v, v.shape[0] - steps, 0)


def small_rows(rows, low, near_ref, away_ref, small_ref):
    def put(to, at, ref):
        small_ref[to, :] = ref[at, :].astype(F32)

    natural(low, near_ref, away_ref, put, rows, near_ref.shape[0] // rows)
    return small_ref[...].T[:8]


def mixer_kernel(
    rows,
    where_ref,
    tokens_ref,
    same_ref,
    near_ref,
    away_ref,
    *refs,
):
    pieces = refs[:16]
    normed_ref, parts_ref, scaled_ref, hidden_ref, next_ref, gains_ref = refs[16:22]
    small_ref, in_ref, outw_ref, in_sem, outw_sem = refs[24:]
    mixer_weights_kernel(rows, where_ref, *pieces, in_ref, outw_ref)
    in_copy = pltpu.make_async_copy(in_ref, refs[22], in_sem)
    outw_copy = pltpu.make_async_copy(outw_ref, refs[23], outw_sem)
    in_copy.start()
    outw_copy.start()
    width = tokens_ref.shape[1]
    step = 256
    gains_ref[...] = small_rows(rows, where_ref[0], near_ref, away_ref, small_ref)
    inputs = tokens_ref[...].astype(F32)
    inverse = lax.rsqrt(jnp.mean(inputs * inputs, axis=1, keepdims=True) + EPSILON)
    normed_ref[...] = (inputs * inverse * gains_ref[0:1, :]).astype(LINK)

    def chunk(q, carry):
        at = pl.ds(pl.multiple_of(q * step, step), step)

        def part(k):
            w = in_ref[:, pl.ds(pl.multiple_of(k * width + q * step, step), step)]
            v = dot_plain(normed_ref[...], w)
            parts_ref[k, :, at] = v
            return v

        b_part = part(0)
        x_part = part(2)
        gated = b_part * x_part
        mixed = (
            gains_ref[2:3, at] * gated
            + gains_ref[3:4, at] * (back_rows(gated, 1) * same_ref[:, 0:1])
            + gains_ref[4:5, at] * (back_rows(gated, 2) * same_ref[:, 1:2])
        )
        scaled_ref[:, at] = (part(1) * mixed).astype(LINK)
        return carry

    lax.fori_loop(0, width // step, chunk, 0)

    def final(q, total):
        at = pl.ds(pl.multiple_of(q * step, step), step)
        v = tokens_ref[:, at].astype(F32) + dot_last(scaled_ref[...], outw_ref[at, :])
        hidden_ref[:, at] = v
        return total + jnp.sum(v * v, axis=1, keepdims=True)

    total = lax.fori_loop(
        0, width // step, final, jnp.zeros((tokens_ref.shape[0], 1), F32)
    )
    inverse_two = lax.rsqrt(total / width + EPSILON)
    next_ref[...] = (hidden_ref[...] * inverse_two * gains_ref[1:2, :]).astype(LINK)
    in_copy.wait()
    outw_copy.wait()


def mixer_back_kernel(
    where_ref,
    own_ref,
    got_ref,
    far_one_ref,
    far_two_ref,
    hidden_ref,
    cot_ref,
    same_ref,
    gains_ref,
    parts_ref,
    outw_ref,
    hidden_grad_ref,
    branch_ref,
    proj_ref,
    sums_ref,
):
    width = hidden_ref.shape[1]
    step = 256
    hidden = hidden_ref[...]
    inverse = lax.rsqrt(jnp.mean(hidden * hidden, axis=1, keepdims=True) + EPSILON)
    far = jnp.concatenate([far_one_ref[...], far_two_ref[...]], axis=0)
    grad = own_ref[...].astype(F32) + got_ref[...].astype(F32) + far.astype(F32)
    sums_ref[0:1, :] = jnp.zeros((1, width), F32)
    sums_ref[1:2, :] = jnp.sum(grad * (hidden * inverse), axis=0, keepdims=True)
    weighted = grad * gains_ref[1:2, :]
    mean = jnp.mean(weighted * hidden, axis=1, keepdims=True)
    total = cot_ref[...].astype(F32) + inverse * (weighted - hidden * (inverse * inverse * mean))
    hidden_grad_ref[...] = total
    branch_ref[...] = total.astype(LINK)

    def chunk(q, carry):
        at = pl.ds(pl.multiple_of(q * step, step), step)
        grad_scaled = dot_plain(branch_ref[...], outw_ref[:, at])
        b_part, c_part, x_part = (parts_ref[k, :, at] for k in range(3))
        same_one, same_two = same_ref[:, 0:1], same_ref[:, 1:2]
        gated = b_part * x_part
        back_one = back_rows(gated, 1) * same_one
        back_two = back_rows(gated, 2) * same_two
        taps = [gains_ref[2 + k : 3 + k, at] for k in range(3)]
        mixed = taps[0] * gated + taps[1] * back_one + taps[2] * back_two
        grad_mixed = grad_scaled * c_part
        sums_ref[2:3, at] = jnp.sum(grad_mixed * gated, axis=0, keepdims=True)
        sums_ref[3:4, at] = jnp.sum(grad_mixed * back_one, axis=0, keepdims=True)
        sums_ref[4:5, at] = jnp.sum(grad_mixed * back_two, axis=0, keepdims=True)
        grad_gated = (
            taps[0] * grad_mixed
            + taps[1] * ahead_rows(grad_mixed * same_one, 1)
            + taps[2] * ahead_rows(grad_mixed * same_two, 2)
        )
        for k, v in enumerate((grad_gated * x_part, grad_scaled * mixed, grad_gated * b_part)):
            proj_ref[:, pl.ds(pl.multiple_of(k * width + q * step, step), step)] = v.astype(LINK)
        return carry

    lax.fori_loop(0, width // step, chunk, 0)
    sums_ref[5:8, :] = jnp.zeros((3, width), F32)


def mixer_grads_kernel(
    rows, order, where_ref, normed_ref, proj_ref, branch_ref, scaled_ref, *refs
):
    low, place = where_ref[0], where_ref[1]
    outs, (total_ref, held_ref, sems) = refs[:8], refs[8:]
    in_half = proj_ref.shape[1] // 8
    out_half = scaled_ref.shape[1] // 8
    for n in range(4):
        i, half = n // 2, n % 2
        block = 2 * lax.bitwise_xor(place, order[i]) + half
        in_at = pl.ds(pl.multiple_of(block * in_half, PAD), in_half)
        out_at = pl.ds(pl.multiple_of(block * out_half, PAD), out_half)
        total_ref[:, :in_half] = dot_rows(normed_ref[...], proj_ref[:, in_at])
        total_ref[:, in_half:] = dot_rows(branch_ref[...], scaled_ref[:, out_at])

        def copy(h, carry, n=n):
            to = pl.ds(pl.multiple_of(h * rows, rows), rows)
            for k, bit in enumerate((low, 1 - low)):
                at = pl.ds(pl.multiple_of((2 * h + bit) * rows, rows), rows)
                held_ref[2 * n + k, to, :] = total_ref[at, :].astype(LINK)
            return carry

        lax.fori_loop(0, held_ref.shape[1] // rows, copy, 0)
        for k in (2 * n, 2 * n + 1):
            pltpu.make_async_copy(held_ref.at[k], outs[k], sems.at[k]).start()
    for k in range(8):
        pltpu.make_async_copy(held_ref.at[k], outs[k], sems.at[k]).wait()


def final_kernel(where_ref, own_ref, *refs):
    gots, (in_ref, outw_ref, one_ref, two_ref, taps_ref) = refs[:-5], refs[-5:]
    in_half, out_half = in_ref.shape[1] // 2, outw_ref.shape[1] // 2
    cut = in_half + out_half

    def total(start, size):
        v = own_ref[:, start : start + size]
        for ref in gots:
            v = v + ref[:, start : start + size].astype(F32)
        return v

    for k in range(2):
        in_ref[:, k * in_half : (k + 1) * in_half] = total(k * cut, in_half)
        outw_ref[:, k * out_half : (k + 1) * out_half] = total(k * cut + in_half, out_half)
    small = total(2 * cut, PAD)
    turned = small.T
    one_ref[...] = turned[0:1]
    two_ref[...] = turned[1:2]
    taps_ref[...] = small[:, 2:5]


def join_kernel(where_ref, *refs):
    for k in range(2):
        a, b, c = (r[...].astype(F32) for r in refs[3 * k : 3 * k + 3])
        refs[6 + k][...] = (a + b + c).astype(LINK)


def add_kernel(where_ref, *refs):
    n = len(refs) // 3
    for a, b, c in zip(refs[:n], refs[n : 2 * n], refs[2 * n :]):
        c[...] = (a[...].astype(F32) + b[...].astype(F32)).astype(c.dtype)


def last_kernel(
    rows, where_ref, a_ref, a_got_ref, a_far_ref, a_row_ref, b_ref, b_got_ref, b_row_ref, b_far_ref, small_ref, *refs
):
    low, high = where_ref[0], where_ref[2]
    cut = a_ref.shape[1]
    own_ref, sends, turned_ref = refs[0], refs[1:-1], refs[-1]
    width = turned_ref.shape[0]
    turned_ref[...] = jnp.concatenate(
        [small_ref[...], jnp.zeros((PAD - 8, width), F32)], axis=0
    ).T

    def total(at, *parts):
        v = parts[0][at, :].astype(F32)
        for p in parts[1:]:
            v = v + p[at, :].astype(F32)
        return v

    for s, ref in enumerate((own_ref, *sends)):
        spot = high + s
        spot = jnp.where(spot >= len(sends) + 1, spot - len(sends) - 1, spot)
        at = pl.ds(pl.multiple_of(spot * rows, rows), rows)
        ref[:, :cut] = total(at, a_ref, a_got_ref, a_far_ref, a_row_ref).astype(ref.dtype)
        ref[:, cut : 2 * cut] = total(at, b_ref, b_got_ref, b_row_ref, b_far_ref).astype(ref.dtype)
        at = pl.ds(pl.multiple_of((2 * spot + low) * rows, rows), rows)
        ref[:, 2 * cut :] = turned_ref[at, :].astype(ref.dtype)


def mixer_input_kernel(
    rows,
    where_ref,
    tokens_ref,
    hidden_grad_ref,
    gains_ref,
    sums_ref,
    proj_ref,
    in_ref,
    input_ref,
    small_ref,
    grad_ref,
):
    width = tokens_ref.shape[1]
    step = 256
    inputs = tokens_ref[...].astype(F32)
    inverse = lax.rsqrt(jnp.mean(inputs * inputs, axis=1, keepdims=True) + EPSILON)

    def chunk(q, carry):
        at = pl.ds(pl.multiple_of(q * step, step), step)
        grad_ref[:, at] = dot_last(proj_ref[...], in_ref[at, :])
        return carry

    lax.fori_loop(0, width // step, chunk, 0)
    grad = grad_ref[...]
    row = lax.broadcasted_iota(jnp.int32, (8, width), 0)
    gain_grad = jnp.sum(grad * (inputs * inverse), axis=0, keepdims=True)
    small_ref[...] = jnp.where(row == 0, gain_grad, sums_ref[...])
    weighted = grad * gains_ref[0:1, :]
    mean = jnp.mean(weighted * inputs, axis=1, keepdims=True)
    input_ref[...] = hidden_grad_ref[...] + inverse * (
        weighted - inputs * (inverse * inverse * mean)
    )


TILE = 256


def piece_specs(pieces, count, width):
    tiles = count // TILE
    return [
        pl.BlockSpec(
            (TILE, width), lambda t, k=k: (jnp.clip(t - k * tiles, 0, tiles - 1), 0)
        )
        for k in range(pieces)
    ]


def pick(refs, tiles):
    v = refs[0][...]
    for k in range(1, len(refs)):
        v = jnp.where(pl.program_id(0) >= k * tiles, refs[k][...], v)
    return v


def put_piece(refs, tiles, v):
    for k, ref in enumerate(refs):

        @pl.when((pl.program_id(0) >= k * tiles) & (pl.program_id(0) < (k + 1) * tiles))
        def _(ref=ref):
            ref[...] = v.astype(ref.dtype)


def whole_spec(v):
    return pl.BlockSpec(v.shape, lambda t: (0, 0))


def tiled(kernel, grid, in_specs, args, out_specs, outs, flops, limit=56, scratch=()):
    moved = sum(a.size * a.dtype.itemsize for a in args) + sum(
        o.size * jnp.dtype(o.dtype).itemsize for o in outs
    )
    return pl.pallas_call(
        kernel,
        grid=(grid,),
        in_specs=in_specs,
        out_specs=out_specs,
        out_shape=outs,
        scratch_shapes=list(scratch),
        compiler_params=pltpu.CompilerParams(vmem_limit_bytes=limit * MIB),
        cost_estimate=pl.CostEstimate(flops=flops, bytes_accessed=moved, transcendentals=0),
    )(*args)


def act_kernel(tiles, rows, where_ref, *refs):
    pieces, woven, (act_ref, silu_ref, slope_ref, gate_ref, up_ref) = refs[:4], refs[4:8], refs[8:]

    @pl.when(pl.program_id(0) == 0)
    def _():
        for k, whole_ref in enumerate((gate_ref, up_ref)):

            def put(to, at, ref, whole_ref=whole_ref):
                whole_ref[to, :] = ref[at, :]

            natural(where_ref[0], *woven[2 * k : 2 * k + 2], put, rows, woven[0].shape[0] // rows)

    normed = pick(pieces, tiles)
    gate = dot_plain(normed, gate_ref[...])
    up = dot_plain(normed, up_ref[...])
    sigmoid = 1.0 / (1.0 + jnp.exp(-gate))
    silu = gate * sigmoid
    act_ref[...] = (silu * up).astype(LINK)
    silu_ref[...] = silu.astype(LINK)
    slope_ref[...] = (up * (sigmoid + silu * (1.0 - sigmoid))).astype(LINK)


def act_call(rows, scalars, pieces, woven):
    count, width = pieces[0].shape
    inner = woven[0].shape[1]
    tiles = count // TILE
    wide = pl.BlockSpec((TILE, inner), lambda t: (t, 0))
    weight = shape((width, inner), LINK)
    return tiled(
        functools.partial(act_kernel, tiles, rows),
        4 * tiles,
        [SCALARS] + piece_specs(4, count, width) + [whole_spec(v) for v in woven],
        [scalars, *pieces, *woven],
        [wide] * 3 + [whole_spec(weight)] * 2,
        [shape((4 * count, inner), LINK)] * 3 + [weight] * 2,
        16 * count * width * inner,
    )


def back_kernel(pieces, tiles, with_got, *refs):
    cots, refs = refs[:pieces], refs[pieces:]
    silu_ref, slope_ref, gate_ref, up_ref, down_ref = refs[:5]
    refs = refs[5:]
    if with_got:
        got_ref, refs = refs[0], refs[1:]
    grad_gate_ref, grad_up_ref = refs[:2]
    grad_act = dot_plain(pick(cots, tiles), down_ref[...])
    grad_up_ref[...] = (grad_act * silu_ref[...].astype(F32)).astype(LINK)
    grad_gate_ref[...] = (grad_act * slope_ref[...].astype(F32)).astype(LINK)
    back = dot_last(grad_gate_ref[...], gate_ref[...]) + dot_last(grad_up_ref[...], up_ref[...])
    if with_got:
        back = back + got_ref[...].astype(F32)
    put_piece(refs[2:], tiles, back)


def back_call(start, cots, silu, slope, gate, up, down, got=None):
    count, width = cots[0].shape
    inner = gate.shape[1]
    tiles, pieces = count // TILE, len(cots)
    wide_in = pl.BlockSpec((TILE, inner), lambda t: (t + start * tiles, 0))
    wide = pl.BlockSpec((TILE, inner), lambda t: (t, 0))
    thin = piece_specs(pieces, count, width)
    extra = [] if got is None else [got]
    return tiled(
        functools.partial(back_kernel, pieces, tiles, got is not None),
        pieces * tiles,
        thin + [wide_in] * 2 + [whole_spec(gate)] * 3 + thin[: len(extra)],
        [*cots, silu, slope, gate, up, down, *extra],
        [wide] * 2 + thin,
        [shape((pieces * count, inner), LINK)] * 2 + [shape((count, width), LINK)] * pieces,
        6 * pieces * count * width * inner,
    )


def out_kernel(tiles, skip, act_ref, down_ref, *refs):
    put_piece(refs[skip:], tiles, dot_last(act_ref[...], down_ref[...]))


def out_call(act, down, count, deps):
    width, inner = down.shape
    tiles = count // TILE
    return tiled(
        functools.partial(out_kernel, tiles, len(deps)),
        4 * tiles,
        [pl.BlockSpec((TILE, inner), lambda t: (t, 0)), whole_spec(down)] + [APART] * len(deps),
        [act, down, *deps],
        piece_specs(4, count, width),
        [shape((count, width), LINK)] * 4,
        8 * count * width * inner,
    )


def weight_grad_kernel(rows, spots, whole, where_ref, *refs):
    lefts, refs = refs[:4], refs[4:]
    low = where_ref[0]
    count = lefts[0].shape[0]
    at = pl.ds(pl.multiple_of(pl.program_id(0) * TILE, TILE), TILE)
    total = None
    for left, (k, start) in zip(lefts, spots):
        v = dot_rows(left[:, at], refs[k][start * count : (start + 1) * count, :])
        total = v if total is None else total + v
    if whole:
        refs[-1][...] = total.astype(LINK)
        return
    near_ref, away_ref, total_ref = refs[-3:]
    total_ref[...] = total
    for h in range(near_ref.shape[0] // rows):
        to = pl.ds(h * rows, rows)
        for ref, bit in ((near_ref, low), (away_ref, 1 - low)):
            at = pl.ds(pl.multiple_of((2 * h + bit) * rows, rows), rows)
            ref[to, :] = total_ref[at, :].astype(ref.dtype)


def pair_grad_kernel(rows, spots, where_ref, *refs):
    lefts, gates, ups = refs[:4], refs[4:7], refs[7:10]
    near_ref, away_ref, up_ref, total_ref = refs[10:]
    low = where_ref[0]
    count = lefts[0].shape[0]
    at = pl.ds(pl.multiple_of(pl.program_id(0) * TILE, TILE), TILE)

    def total(rights):
        v = None
        for left, (k, start) in zip(lefts, spots):
            part = dot_rows(left[:, at], rights[k][start * count : (start + 1) * count, :])
            v = part if v is None else v + part
        return v

    up_ref[...] = total(ups).astype(LINK)
    total_ref[...] = total(gates)
    for h in range(near_ref.shape[0] // rows):
        to = pl.ds(h * rows, rows)
        for ref, bit in ((near_ref, low), (away_ref, 1 - low)):
            at_rows = pl.ds(pl.multiple_of((2 * h + bit) * rows, rows), rows)
            ref[to, :] = total_ref[at_rows, :].astype(ref.dtype)


def pair_grad(rows, scalars, lefts, gates, ups, spots):
    count, width = lefts[0].shape
    inner = gates[0].shape[1]
    half = pl.BlockSpec((TILE // 2, inner), lambda t: (t, 0))
    args = [*lefts, *gates, *ups]
    return tiled(
        functools.partial(pair_grad_kernel, rows, spots),
        width // TILE,
        [SCALARS] + [whole_spec(v) for v in args],
        [scalars, *args],
        [half, half, pl.BlockSpec((TILE, inner), lambda t: (t, 0))],
        [
            shape((width // 2, inner), F32),
            shape((width // 2, inner), LINK),
            shape((width, inner), LINK),
        ],
        16 * count * width * inner,
        scratch=[pltpu.VMEM((TILE, inner), F32)],
    )


def weight_grad(rows, scalars, lefts, rights, spots, whole=False):
    count, width = lefts[0].shape
    inner = rights[0].shape[1]
    half = pl.BlockSpec((TILE // 2, inner), lambda t: (t, 0))
    return tiled(
        functools.partial(weight_grad_kernel, rows, spots, whole),
        width // TILE,
        [SCALARS] + [whole_spec(v) for v in (*lefts, *rights)],
        [scalars, *lefts, *rights],
        [pl.BlockSpec((TILE, inner), lambda t: (t, 0))] if whole else [half, half],
        [shape((width, inner), LINK)]
        if whole
        else [shape((width // 2, inner), F32), shape((width // 2, inner), LINK)],
        8 * count * width * inner,
        scratch=[] if whole else [pltpu.VMEM((TILE, inner), F32)],
    )


def body(
    tokens,
    segments,
    mixer_gain,
    in_weight,
    conv_kernel,
    out_weight,
    ffn_gain,
    gate_weight,
    up_weight,
    down_weight,
    cotangent,
):
    count, width = tokens.shape
    rows = in_weight.shape[0]
    in_cols, out_cols = in_weight.shape[1], out_weight.shape[1]
    cut = (in_cols + out_cols) // 2
    ways = width // rows
    half = ways // 2
    columns = lax.axis_size("dp")
    place = lax.axis_index("dp")
    low = lax.rem(lax.axis_index("fsdp"), 2)
    high = lax.axis_index("fsdp") // 2
    scalars = jnp.stack([low, place, high]).astype(jnp.int32)
    strides = [[2 * h + bit for h in range(half)] for bit in range(2)]

    def swap_row(v):
        return lax.ppermute(v, "fsdp", [(i, i ^ 1) for i in range(ways)])

    def swap_far(v):
        return lax.ppermute(v, "dp", [(i, i ^ 2) for i in range(columns)])

    def swap_core(v):
        return lax.ppermute(v, "dp", [(i, i ^ 1) for i in range(columns)])

    def shift_high(v, s):
        return lax.ppermute(v, "fsdp", [(i, (i + 2 * s) % ways) for i in range(ways)])

    def gather_high(v):
        return lax.all_gather(v, "fsdp", axis=0, tiled=True, axis_index_groups=strides)

    def scatter_high(v):
        return lax.psum_scatter(
            v, "fsdp", scatter_dimension=0, tiled=True, axis_index_groups=strides
        )

    (packed,) = call(
        pack_kernel,
        scalars,
        [in_weight, out_weight, mixer_gain[None, :], ffn_gain[None, :], conv_kernel],
        [shape((rows, 2 * cut + PAD), LINK)],
    )
    shifts = [packed] + [shift_high(packed, s) for s in range(1, half)]
    tall = half * rows
    down_other = swap_row(after(down_weight, packed))
    down_pair = jnp.where(
        low == 0,
        jnp.concatenate([down_weight, down_other], axis=0),
        jnp.concatenate([down_other, down_weight], axis=0),
    )
    shifts[0] = after(shifts[0], down_pair)
    first, second, small_near = call(
        merge_kernel,
        scalars,
        shifts,
        [shape((tall, cut), LINK), shape((tall, cut), LINK), shape((tall, PAD), LINK)],
    )
    gate_near = gather_high(after(gate_weight, first))
    up_near = gather_high(after(up_weight, first))
    down_all = gather_high(after(down_pair, first))
    first_row = swap_row(first)
    second_far = swap_far(second)
    small_away = swap_row(small_near)
    second_row = swap_row(second)
    first_far = swap_far(first)
    second_far_row = swap_row(second_far)
    first_row_far = swap_far(first_row)
    cot_far = swap_far(after(cotangent, first_row_far))
    chip = [[[first, first_row], [first_far, first_row_far]], [[second, second_row], [second_far, second_far_row]]]
    pieces = []
    for k in range(2):
        other = [[swap_core(v) for v in pair] for pair in chip[k]]
        for pair in (chip[k][0], other[0], chip[k][1], other[1]):
            pieces += pair
    pieces[0] = after(pieces[0], gate_near, small_away)
    gate_row = swap_row(gate_near)
    up_row = swap_row(up_near)

    def gather_tokens(v, far):
        return [v, swap_core(v), far, swap_core(far)]

    cots = gather_tokens(cotangent, cot_far)

    seg_ids = segments[0]
    zero = jnp.zeros((2,), F32)
    same = jnp.stack(
        [
            jnp.concatenate([zero[:1], (seg_ids[1:] == seg_ids[:-1]).astype(F32)]),
            jnp.concatenate([zero, (seg_ids[2:] == seg_ids[:-2]).astype(F32)]),
        ],
        axis=1,
    )
    normed, parts, scaled, hidden, normed_two, gains, in_all, outw_all = call(
        functools.partial(mixer_kernel, rows),
        scalars,
        [tokens, same, small_near, small_away, *pieces],
        [
            shape((count, width), LINK),
            shape((3, count, width), F32),
            shape((count, width), LINK),
            shape((count, width), F32),
            shape((count, width), LINK),
            shape((8, width), F32),
            shape((width, columns * in_cols), LINK),
            shape((width, columns * out_cols), LINK),
        ],
        apart=2,
        flops=8 * count * width * width,
        scratch=[
            pltpu.VMEM((width, PAD), F32),
            pltpu.VMEM((width, columns * in_cols), LINK),
            pltpu.VMEM((width, columns * out_cols), LINK),
            pltpu.SemaphoreType.DMA,
            pltpu.SemaphoreType.DMA,
        ],
        limit=56,
    )

    normed_two = after(normed_two, up_near, cot_far, gate_row)
    normeds = gather_tokens(normed_two, swap_far(normed_two))
    act, silu, slope, gate_all, up_all = act_call(
        rows, scalars, normeds, [gate_near, gate_row, up_near, up_row]
    )

    def add(*pairs):
        return call(
            add_kernel,
            scalars,
            [p[0] for p in pairs] + [p[1] for p in pairs],
            [shape(p[0].shape, LINK) for p in pairs],
        )

    def join(near, away_got):
        return call(add_kernel, scalars, [near, away_got], [shape(near.shape, LINK)])[0]

    weights = (silu, slope, gate_all, up_all, down_all)
    gate_xc, up_xc, back_xc = back_call(3, [cots[3]], *weights)
    down_near, down_away = weight_grad(
        rows,
        scalars,
        [after(cots[0], back_xc), *cots[1:]],
        [act],
        [(0, 0), (0, 1), (0, 2), (0, 3)],
    )
    gate_x, up_x, back_far = back_call(
        2, [after(cots[2], down_away)], *weights, got=swap_core(back_xc)
    )
    gate_o, up_o, back_own, back_c = back_call(
        0, [after(cots[0], back_far), cots[1]], *weights
    )
    down_got = swap_row(down_away)
    back_one = swap_far(back_far[: count // 2])
    back_two = swap_far(back_far[count // 2 :])
    spots = [(0, 0), (0, 1), (1, 0), (2, 0)]
    down_sum = join(down_near, down_got)
    gate_near_grad, gate_away, up_whole = pair_grad(
        rows,
        scalars,
        [after(normeds[0], down_sum, back_one), *normeds[1:]],
        [gate_o, gate_x, gate_xc],
        [up_o, up_x, up_xc],
        spots,
    )
    up_pair = scatter_high(up_whole).reshape(2, rows, -1)
    up_mine = jnp.where(low == 0, up_pair[0], up_pair[1])
    up_other = jnp.where(low == 0, up_pair[1], up_pair[0])
    grad_down = scatter_high(down_sum).astype(F32)
    gate_one = swap_row(gate_away[: tall // 2])
    gate_two = swap_row(gate_away[tall // 2 :])

    hidden_grad, branch, proj, sums = call(
        mixer_back_kernel,
        scalars,
        [after(back_own, gate_away), swap_core(back_c), back_one, back_two, hidden, cotangent, same, gains, parts, outw_all],
        [
            shape((count, width), F32),
            shape((count, width), LINK),
            shape((count, 3 * width), LINK),
            shape((8, width), F32),
        ],
        flops=2 * count * width * width,
        limit=48,
    )

    def mixer_grads(order, first_arg):
        return call(
            functools.partial(mixer_grads_kernel, rows, order),
            scalars,
            [first_arg, proj, branch, scaled],
            [shape((tall, cut), LINK)] * 8,
            flops=4 * count * width * width,
            scratch=[
                pltpu.VMEM((width, cut), F32),
                pltpu.VMEM((8, tall, cut), LINK),
                pltpu.SemaphoreType.DMA((8,)),
            ],
            apart=8,
        )

    send = mixer_grads((1, 3), after(normed, gate_one))
    got = [swap_core(v) for v in send]
    mine = mixer_grads((0, 2), after(normed, send[0]))
    input_grad, sums = call(
        functools.partial(mixer_input_kernel, rows),
        scalars,
        [tokens, after(hidden_grad, mine[0]), gains, sums, proj, in_all],
        [shape((count, width), F32), shape((8, width), F32)],
        flops=6 * count * width * width,
        scratch=[pltpu.VMEM((count, width), F32)],
    )
    mine = [*mine[:5], after(mine[5], input_grad), *mine[6:]]
    a_away_far, b_away_far, a_near_far, b_away_own = add(
        *((after(mine[k], gate_two), got[k]) for k in (5, 7, 4, 3))
    )
    a_away_got = swap_far(a_away_far)
    b_away_got = swap_row(b_away_far)
    a_near_got = swap_far(a_near_far)
    b_own_got = swap_row(b_away_own)
    sums_core = sums + swap_core(sums)
    sums_far = sums_core + swap_far(sums_core)

    out_own, out_c, out_x, out_xc = out_call(after(act, a_near_far), down_all, count, [up_pair])
    gate_got = jnp.concatenate([gate_one, gate_two], axis=0)
    gate_sum = join(after(gate_near_grad, out_own), gate_got)
    grad_gate = scatter_high(gate_sum).astype(F32)
    a_away, b_far = call(
        join_kernel,
        scalars,
        [mine[1], got[1], a_away_got, mine[6], got[6], b_away_got],
        [shape((tall, cut), LINK)] * 2,
        deps=[out_own, a_near_got, b_own_got],
    )
    own, *sends = call(
        functools.partial(last_kernel, rows),
        scalars,
        [
            mine[0],
            got[0],
            a_near_got,
            swap_row(a_away),
            mine[2],
            got[2],
            b_own_got,
            swap_far(b_far),
            sums_far + swap_row(sums_far),
        ],
        [shape((rows, 2 * cut + PAD), F32)] + [shape((rows, 2 * cut + PAD), LINK)] * (half - 1),
        scratch=[pltpu.VMEM((width, PAD), F32)],
        deps=[gate_sum],
    )
    gots = [shift_high(sends[s - 1], s) for s in range(1, half)]
    (out_far,) = add((after(out_x, own), swap_core(out_xc)))
    out_got, out_got_far = swap_core(out_c), swap_far(out_far)
    up_row = swap_row(after(up_other, own))
    grad_in, grad_outw, one_grad, two_grad, taps_grad = call(
        final_kernel,
        scalars,
        [own, *gots],
        [
            shape((rows, in_cols), F32),
            shape((rows, out_cols), F32),
            shape((1, rows), F32),
            shape((1, rows), F32),
            shape((rows, 3), F32),
        ],
    )
    grad_up = up_mine.astype(F32) + up_row.astype(F32)
    result = (
        hidden + (out_own.astype(F32) + out_got.astype(F32) + out_got_far.astype(F32))
    ).astype(LINK)
    return (
        result,
        input_grad,
        one_grad[0],
        grad_in,
        taps_grad,
        grad_outw,
        two_grad[0],
        grad_gate,
        grad_up,
        grad_down,
    )


def solution(mesh):
    rows_spec, cols_spec = P(("dp", "fsdp"), None), P("fsdp", "dp")
    gain_spec, taps_spec = P("fsdp"), P("fsdp", None)
    return jax.shard_map(
        body,
        mesh=mesh,
        in_specs=(
            rows_spec,
            rows_spec,
            gain_spec,
            cols_spec,
            taps_spec,
            cols_spec,
            gain_spec,
            cols_spec,
            cols_spec,
            cols_spec,
            rows_spec,
        ),
        out_specs=(
            rows_spec,
            rows_spec,
            gain_spec,
            cols_spec,
            taps_spec,
            cols_spec,
            gain_spec,
            cols_spec,
            cols_spec,
            cols_spec,
        ),
        check_vma=False,
    )
```

```python
import functools

import jax
import jax.numpy as jnp
from jax import lax
from jax.experimental import pallas as pl
from jax.experimental.pallas import tpu as pltpu
from jax.sharding import PartitionSpec as P

EPSILON = 1e-05
LINK = jnp.bfloat16
F32 = jnp.float32
PAD = 128
MIB = 1 << 20


def dot_plain(left, right):
    return jnp.dot(left, right, preferred_element_type=F32)


def dot_rows(left, right):
    return lax.dot_general(left, right, (((0,), (0,)), ((), ())), preferred_element_type=F32)


def dot_last(left, right):
    return lax.dot_general(left, right, (((1,), (1,)), ((), ())), preferred_element_type=F32)


def after(v, *others):
    return lax.optimization_barrier((v, *others))[0]


def shape(dims, dtype):
    return jax.ShapeDtypeStruct(dims, dtype)


SCALARS = pl.BlockSpec(memory_space=pltpu.SMEM)
WHOLE = pl.BlockSpec(memory_space=pltpu.VMEM)
APART = pl.BlockSpec(memory_space=pl.ANY)


def call(kernel, scalars, args, outs, flops=0, limit=40, scratch=(), apart=0, deps=()):
    moved = sum(a.size * a.dtype.itemsize for a in args) + sum(
        o.size * jnp.dtype(o.dtype).itemsize for o in outs
    )
    first, last = 1 + len(args), 1 + len(args) + len(deps)

    def run(*refs):
        kernel(*refs[:first], *refs[last:])

    return pl.pallas_call(
        run,
        out_shape=outs,
        in_specs=[SCALARS] + [WHOLE] * len(args) + [APART] * len(deps),
        out_specs=[WHOLE] * (len(outs) - apart) + [APART] * apart,
        scratch_shapes=list(scratch),
        compiler_params=pltpu.CompilerParams(vmem_limit_bytes=limit * MIB),
        cost_estimate=pl.CostEstimate(flops=flops, bytes_accessed=moved, transcendentals=0),
    )(scalars, *args, *deps)


def pack_kernel(where_ref, in_ref, out_ref, one_ref, two_ref, taps_ref, packed_ref):
    rows = in_ref.shape[0]
    in_half, out_half = in_ref.shape[1] // 2, out_ref.shape[1] // 2
    cut = in_half + out_half
    packed_ref[:, :in_half] = in_ref[:, :in_half]
    packed_ref[:, in_half:cut] = out_ref[:, :out_half]
    packed_ref[:, cut : cut + in_half] = in_ref[:, in_half:]
    packed_ref[:, cut + in_half : 2 * cut] = out_ref[:, out_half:]
    eye = lax.broadcasted_iota(jnp.int32, (rows, rows), 0) == lax.broadcasted_iota(
        jnp.int32, (rows, rows), 1
    )
    lane = lax.broadcasted_iota(jnp.int32, (rows, PAD), 1)
    small = jnp.zeros((rows, PAD), F32)
    for k, ref in enumerate((one_ref, two_ref)):
        column = jnp.sum(jnp.where(eye, ref[...].astype(F32), 0.0), axis=1, keepdims=True)
        small = jnp.where(lane == k, column, small)
    for k in range(3):
        small = jnp.where(lane == 2 + k, taps_ref[:, k : k + 1].astype(F32), small)
    packed_ref[:, 2 * cut :] = small.astype(LINK)


def merge_kernel(where_ref, *refs):
    pieces, (first_ref, second_ref, small_ref) = refs[:-3], refs[-3:]
    rows = pieces[0].shape[0]
    high = where_ref[2]
    cut = first_ref.shape[1]
    for s, piece in enumerate(pieces):
        spot = high - s
        spot = jnp.where(spot < 0, spot + len(pieces), spot)
        at = pl.ds(pl.multiple_of(spot * rows, rows), rows)
        first_ref[at, :] = piece[:, :cut]
        second_ref[at, :] = piece[:, cut : 2 * cut]
        small_ref[at, :] = piece[:, 2 * cut :]


def natural(low, near, away, put, rows, blocks):
    def one(h, carry):
        at = pl.ds(pl.multiple_of(h * rows, rows), rows)
        put(pl.ds(pl.multiple_of((2 * h + low) * rows, rows), rows), at, near)
        put(pl.ds(pl.multiple_of((2 * h + 1 - low) * rows, rows), rows), at, away)
        return carry

    lax.fori_loop(0, blocks, one, 0)


def mixer_weights_kernel(rows, where_ref, *refs):
    pieces, (in_ref, out_ref) = refs[:16], refs[16:18]
    low, place = where_ref[0], where_ref[1]
    in_half, out_half = in_ref.shape[1] // 8, out_ref.shape[1] // 8
    for k in range(8):
        half, r = k // 4, k % 4
        block = lax.bitwise_xor(place, r)
        in_at = pl.ds(pl.multiple_of((2 * block + half) * in_half, PAD), in_half)
        out_at = pl.ds(pl.multiple_of((2 * block + half) * out_half, PAD), out_half)

        def put(to, at, ref):
            in_ref[to, in_at] = ref[at, :in_half]
            out_ref[to, out_at] = ref[at, in_half:]

        natural(low, pieces[2 * k], pieces[2 * k + 1], put, rows, pieces[0].shape[0] // rows)


def back_rows(v, steps):
    return pltpu.roll(v, steps, 0)


def ahead_rows(v, steps):
    return pltpu.roll(v, v.shape[0] - steps, 0)


def small_rows(rows, low, near_ref, away_ref, small_ref):
    def put(to, at, ref):
        small_ref[to, :] = ref[at, :].astype(F32)

    natural(low, near_ref, away_ref, put, rows, near_ref.shape[0] // rows)
    return small_ref[...].T[:8]


def mixer_kernel(
    rows,
    where_ref,
    tokens_ref,
    same_ref,
    near_ref,
    away_ref,
    *refs,
):
    pieces = refs[:16]
    normed_ref, parts_ref, scaled_ref, hidden_ref, next_ref, gains_ref = refs[16:22]
    small_ref, in_ref, outw_ref, in_sem, outw_sem = refs[24:]
    mixer_weights_kernel(rows, where_ref, *pieces, in_ref, outw_ref)
    in_copy = pltpu.make_async_copy(in_ref, refs[22], in_sem)
    outw_copy = pltpu.make_async_copy(outw_ref, refs[23], outw_sem)
    in_copy.start()
    outw_copy.start()
    width = tokens_ref.shape[1]
    step = 256
    gains_ref[...] = small_rows(rows, where_ref[0], near_ref, away_ref, small_ref)
    inputs = tokens_ref[...].astype(F32)
    inverse = lax.rsqrt(jnp.mean(inputs * inputs, axis=1, keepdims=True) + EPSILON)
    normed_ref[...] = (inputs * inverse * gains_ref[0:1, :]).astype(LINK)

    def chunk(q, carry):
        at = pl.ds(q * step, step)

        def part(k):
            w = in_ref[:, pl.ds(k * width + q * step, step)]
            v = dot_plain(normed_ref[...], w)
            parts_ref[k, :, at] = v
            return v

        b_part = part(0)
        x_part = part(2)
        gated = b_part * x_part
        mixed = (
            gains_ref[2:3, at] * gated
            + gains_ref[3:4, at] * (back_rows(gated, 1) * same_ref[:, 0:1])
            + gains_ref[4:5, at] * (back_rows(gated, 2) * same_ref[:, 1:2])
        )
        scaled_ref[:, at] = (part(1) * mixed).astype(LINK)
        return carry

    for q in range(width // step):
        chunk(q, 0)

    def final(q, total):
        at = pl.ds(q * step, step)
        v = tokens_ref[:, at].astype(F32) + dot_last(scaled_ref[...], outw_ref[at, :])
        hidden_ref[:, at] = v
        return total + jnp.sum(v * v, axis=1, keepdims=True)

    total = jnp.zeros((tokens_ref.shape[0], 1), F32)
    for q in range(width // step):
        total = final(q, total)
    inverse_two = lax.rsqrt(total / width + EPSILON)
    next_ref[...] = (hidden_ref[...] * inverse_two * gains_ref[1:2, :]).astype(LINK)
    in_copy.wait()
    outw_copy.wait()


def mixer_back_kernel(
    where_ref,
    own_ref,
    got_ref,
    far_one_ref,
    far_two_ref,
    hidden_ref,
    cot_ref,
    same_ref,
    gains_ref,
    parts_ref,
    outw_ref,
    hidden_grad_ref,
    branch_ref,
    proj_ref,
    sums_ref,
):
    width = hidden_ref.shape[1]
    step = 256
    hidden = hidden_ref[...]
    inverse = lax.rsqrt(jnp.mean(hidden * hidden, axis=1, keepdims=True) + EPSILON)
    far = jnp.concatenate([far_one_ref[...], far_two_ref[...]], axis=0)
    grad = own_ref[...].astype(F32) + got_ref[...].astype(F32) + far.astype(F32)
    sums_ref[0:1, :] = jnp.zeros((1, width), F32)
    sums_ref[1:2, :] = jnp.sum(grad * (hidden * inverse), axis=0, keepdims=True)
    weighted = grad * gains_ref[1:2, :]
    mean = jnp.mean(weighted * hidden, axis=1, keepdims=True)
    total = cot_ref[...].astype(F32) + inverse * (weighted - hidden * (inverse * inverse * mean))
    hidden_grad_ref[...] = total
    branch_ref[...] = total.astype(LINK)

    def chunk(q, carry):
        at = pl.ds(q * step, step)
        grad_scaled = dot_plain(branch_ref[...], outw_ref[:, at])
        b_part, c_part, x_part = (parts_ref[k, :, at] for k in range(3))
        same_one, same_two = same_ref[:, 0:1], same_ref[:, 1:2]
        gated = b_part * x_part
        back_one = back_rows(gated, 1) * same_one
        back_two = back_rows(gated, 2) * same_two
        taps = [gains_ref[2 + k : 3 + k, at] for k in range(3)]
        mixed = taps[0] * gated + taps[1] * back_one + taps[2] * back_two
        grad_mixed = grad_scaled * c_part
        sums_ref[2:3, at] = jnp.sum(grad_mixed * gated, axis=0, keepdims=True)
        sums_ref[3:4, at] = jnp.sum(grad_mixed * back_one, axis=0, keepdims=True)
        sums_ref[4:5, at] = jnp.sum(grad_mixed * back_two, axis=0, keepdims=True)
        grad_gated = (
            taps[0] * grad_mixed
            + taps[1] * ahead_rows(grad_mixed * same_one, 1)
            + taps[2] * ahead_rows(grad_mixed * same_two, 2)
        )
        for k, v in enumerate((grad_gated * x_part, grad_scaled * mixed, grad_gated * b_part)):
            proj_ref[:, pl.ds(k * width + q * step, step)] = v.astype(LINK)
        return carry

    for q in range(width // step):
        chunk(q, 0)
    sums_ref[5:8, :] = jnp.zeros((3, width), F32)


def mixer_grads_kernel(
    rows, order, where_ref, normed_ref, proj_ref, branch_ref, scaled_ref, *refs
):
    low, place = where_ref[0], where_ref[1]
    outs, (total_ref, held_ref, sems) = refs[:8], refs[8:]
    in_half = proj_ref.shape[1] // 8
    out_half = scaled_ref.shape[1] // 8
    for n in range(4):
        i, half = n // 2, n % 2
        block = 2 * lax.bitwise_xor(place, order[i]) + half
        in_at = pl.ds(pl.multiple_of(block * in_half, PAD), in_half)
        out_at = pl.ds(pl.multiple_of(block * out_half, PAD), out_half)
        total_ref[:, :in_half] = dot_rows(normed_ref[...], proj_ref[:, in_at])
        total_ref[:, in_half:] = dot_rows(branch_ref[...], scaled_ref[:, out_at])

        def copy(h, carry, n=n):
            to = pl.ds(pl.multiple_of(h * rows, rows), rows)
            for k, bit in enumerate((low, 1 - low)):
                at = pl.ds(pl.multiple_of((2 * h + bit) * rows, rows), rows)
                held_ref[2 * n + k, to, :] = total_ref[at, :].astype(LINK)
            return carry

        lax.fori_loop(0, held_ref.shape[1] // rows, copy, 0)
        for k in (2 * n, 2 * n + 1):
            pltpu.make_async_copy(held_ref.at[k], outs[k], sems.at[k]).start()
    for k in range(8):
        pltpu.make_async_copy(held_ref.at[k], outs[k], sems.at[k]).wait()


def final_kernel(where_ref, own_ref, *refs):
    gots, (in_ref, outw_ref, one_ref, two_ref, taps_ref) = refs[:-5], refs[-5:]
    in_half, out_half = in_ref.shape[1] // 2, outw_ref.shape[1] // 2
    cut = in_half + out_half

    def total(start, size):
        v = own_ref[:, start : start + size]
        for ref in gots:
            v = v + ref[:, start : start + size].astype(F32)
        return v

    for k in range(2):
        in_ref[:, k * in_half : (k + 1) * in_half] = total(k * cut, in_half)
        outw_ref[:, k * out_half : (k + 1) * out_half] = total(k * cut + in_half, out_half)
    small = total(2 * cut, PAD)
    turned = small.T
    one_ref[...] = turned[0:1]
    two_ref[...] = turned[1:2]
    taps_ref[...] = small[:, 2:5]


def join_kernel(where_ref, *refs):
    for k in range(2):
        a, b, c = (r[...].astype(F32) for r in refs[3 * k : 3 * k + 3])
        refs[6 + k][...] = (a + b + c).astype(LINK)


def add_kernel(where_ref, *refs):
    n = len(refs) // 3
    for a, b, c in zip(refs[:n], refs[n : 2 * n], refs[2 * n :]):
        c[...] = (a[...].astype(F32) + b[...].astype(F32)).astype(c.dtype)


def last_kernel(
    rows, where_ref, a_ref, a_got_ref, a_far_ref, a_row_ref, b_ref, b_got_ref, b_row_ref, b_far_ref, small_ref, *refs
):
    low, high = where_ref[0], where_ref[2]
    cut = a_ref.shape[1]
    own_ref, sends, turned_ref = refs[0], refs[1:-1], refs[-1]
    width = turned_ref.shape[0]
    turned_ref[...] = jnp.concatenate(
        [small_ref[...], jnp.zeros((PAD - 8, width), F32)], axis=0
    ).T

    def total(at, *parts):
        v = parts[0][at, :].astype(F32)
        for p in parts[1:]:
            v = v + p[at, :].astype(F32)
        return v

    for s, ref in enumerate((own_ref, *sends)):
        spot = high + s
        spot = jnp.where(spot >= len(sends) + 1, spot - len(sends) - 1, spot)
        at = pl.ds(pl.multiple_of(spot * rows, rows), rows)
        ref[:, :cut] = total(at, a_ref, a_got_ref, a_far_ref, a_row_ref).astype(ref.dtype)
        ref[:, cut : 2 * cut] = total(at, b_ref, b_got_ref, b_row_ref, b_far_ref).astype(ref.dtype)
        at = pl.ds(pl.multiple_of((2 * spot + low) * rows, rows), rows)
        ref[:, 2 * cut :] = turned_ref[at, :].astype(ref.dtype)


def mixer_input_kernel(
    rows,
    where_ref,
    tokens_ref,
    hidden_grad_ref,
    gains_ref,
    sums_ref,
    proj_ref,
    in_ref,
    input_ref,
    small_ref,
    grad_ref,
):
    width = tokens_ref.shape[1]
    step = 256
    inputs = tokens_ref[...].astype(F32)
    inverse = lax.rsqrt(jnp.mean(inputs * inputs, axis=1, keepdims=True) + EPSILON)

    def chunk(q, carry):
        at = pl.ds(q * step, step)
        grad_ref[:, at] = dot_last(proj_ref[...], in_ref[at, :])
        return carry

    for q in range(width // step):
        chunk(q, 0)
    grad = grad_ref[...]
    row = lax.broadcasted_iota(jnp.int32, (8, width), 0)
    gain_grad = jnp.sum(grad * (inputs * inverse), axis=0, keepdims=True)
    small_ref[...] = jnp.where(row == 0, gain_grad, sums_ref[...])
    weighted = grad * gains_ref[0:1, :]
    mean = jnp.mean(weighted * inputs, axis=1, keepdims=True)
    input_ref[...] = hidden_grad_ref[...] + inverse * (
        weighted - inputs * (inverse * inverse * mean)
    )


TILE = 256


def piece_specs(pieces, count, width):
    tiles = count // TILE
    return [
        pl.BlockSpec(
            (TILE, width), lambda t, k=k: (jnp.clip(t - k * tiles, 0, tiles - 1), 0)
        )
        for k in range(pieces)
    ]


def pick(refs, tiles):
    v = refs[0][...]
    for k in range(1, len(refs)):
        v = jnp.where(pl.program_id(0) >= k * tiles, refs[k][...], v)
    return v


def put_piece(refs, tiles, v):
    for k, ref in enumerate(refs):

        @pl.when((pl.program_id(0) >= k * tiles) & (pl.program_id(0) < (k + 1) * tiles))
        def _(ref=ref):
            ref[...] = v.astype(ref.dtype)


def whole_spec(v):
    return pl.BlockSpec(v.shape, lambda t: (0, 0))


def tiled(kernel, grid, in_specs, args, out_specs, outs, flops, limit=56, scratch=()):
    moved = sum(a.size * a.dtype.itemsize for a in args) + sum(
        o.size * jnp.dtype(o.dtype).itemsize for o in outs
    )
    return pl.pallas_call(
        kernel,
        grid=(grid,),
        in_specs=in_specs,
        out_specs=out_specs,
        out_shape=outs,
        scratch_shapes=list(scratch),
        compiler_params=pltpu.CompilerParams(vmem_limit_bytes=limit * MIB),
        cost_estimate=pl.CostEstimate(flops=flops, bytes_accessed=moved, transcendentals=0),
    )(*args)


def act_kernel(tiles, rows, where_ref, *refs):
    pieces, woven, (act_ref, silu_ref, slope_ref, gate_ref, up_ref) = refs[:4], refs[4:8], refs[8:]

    @pl.when(pl.program_id(0) == 0)
    def _():
        for k, whole_ref in enumerate((gate_ref, up_ref)):

            def put(to, at, ref, whole_ref=whole_ref):
                whole_ref[to, :] = ref[at, :]

            natural(where_ref[0], *woven[2 * k : 2 * k + 2], put, rows, woven[0].shape[0] // rows)

    normed = pick(pieces, tiles)
    gate = dot_plain(normed, gate_ref[...])
    up = dot_plain(normed, up_ref[...])
    sigmoid = 1.0 / (1.0 + jnp.exp(-gate))
    silu = gate * sigmoid
    act_ref[...] = (silu * up).astype(LINK)
    silu_ref[...] = silu.astype(LINK)
    slope_ref[...] = (up * (sigmoid + silu * (1.0 - sigmoid))).astype(LINK)


def act_call(rows, scalars, pieces, woven):
    count, width = pieces[0].shape
    inner = woven[0].shape[1]
    tiles = count // TILE
    wide = pl.BlockSpec((TILE, inner), lambda t: (t, 0))
    weight = shape((width, inner), LINK)
    return tiled(
        functools.partial(act_kernel, tiles, rows),
        4 * tiles,
        [SCALARS] + piece_specs(4, count, width) + [whole_spec(v) for v in woven],
        [scalars, *pieces, *woven],
        [wide] * 3 + [whole_spec(weight)] * 2,
        [shape((4 * count, inner), LINK)] * 3 + [weight] * 2,
        16 * count * width * inner,
    )


def back_kernel(pieces, tiles, with_got, *refs):
    cots, refs = refs[:pieces], refs[pieces:]
    silu_ref, slope_ref, gate_ref, up_ref, down_ref = refs[:5]
    refs = refs[5:]
    if with_got:
        got_ref, refs = refs[0], refs[1:]
    grad_gate_ref, grad_up_ref = refs[:2]
    grad_act = dot_plain(pick(cots, tiles), down_ref[...])
    grad_up_ref[...] = (grad_act * silu_ref[...].astype(F32)).astype(LINK)
    grad_gate_ref[...] = (grad_act * slope_ref[...].astype(F32)).astype(LINK)
    back = dot_last(grad_gate_ref[...], gate_ref[...]) + dot_last(grad_up_ref[...], up_ref[...])
    if with_got:
        back = back + got_ref[...].astype(F32)
    put_piece(refs[2:], tiles, back)


def back_call(start, cots, silu, slope, gate, up, down, got=None):
    count, width = cots[0].shape
    inner = gate.shape[1]
    tiles, pieces = count // TILE, len(cots)
    wide_in = pl.BlockSpec((TILE, inner), lambda t: (t + start * tiles, 0))
    wide = pl.BlockSpec((TILE, inner), lambda t: (t, 0))
    thin = piece_specs(pieces, count, width)
    extra = [] if got is None else [got]
    return tiled(
        functools.partial(back_kernel, pieces, tiles, got is not None),
        pieces * tiles,
        thin + [wide_in] * 2 + [whole_spec(gate)] * 3 + thin[: len(extra)],
        [*cots, silu, slope, gate, up, down, *extra],
        [wide] * 2 + thin,
        [shape((pieces * count, inner), LINK)] * 2 + [shape((count, width), LINK)] * pieces,
        6 * pieces * count * width * inner,
    )


def out_kernel(tiles, skip, act_ref, down_ref, *refs):
    put_piece(refs[skip:], tiles, dot_last(act_ref[...], down_ref[...]))


def out_call(act, down, count, deps):
    width, inner = down.shape
    tiles = count // TILE
    return tiled(
        functools.partial(out_kernel, tiles, len(deps)),
        4 * tiles,
        [pl.BlockSpec((TILE, inner), lambda t: (t, 0)), whole_spec(down)] + [APART] * len(deps),
        [act, down, *deps],
        piece_specs(4, count, width),
        [shape((count, width), LINK)] * 4,
        8 * count * width * inner,
    )


def weight_grad_kernel(rows, spots, whole, where_ref, *refs):
    lefts, refs = refs[:4], refs[4:]
    low = where_ref[0]
    count = lefts[0].shape[0]
    at = pl.ds(pl.multiple_of(pl.program_id(0) * TILE, TILE), TILE)
    total = None
    for left, (k, start) in zip(lefts, spots):
        v = dot_rows(left[:, at], refs[k][start * count : (start + 1) * count, :])
        total = v if total is None else total + v
    if whole:
        refs[-1][...] = total.astype(LINK)
        return
    near_ref, away_ref, total_ref = refs[-3:]
    total_ref[...] = total
    for h in range(near_ref.shape[0] // rows):
        to = pl.ds(h * rows, rows)
        for ref, bit in ((near_ref, low), (away_ref, 1 - low)):
            at = pl.ds(pl.multiple_of((2 * h + bit) * rows, rows), rows)
            ref[to, :] = total_ref[at, :].astype(ref.dtype)


def pair_grad_kernel(rows, spots, where_ref, *refs):
    lefts, gates, ups = refs[:4], refs[4:7], refs[7:10]
    near_ref, away_ref, up_ref, total_ref = refs[10:]
    low = where_ref[0]
    count = lefts[0].shape[0]
    at = pl.ds(pl.multiple_of(pl.program_id(0) * TILE, TILE), TILE)

    def total(rights):
        v = None
        for left, (k, start) in zip(lefts, spots):
            part = dot_rows(left[:, at], rights[k][start * count : (start + 1) * count, :])
            v = part if v is None else v + part
        return v

    up_ref[...] = total(ups).astype(LINK)
    total_ref[...] = total(gates)
    for h in range(near_ref.shape[0] // rows):
        to = pl.ds(h * rows, rows)
        for ref, bit in ((near_ref, low), (away_ref, 1 - low)):
            at_rows = pl.ds(pl.multiple_of((2 * h + bit) * rows, rows), rows)
            ref[to, :] = total_ref[at_rows, :].astype(ref.dtype)


def pair_grad(rows, scalars, lefts, gates, ups, spots):
    count, width = lefts[0].shape
    inner = gates[0].shape[1]
    half = pl.BlockSpec((TILE // 2, inner), lambda t: (t, 0))
    args = [*lefts, *gates, *ups]
    return tiled(
        functools.partial(pair_grad_kernel, rows, spots),
        width // TILE,
        [SCALARS] + [whole_spec(v) for v in args],
        [scalars, *args],
        [half, half, pl.BlockSpec((TILE, inner), lambda t: (t, 0))],
        [
            shape((width // 2, inner), F32),
            shape((width // 2, inner), LINK),
            shape((width, inner), LINK),
        ],
        16 * count * width * inner,
        scratch=[pltpu.VMEM((TILE, inner), F32)],
    )


def weight_grad(rows, scalars, lefts, rights, spots, whole=False):
    count, width = lefts[0].shape
    inner = rights[0].shape[1]
    half = pl.BlockSpec((TILE // 2, inner), lambda t: (t, 0))
    return tiled(
        functools.partial(weight_grad_kernel, rows, spots, whole),
        width // TILE,
        [SCALARS] + [whole_spec(v) for v in (*lefts, *rights)],
        [scalars, *lefts, *rights],
        [pl.BlockSpec((TILE, inner), lambda t: (t, 0))] if whole else [half, half],
        [shape((width, inner), LINK)]
        if whole
        else [shape((width // 2, inner), F32), shape((width // 2, inner), LINK)],
        8 * count * width * inner,
        scratch=[] if whole else [pltpu.VMEM((TILE, inner), F32)],
    )


def body(
    tokens,
    segments,
    mixer_gain,
    in_weight,
    conv_kernel,
    out_weight,
    ffn_gain,
    gate_weight,
    up_weight,
    down_weight,
    cotangent,
):
    count, width = tokens.shape
    rows = in_weight.shape[0]
    in_cols, out_cols = in_weight.shape[1], out_weight.shape[1]
    cut = (in_cols + out_cols) // 2
    ways = width // rows
    half = ways // 2
    columns = lax.axis_size("dp")
    place = lax.axis_index("dp")
    low = lax.rem(lax.axis_index("fsdp"), 2)
    high = lax.axis_index("fsdp") // 2
    scalars = jnp.stack([low, place, high]).astype(jnp.int32)
    strides = [[2 * h + bit for h in range(half)] for bit in range(2)]

    def swap_row(v):
        return lax.ppermute(v, "fsdp", [(i, i ^ 1) for i in range(ways)])

    def swap_far(v):
        return lax.ppermute(v, "dp", [(i, i ^ 2) for i in range(columns)])

    def swap_core(v):
        return lax.ppermute(v, "dp", [(i, i ^ 1) for i in range(columns)])

    def shift_high(v, s):
        return lax.ppermute(v, "fsdp", [(i, (i + 2 * s) % ways) for i in range(ways)])

    def gather_high(v):
        return lax.all_gather(v, "fsdp", axis=0, tiled=True, axis_index_groups=strides)

    def scatter_high(v):
        return lax.psum_scatter(
            v, "fsdp", scatter_dimension=0, tiled=True, axis_index_groups=strides
        )

    (packed,) = call(
        pack_kernel,
        scalars,
        [in_weight, out_weight, mixer_gain[None, :], ffn_gain[None, :], conv_kernel],
        [shape((rows, 2 * cut + PAD), LINK)],
    )
    shifts = [packed] + [shift_high(packed, s) for s in range(1, half)]
    tall = half * rows
    down_other = swap_row(after(down_weight, packed))
    down_pair = jnp.where(
        low == 0,
        jnp.concatenate([down_weight, down_other], axis=0),
        jnp.concatenate([down_other, down_weight], axis=0),
    )
    shifts[0] = after(shifts[0], down_pair)
    first, second, small_near = call(
        merge_kernel,
        scalars,
        shifts,
        [shape((tall, cut), LINK), shape((tall, cut), LINK), shape((tall, PAD), LINK)],
    )
    gate_near = gather_high(after(gate_weight, first))
    up_near = gather_high(after(up_weight, first))
    down_all = gather_high(after(down_pair, first))
    first_row = swap_row(first)
    second_far = swap_far(second)
    small_away = swap_row(small_near)
    second_row = swap_row(second)
    first_far = swap_far(first)
    second_far_row = swap_row(second_far)
    first_row_far = swap_far(first_row)
    cot_far = swap_far(after(cotangent, first_row_far))
    chip = [[[first, first_row], [first_far, first_row_far]], [[second, second_row], [second_far, second_far_row]]]
    pieces = []
    for k in range(2):
        other = [[swap_core(v) for v in pair] for pair in chip[k]]
        for pair in (chip[k][0], other[0], chip[k][1], other[1]):
            pieces += pair
    pieces[0] = after(pieces[0], gate_near, small_away)
    gate_row = swap_row(gate_near)
    up_row = swap_row(up_near)

    def gather_tokens(v, far):
        return [v, swap_core(v), far, swap_core(far)]

    cots = gather_tokens(cotangent, cot_far)

    seg_ids = segments[0]
    zero = jnp.zeros((2,), F32)
    same = jnp.stack(
        [
            jnp.concatenate([zero[:1], (seg_ids[1:] == seg_ids[:-1]).astype(F32)]),
            jnp.concatenate([zero, (seg_ids[2:] == seg_ids[:-2]).astype(F32)]),
        ],
        axis=1,
    )
    normed, parts, scaled, hidden, normed_two, gains, in_all, outw_all = call(
        functools.partial(mixer_kernel, rows),
        scalars,
        [tokens, same, small_near, small_away, *pieces],
        [
            shape((count, width), LINK),
            shape((3, count, width), F32),
            shape((count, width), LINK),
            shape((count, width), F32),
            shape((count, width), LINK),
            shape((8, width), F32),
            shape((width, columns * in_cols), LINK),
            shape((width, columns * out_cols), LINK),
        ],
        apart=2,
        flops=8 * count * width * width,
        scratch=[
            pltpu.VMEM((width, PAD), F32),
            pltpu.VMEM((width, columns * in_cols), LINK),
            pltpu.VMEM((width, columns * out_cols), LINK),
            pltpu.SemaphoreType.DMA,
            pltpu.SemaphoreType.DMA,
        ],
        limit=56,
    )

    normed_two = after(normed_two, up_near, cot_far, gate_row)
    normeds = gather_tokens(normed_two, swap_far(normed_two))
    act, silu, slope, gate_all, up_all = act_call(
        rows, scalars, normeds, [gate_near, gate_row, up_near, up_row]
    )

    def add(*pairs):
        return call(
            add_kernel,
            scalars,
            [p[0] for p in pairs] + [p[1] for p in pairs],
            [shape(p[0].shape, LINK) for p in pairs],
        )

    def join(near, away_got):
        return call(add_kernel, scalars, [near, away_got], [shape(near.shape, LINK)])[0]

    weights = (silu, slope, gate_all, up_all, down_all)
    gate_xc, up_xc, back_xc = back_call(3, [cots[3]], *weights)
    down_near, down_away = weight_grad(
        rows,
        scalars,
        [after(cots[0], back_xc), *cots[1:]],
        [act],
        [(0, 0), (0, 1), (0, 2), (0, 3)],
    )
    gate_x, up_x, back_far = back_call(
        2, [after(cots[2], down_away)], *weights, got=swap_core(back_xc)
    )
    gate_o, up_o, back_own, back_c = back_call(
        0, [after(cots[0], back_far), cots[1]], *weights
    )
    down_got = swap_row(down_away)
    back_one = swap_far(back_far[: 3 * count // 4])
    back_two = swap_far(back_far[3 * count // 4 :])
    spots = [(0, 0), (0, 1), (1, 0), (2, 0)]
    down_sum = join(down_near, down_got)
    gate_near_grad, gate_away, up_whole = pair_grad(
        rows,
        scalars,
        [after(normeds[0], down_sum, back_one), *normeds[1:]],
        [gate_o, gate_x, gate_xc],
        [up_o, up_x, up_xc],
        spots,
    )
    up_pair = scatter_high(up_whole).reshape(2, rows, -1)
    up_mine = jnp.where(low == 0, up_pair[0], up_pair[1])
    up_other = jnp.where(low == 0, up_pair[1], up_pair[0])
    grad_down = scatter_high(down_sum).astype(F32)
    gate_one = swap_row(gate_away[: tall // 2])
    gate_two = swap_row(gate_away[tall // 2 :])

    hidden_grad, branch, proj, sums = call(
        mixer_back_kernel,
        scalars,
        [after(back_own, gate_away), swap_core(back_c), back_one, back_two, hidden, cotangent, same, gains, parts, outw_all],
        [
            shape((count, width), F32),
            shape((count, width), LINK),
            shape((count, 3 * width), LINK),
            shape((8, width), F32),
        ],
        flops=2 * count * width * width,
        limit=48,
    )

    def mixer_grads(order, first_arg):
        return call(
            functools.partial(mixer_grads_kernel, rows, order),
            scalars,
            [first_arg, proj, branch, scaled],
            [shape((tall, cut), LINK)] * 8,
            flops=4 * count * width * width,
            scratch=[
                pltpu.VMEM((width, cut), F32),
                pltpu.VMEM((8, tall, cut), LINK),
                pltpu.SemaphoreType.DMA((8,)),
            ],
            apart=8,
        )

    input_grad, sums = call(
        functools.partial(mixer_input_kernel, rows),
        scalars,
        [tokens, hidden_grad, gains, sums, proj, in_all],
        [shape((count, width), F32), shape((8, width), F32)],
        flops=6 * count * width * width,
        scratch=[pltpu.VMEM((count, width), F32)],
    )
    sums_core = sums + swap_core(sums)
    sums_far = sums_core + swap_far(sums_core)
    send = mixer_grads((1, 3), after(normed, gate_one, input_grad))
    got = [swap_core(v) for v in send]
    mine = mixer_grads((0, 2), after(normed, send[0], sums_core))
    mine = [*mine[:5], after(mine[5], sums_far), *mine[6:]]
    a_away_far, b_away_far, a_near_far, b_away_own = add(
        *((after(mine[k], gate_two), got[k]) for k in (5, 7, 4, 3))
    )
    a_away_got = swap_far(a_away_far)
    b_away_got = swap_row(b_away_far)
    a_near_got = swap_far(a_near_far)
    b_own_got = swap_row(b_away_own)

    out_own, out_c, out_x, out_xc = out_call(after(act, a_near_far), down_all, count, [up_pair])
    gate_got = jnp.concatenate([gate_one, gate_two], axis=0)
    gate_sum = join(after(gate_near_grad, out_own), gate_got)
    grad_gate = scatter_high(gate_sum).astype(F32)
    a_away, b_far = call(
        join_kernel,
        scalars,
        [mine[1], got[1], a_away_got, mine[6], got[6], b_away_got],
        [shape((tall, cut), LINK)] * 2,
        deps=[out_own, a_near_got, b_own_got],
    )
    own, *sends = call(
        functools.partial(last_kernel, rows),
        scalars,
        [
            mine[0],
            got[0],
            a_near_got,
            swap_row(a_away),
            mine[2],
            got[2],
            b_own_got,
            swap_far(b_far),
            sums_far + swap_row(sums_far),
        ],
        [shape((rows, 2 * cut + PAD), F32)] + [shape((rows, 2 * cut + PAD), LINK)] * (half - 1),
        scratch=[pltpu.VMEM((width, PAD), F32)],
        deps=[gate_sum],
    )
    gots = [shift_high(sends[s - 1], s) for s in range(1, half)]
    (out_far,) = add((after(out_x, own), swap_core(out_xc)))
    out_got, out_got_far = swap_core(out_c), swap_far(out_far)
    up_row = swap_row(after(up_other, own))
    grad_up = up_mine.astype(F32) + up_row.astype(F32)
    grad_in, grad_outw, one_grad, two_grad, taps_grad = call(
        final_kernel,
        scalars,
        [own, *gots],
        [
            shape((rows, in_cols), F32),
            shape((rows, out_cols), F32),
            shape((1, rows), F32),
            shape((1, rows), F32),
            shape((rows, 3), F32),
        ],
        deps=[grad_up, grad_gate, grad_down],
    )
    result = (
        hidden + (out_own.astype(F32) + out_got.astype(F32) + out_got_far.astype(F32))
    ).astype(LINK)
    return (
        result,
        input_grad,
        one_grad[0],
        grad_in,
        taps_grad,
        grad_outw,
        two_grad[0],
        grad_gate,
        grad_up,
        grad_down,
    )


def solution(mesh):
    rows_spec, cols_spec = P(("dp", "fsdp"), None), P("fsdp", "dp")
    gain_spec, taps_spec = P("fsdp"), P("fsdp", None)
    return jax.shard_map(
        body,
        mesh=mesh,
        in_specs=(
            rows_spec,
            rows_spec,
            gain_spec,
            cols_spec,
            taps_spec,
            cols_spec,
            gain_spec,
            cols_spec,
            cols_spec,
            cols_spec,
            rows_spec,
        ),
        out_specs=(
            rows_spec,
            rows_spec,
            gain_spec,
            cols_spec,
            taps_spec,
            cols_spec,
            gain_spec,
            cols_spec,
            cols_spec,
            cols_spec,
        ),
        check_vma=False,
    )
```

```python
import functools

import jax
import jax.numpy as jnp
from jax import lax
from jax.experimental import pallas as pl
from jax.experimental.pallas import tpu as pltpu
from jax.sharding import PartitionSpec as P

EPSILON = 1e-05
LINK = jnp.bfloat16
F32 = jnp.float32
PAD = 128
MIB = 1 << 20


def dot_plain(left, right):
    return jnp.dot(left, right, preferred_element_type=F32)


def dot_rows(left, right):
    return lax.dot_general(left, right, (((0,), (0,)), ((), ())), preferred_element_type=F32)


def dot_last(left, right):
    return lax.dot_general(left, right, (((1,), (1,)), ((), ())), preferred_element_type=F32)


def after(v, *others):
    return lax.optimization_barrier((v, *others))[0]


def shape(dims, dtype):
    return jax.ShapeDtypeStruct(dims, dtype)


SCALARS = pl.BlockSpec(memory_space=pltpu.SMEM)
WHOLE = pl.BlockSpec(memory_space=pltpu.VMEM)
APART = pl.BlockSpec(memory_space=pl.ANY)


def call(kernel, scalars, args, outs, flops=0, limit=40, scratch=(), apart=0, deps=()):
    moved = sum(a.size * a.dtype.itemsize for a in args) + sum(
        o.size * jnp.dtype(o.dtype).itemsize for o in outs
    )
    first, last = 1 + len(args), 1 + len(args) + len(deps)

    def run(*refs):
        kernel(*refs[:first], *refs[last:])

    return pl.pallas_call(
        run,
        out_shape=outs,
        in_specs=[SCALARS] + [WHOLE] * len(args) + [APART] * len(deps),
        out_specs=[WHOLE] * (len(outs) - apart) + [APART] * apart,
        scratch_shapes=list(scratch),
        compiler_params=pltpu.CompilerParams(vmem_limit_bytes=limit * MIB),
        cost_estimate=pl.CostEstimate(flops=flops, bytes_accessed=moved, transcendentals=0),
    )(scalars, *args, *deps)


def pack_kernel(where_ref, in_ref, out_ref, one_ref, two_ref, taps_ref, packed_ref):
    rows = in_ref.shape[0]
    in_half, out_half = in_ref.shape[1] // 2, out_ref.shape[1] // 2
    cut = in_half + out_half
    packed_ref[:, :in_half] = in_ref[:, :in_half]
    packed_ref[:, in_half:cut] = out_ref[:, :out_half]
    packed_ref[:, cut : cut + in_half] = in_ref[:, in_half:]
    packed_ref[:, cut + in_half : 2 * cut] = out_ref[:, out_half:]
    eye = lax.broadcasted_iota(jnp.int32, (rows, rows), 0) == lax.broadcasted_iota(
        jnp.int32, (rows, rows), 1
    )
    lane = lax.broadcasted_iota(jnp.int32, (rows, PAD), 1)
    small = jnp.zeros((rows, PAD), F32)
    for k, ref in enumerate((one_ref, two_ref)):
        column = jnp.sum(jnp.where(eye, ref[...].astype(F32), 0.0), axis=1, keepdims=True)
        small = jnp.where(lane == k, column, small)
    for k in range(3):
        small = jnp.where(lane == 2 + k, taps_ref[:, k : k + 1].astype(F32), small)
    packed_ref[:, 2 * cut :] = small.astype(LINK)


def merge_kernel(where_ref, *refs):
    pieces, (first_ref, second_ref, small_ref) = refs[:-3], refs[-3:]
    rows = pieces[0].shape[0]
    high = where_ref[2]
    cut = first_ref.shape[1]
    for s, piece in enumerate(pieces):
        spot = high - s
        spot = jnp.where(spot < 0, spot + len(pieces), spot)
        at = pl.ds(pl.multiple_of(spot * rows, rows), rows)
        first_ref[at, :] = piece[:, :cut]
        second_ref[at, :] = piece[:, cut : 2 * cut]
        small_ref[at, :] = piece[:, 2 * cut :]


def natural(low, near, away, put, rows, blocks):
    def one(h, carry):
        at = pl.ds(pl.multiple_of(h * rows, rows), rows)
        put(pl.ds(pl.multiple_of((2 * h + low) * rows, rows), rows), at, near)
        put(pl.ds(pl.multiple_of((2 * h + 1 - low) * rows, rows), rows), at, away)
        return carry

    lax.fori_loop(0, blocks, one, 0)


def mixer_weights_kernel(rows, where_ref, *refs):
    pieces, (in_ref, out_ref) = refs[:16], refs[16:18]
    low, place = where_ref[0], where_ref[1]
    in_half, out_half = in_ref.shape[1] // 8, out_ref.shape[1] // 8
    for k in range(8):
        half, r = k // 4, k % 4
        block = lax.bitwise_xor(place, r)
        in_at = pl.ds(pl.multiple_of((2 * block + half) * in_half, PAD), in_half)
        out_at = pl.ds(pl.multiple_of((2 * block + half) * out_half, PAD), out_half)

        def put(to, at, ref):
            in_ref[to, in_at] = ref[at, :in_half]
            out_ref[to, out_at] = ref[at, in_half:]

        natural(low, pieces[2 * k], pieces[2 * k + 1], put, rows, pieces[0].shape[0] // rows)


def back_rows(v, steps):
    return pltpu.roll(v, steps, 0)


def ahead_rows(v, steps):
    return pltpu.roll(v, v.shape[0] - steps, 0)


def small_rows(rows, low, near_ref, away_ref, small_ref):
    def put(to, at, ref):
        small_ref[to, :] = ref[at, :].astype(F32)

    natural(low, near_ref, away_ref, put, rows, near_ref.shape[0] // rows)
    return small_ref[...].T[:8]


def mixer_kernel(
    rows,
    where_ref,
    tokens_ref,
    same_ref,
    near_ref,
    away_ref,
    *refs,
):
    pieces = refs[:16]
    normed_ref, parts_ref, scaled_ref, hidden_ref, next_ref, gains_ref = refs[16:22]
    small_ref, in_ref, outw_ref, in_sem, outw_sem = refs[24:]
    mixer_weights_kernel(rows, where_ref, *pieces, in_ref, outw_ref)
    in_copy = pltpu.make_async_copy(in_ref, refs[22], in_sem)
    outw_copy = pltpu.make_async_copy(outw_ref, refs[23], outw_sem)
    in_copy.start()
    outw_copy.start()
    width = tokens_ref.shape[1]
    step = 256
    gains_ref[...] = small_rows(rows, where_ref[0], near_ref, away_ref, small_ref)
    inputs = tokens_ref[...].astype(F32)
    inverse = lax.rsqrt(jnp.mean(inputs * inputs, axis=1, keepdims=True) + EPSILON)
    normed_ref[...] = (inputs * inverse * gains_ref[0:1, :]).astype(LINK)

    def chunk(q, carry):
        at = pl.ds(q * step, step)

        def part(k):
            w = in_ref[:, pl.ds(k * width + q * step, step)]
            v = dot_plain(normed_ref[...], w)
            parts_ref[k, :, at] = v
            return v

        b_part = part(0)
        x_part = part(2)
        gated = b_part * x_part
        mixed = (
            gains_ref[2:3, at] * gated
            + gains_ref[3:4, at] * (back_rows(gated, 1) * same_ref[:, 0:1])
            + gains_ref[4:5, at] * (back_rows(gated, 2) * same_ref[:, 1:2])
        )
        scaled_ref[:, at] = (part(1) * mixed).astype(LINK)
        return carry

    for q in range(width // step):
        chunk(q, 0)

    def final(q, total):
        at = pl.ds(q * step, step)
        v = tokens_ref[:, at].astype(F32) + dot_last(scaled_ref[...], outw_ref[at, :])
        hidden_ref[:, at] = v
        return total + jnp.sum(v * v, axis=1, keepdims=True)

    total = jnp.zeros((tokens_ref.shape[0], 1), F32)
    for q in range(width // step):
        total = final(q, total)
    inverse_two = lax.rsqrt(total / width + EPSILON)
    next_ref[...] = (hidden_ref[...] * inverse_two * gains_ref[1:2, :]).astype(LINK)
    in_copy.wait()
    outw_copy.wait()


def mixer_back_kernel(
    where_ref,
    own_ref,
    got_ref,
    far_one_ref,
    far_two_ref,
    hidden_ref,
    cot_ref,
    same_ref,
    gains_ref,
    parts_ref,
    outw_ref,
    hidden_grad_ref,
    branch_ref,
    proj_ref,
    sums_ref,
):
    width = hidden_ref.shape[1]
    step = 256
    hidden = hidden_ref[...]
    inverse = lax.rsqrt(jnp.mean(hidden * hidden, axis=1, keepdims=True) + EPSILON)
    far = jnp.concatenate([far_one_ref[...], far_two_ref[...]], axis=0)
    grad = own_ref[...].astype(F32) + got_ref[...].astype(F32) + far.astype(F32)
    sums_ref[0:1, :] = jnp.zeros((1, width), F32)
    sums_ref[1:2, :] = jnp.sum(grad * (hidden * inverse), axis=0, keepdims=True)
    weighted = grad * gains_ref[1:2, :]
    mean = jnp.mean(weighted * hidden, axis=1, keepdims=True)
    total = cot_ref[...].astype(F32) + inverse * (weighted - hidden * (inverse * inverse * mean))
    hidden_grad_ref[...] = total
    branch_ref[...] = total.astype(LINK)

    def chunk(q, carry):
        at = pl.ds(q * step, step)
        grad_scaled = dot_plain(branch_ref[...], outw_ref[:, at])
        b_part, c_part, x_part = (parts_ref[k, :, at] for k in range(3))
        same_one, same_two = same_ref[:, 0:1], same_ref[:, 1:2]
        gated = b_part * x_part
        back_one = back_rows(gated, 1) * same_one
        back_two = back_rows(gated, 2) * same_two
        taps = [gains_ref[2 + k : 3 + k, at] for k in range(3)]
        mixed = taps[0] * gated + taps[1] * back_one + taps[2] * back_two
        grad_mixed = grad_scaled * c_part
        sums_ref[2:3, at] = jnp.sum(grad_mixed * gated, axis=0, keepdims=True)
        sums_ref[3:4, at] = jnp.sum(grad_mixed * back_one, axis=0, keepdims=True)
        sums_ref[4:5, at] = jnp.sum(grad_mixed * back_two, axis=0, keepdims=True)
        grad_gated = (
            taps[0] * grad_mixed
            + taps[1] * ahead_rows(grad_mixed * same_one, 1)
            + taps[2] * ahead_rows(grad_mixed * same_two, 2)
        )
        for k, v in enumerate((grad_gated * x_part, grad_scaled * mixed, grad_gated * b_part)):
            proj_ref[:, pl.ds(k * width + q * step, step)] = v.astype(LINK)
        return carry

    for q in range(width // step):
        chunk(q, 0)
    sums_ref[5:8, :] = jnp.zeros((3, width), F32)


def mixer_grads_kernel(
    rows, order, where_ref, normed_ref, proj_ref, branch_ref, scaled_ref, *refs
):
    low, place = where_ref[0], where_ref[1]
    outs, (total_ref, held_ref, sems) = refs[:8], refs[8:]
    in_half = proj_ref.shape[1] // 8
    out_half = scaled_ref.shape[1] // 8
    for n in range(4):
        i, half = n // 2, n % 2
        block = 2 * lax.bitwise_xor(place, order[i]) + half
        in_at = pl.ds(pl.multiple_of(block * in_half, PAD), in_half)
        out_at = pl.ds(pl.multiple_of(block * out_half, PAD), out_half)
        total_ref[:, :in_half] = dot_rows(normed_ref[...], proj_ref[:, in_at])
        total_ref[:, in_half:] = dot_rows(branch_ref[...], scaled_ref[:, out_at])

        def copy(h, carry, n=n):
            to = pl.ds(pl.multiple_of(h * rows, rows), rows)
            for k, bit in enumerate((low, 1 - low)):
                at = pl.ds(pl.multiple_of((2 * h + bit) * rows, rows), rows)
                held_ref[2 * n + k, to, :] = total_ref[at, :].astype(LINK)
            return carry

        lax.fori_loop(0, held_ref.shape[1] // rows, copy, 0)
        for k in (2 * n, 2 * n + 1):
            pltpu.make_async_copy(held_ref.at[k], outs[k], sems.at[k]).start()
    for k in range(8):
        pltpu.make_async_copy(held_ref.at[k], outs[k], sems.at[k]).wait()


def final_kernel(where_ref, own_ref, *refs):
    gots, (in_ref, outw_ref, one_ref, two_ref, taps_ref) = refs[:-5], refs[-5:]
    in_half, out_half = in_ref.shape[1] // 2, outw_ref.shape[1] // 2
    cut = in_half + out_half

    def total(start, size):
        v = own_ref[:, start : start + size]
        for ref in gots:
            v = v + ref[:, start : start + size].astype(F32)
        return v

    for k in range(2):
        in_ref[:, k * in_half : (k + 1) * in_half] = total(k * cut, in_half)
        outw_ref[:, k * out_half : (k + 1) * out_half] = total(k * cut + in_half, out_half)
    small = total(2 * cut, PAD)
    turned = small.T
    one_ref[...] = turned[0:1]
    two_ref[...] = turned[1:2]
    taps_ref[...] = small[:, 2:5]


def join_kernel(where_ref, *refs):
    a, b, c = (r[...].astype(F32) for r in refs[:3])
    refs[3][...] = (a + b + c).astype(LINK)


def add_kernel(where_ref, *refs):
    n = len(refs) // 3
    for a, b, c in zip(refs[:n], refs[n : 2 * n], refs[2 * n :]):
        c[...] = (a[...].astype(F32) + b[...].astype(F32)).astype(c.dtype)


def last_kernel(
    rows, where_ref, a_ref, a_got_ref, a_far_ref, a_row_ref, b_ref, b_got_ref, b_row_ref, b_far_ref, small_ref, *refs
):
    low, high = where_ref[0], where_ref[2]
    cut = a_ref.shape[1]
    own_ref, sends, turned_ref = refs[0], refs[1:-1], refs[-1]
    width = turned_ref.shape[0]
    turned_ref[...] = jnp.concatenate(
        [small_ref[...], jnp.zeros((PAD - 8, width), F32)], axis=0
    ).T

    def total(at, *parts):
        v = parts[0][at, :].astype(F32)
        for p in parts[1:]:
            v = v + p[at, :].astype(F32)
        return v

    for s, ref in enumerate((own_ref, *sends)):
        spot = high + s
        spot = jnp.where(spot >= len(sends) + 1, spot - len(sends) - 1, spot)
        at = pl.ds(pl.multiple_of(spot * rows, rows), rows)
        ref[:, :cut] = total(at, a_ref, a_got_ref, a_far_ref, a_row_ref).astype(ref.dtype)
        ref[:, cut : 2 * cut] = total(at, b_ref, b_got_ref, b_row_ref, b_far_ref).astype(ref.dtype)
        at = pl.ds(pl.multiple_of((2 * spot + low) * rows, rows), rows)
        ref[:, 2 * cut :] = turned_ref[at, :].astype(ref.dtype)


def mixer_input_kernel(
    rows,
    where_ref,
    tokens_ref,
    hidden_grad_ref,
    gains_ref,
    sums_ref,
    proj_ref,
    in_ref,
    input_ref,
    small_ref,
    grad_ref,
):
    width = tokens_ref.shape[1]
    step = 256
    inputs = tokens_ref[...].astype(F32)
    inverse = lax.rsqrt(jnp.mean(inputs * inputs, axis=1, keepdims=True) + EPSILON)

    def chunk(q, carry):
        at = pl.ds(q * step, step)
        grad_ref[:, at] = dot_last(proj_ref[...], in_ref[at, :])
        return carry

    for q in range(width // step):
        chunk(q, 0)
    grad = grad_ref[...]
    row = lax.broadcasted_iota(jnp.int32, (8, width), 0)
    gain_grad = jnp.sum(grad * (inputs * inverse), axis=0, keepdims=True)
    small_ref[...] = jnp.where(row == 0, gain_grad, sums_ref[...])
    weighted = grad * gains_ref[0:1, :]
    mean = jnp.mean(weighted * inputs, axis=1, keepdims=True)
    input_ref[...] = hidden_grad_ref[...] + inverse * (
        weighted - inputs * (inverse * inverse * mean)
    )


TILE = 256


def piece_specs(pieces, count, width):
    tiles = count // TILE
    return [
        pl.BlockSpec(
            (TILE, width), lambda t, k=k: (jnp.clip(t - k * tiles, 0, tiles - 1), 0)
        )
        for k in range(pieces)
    ]


def pick(refs, tiles):
    v = refs[0][...]
    for k in range(1, len(refs)):
        v = jnp.where(pl.program_id(0) >= k * tiles, refs[k][...], v)
    return v


def put_piece(refs, tiles, v):
    for k, ref in enumerate(refs):

        @pl.when((pl.program_id(0) >= k * tiles) & (pl.program_id(0) < (k + 1) * tiles))
        def _(ref=ref):
            ref[...] = v.astype(ref.dtype)


def whole_spec(v):
    return pl.BlockSpec(v.shape, lambda t: (0, 0))


def tiled(kernel, grid, in_specs, args, out_specs, outs, flops, limit=56, scratch=()):
    moved = sum(a.size * a.dtype.itemsize for a in args) + sum(
        o.size * jnp.dtype(o.dtype).itemsize for o in outs
    )
    return pl.pallas_call(
        kernel,
        grid=(grid,),
        in_specs=in_specs,
        out_specs=out_specs,
        out_shape=outs,
        scratch_shapes=list(scratch),
        compiler_params=pltpu.CompilerParams(vmem_limit_bytes=limit * MIB),
        cost_estimate=pl.CostEstimate(flops=flops, bytes_accessed=moved, transcendentals=0),
    )(*args)


def act_kernel(tiles, rows, where_ref, *refs):
    pieces, woven, (act_ref, silu_ref, slope_ref, gate_ref, up_ref) = refs[:4], refs[4:8], refs[8:]

    @pl.when(pl.program_id(0) == 0)
    def _():
        for k, whole_ref in enumerate((gate_ref, up_ref)):

            def put(to, at, ref, whole_ref=whole_ref):
                whole_ref[to, :] = ref[at, :]

            natural(where_ref[0], *woven[2 * k : 2 * k + 2], put, rows, woven[0].shape[0] // rows)

    normed = pick(pieces, tiles)
    gate = dot_plain(normed, gate_ref[...])
    up = dot_plain(normed, up_ref[...])
    sigmoid = 1.0 / (1.0 + jnp.exp(-gate))
    silu = gate * sigmoid
    act_ref[...] = (silu * up).astype(LINK)
    silu_ref[...] = silu.astype(LINK)
    slope_ref[...] = (up * (sigmoid + silu * (1.0 - sigmoid))).astype(LINK)


def act_call(rows, scalars, pieces, woven):
    count, width = pieces[0].shape
    inner = woven[0].shape[1]
    tiles = count // TILE
    wide = pl.BlockSpec((TILE, inner), lambda t: (t, 0))
    weight = shape((width, inner), LINK)
    return tiled(
        functools.partial(act_kernel, tiles, rows),
        4 * tiles,
        [SCALARS] + piece_specs(4, count, width) + [whole_spec(v) for v in woven],
        [scalars, *pieces, *woven],
        [wide] * 3 + [whole_spec(weight)] * 2,
        [shape((4 * count, inner), LINK)] * 3 + [weight] * 2,
        16 * count * width * inner,
    )


def back_kernel(pieces, tiles, with_got, *refs):
    cots, refs = refs[:pieces], refs[pieces:]
    silu_ref, slope_ref, gate_ref, up_ref, down_ref = refs[:5]
    refs = refs[5:]
    if with_got:
        got_ref, refs = refs[0], refs[1:]
    grad_gate_ref, grad_up_ref = refs[:2]
    grad_act = dot_plain(pick(cots, tiles), down_ref[...])
    grad_up_ref[...] = (grad_act * silu_ref[...].astype(F32)).astype(LINK)
    grad_gate_ref[...] = (grad_act * slope_ref[...].astype(F32)).astype(LINK)
    back = dot_last(grad_gate_ref[...], gate_ref[...]) + dot_last(grad_up_ref[...], up_ref[...])
    if with_got:
        back = back + got_ref[...].astype(F32)
    put_piece(refs[2:], tiles, back)


def back_call(start, cots, silu, slope, gate, up, down, got=None):
    count, width = cots[0].shape
    inner = gate.shape[1]
    tiles, pieces = count // TILE, len(cots)
    wide_in = pl.BlockSpec((TILE, inner), lambda t: (t + start * tiles, 0))
    wide = pl.BlockSpec((TILE, inner), lambda t: (t, 0))
    thin = piece_specs(pieces, count, width)
    extra = [] if got is None else [got]
    return tiled(
        functools.partial(back_kernel, pieces, tiles, got is not None),
        pieces * tiles,
        thin + [wide_in] * 2 + [whole_spec(gate)] * 3 + thin[: len(extra)],
        [*cots, silu, slope, gate, up, down, *extra],
        [wide] * 2 + thin,
        [shape((pieces * count, inner), LINK)] * 2 + [shape((count, width), LINK)] * pieces,
        6 * pieces * count * width * inner,
    )


def out_kernel(tiles, skip, act_ref, down_ref, *refs):
    put_piece(refs[skip:], tiles, dot_last(act_ref[...], down_ref[...]))


def out_call(act, down, count, deps):
    width, inner = down.shape
    tiles = count // TILE
    return tiled(
        functools.partial(out_kernel, tiles, len(deps)),
        4 * tiles,
        [pl.BlockSpec((TILE, inner), lambda t: (t, 0)), whole_spec(down)] + [APART] * len(deps),
        [act, down, *deps],
        piece_specs(4, count, width),
        [shape((count, width), LINK)] * 4,
        8 * count * width * inner,
    )


def weight_grad_kernel(rows, spots, whole, where_ref, *refs):
    lefts, refs = refs[:4], refs[4:]
    low = where_ref[0]
    count = lefts[0].shape[0]
    at = pl.ds(pl.multiple_of(pl.program_id(0) * TILE, TILE), TILE)
    total = None
    for left, (k, start) in zip(lefts, spots):
        v = dot_rows(left[:, at], refs[k][start * count : (start + 1) * count, :])
        total = v if total is None else total + v
    if whole:
        refs[-1][...] = total.astype(LINK)
        return
    near_ref, away_ref, total_ref = refs[-3:]
    total_ref[...] = total
    for h in range(near_ref.shape[0] // rows):
        to = pl.ds(h * rows, rows)
        for ref, bit in ((near_ref, low), (away_ref, 1 - low)):
            at = pl.ds(pl.multiple_of((2 * h + bit) * rows, rows), rows)
            ref[to, :] = total_ref[at, :].astype(ref.dtype)


def pair_grad_kernel(rows, spots, where_ref, *refs):
    lefts, gates, ups = refs[:4], refs[4:7], refs[7:10]
    near_ref, away_ref, up_ref, total_ref = refs[10:]
    low = where_ref[0]
    count = lefts[0].shape[0]
    at = pl.ds(pl.multiple_of(pl.program_id(0) * TILE, TILE), TILE)

    def total(rights):
        v = None
        for left, (k, start) in zip(lefts, spots):
            part = dot_rows(left[:, at], rights[k][start * count : (start + 1) * count, :])
            v = part if v is None else v + part
        return v

    up_ref[...] = total(ups).astype(LINK)
    total_ref[...] = total(gates)
    for h in range(near_ref.shape[0] // rows):
        to = pl.ds(h * rows, rows)
        for ref, bit in ((near_ref, low), (away_ref, 1 - low)):
            at_rows = pl.ds(pl.multiple_of((2 * h + bit) * rows, rows), rows)
            ref[to, :] = total_ref[at_rows, :].astype(ref.dtype)


def pair_grad(rows, scalars, lefts, gates, ups, spots):
    count, width = lefts[0].shape
    inner = gates[0].shape[1]
    half = pl.BlockSpec((TILE // 2, inner), lambda t: (t, 0))
    args = [*lefts, *gates, *ups]
    return tiled(
        functools.partial(pair_grad_kernel, rows, spots),
        width // TILE,
        [SCALARS] + [whole_spec(v) for v in args],
        [scalars, *args],
        [half, half, pl.BlockSpec((TILE, inner), lambda t: (t, 0))],
        [
            shape((width // 2, inner), F32),
            shape((width // 2, inner), LINK),
            shape((width, inner), LINK),
        ],
        16 * count * width * inner,
        scratch=[pltpu.VMEM((TILE, inner), F32)],
    )


def weight_grad(rows, scalars, lefts, rights, spots, whole=False):
    count, width = lefts[0].shape
    inner = rights[0].shape[1]
    half = pl.BlockSpec((TILE // 2, inner), lambda t: (t, 0))
    return tiled(
        functools.partial(weight_grad_kernel, rows, spots, whole),
        width // TILE,
        [SCALARS] + [whole_spec(v) for v in (*lefts, *rights)],
        [scalars, *lefts, *rights],
        [pl.BlockSpec((TILE, inner), lambda t: (t, 0))] if whole else [half, half],
        [shape((width, inner), LINK)]
        if whole
        else [shape((width // 2, inner), F32), shape((width // 2, inner), LINK)],
        8 * count * width * inner,
        scratch=[] if whole else [pltpu.VMEM((TILE, inner), F32)],
    )


def body(
    tokens,
    segments,
    mixer_gain,
    in_weight,
    conv_kernel,
    out_weight,
    ffn_gain,
    gate_weight,
    up_weight,
    down_weight,
    cotangent,
):
    count, width = tokens.shape
    rows = in_weight.shape[0]
    in_cols, out_cols = in_weight.shape[1], out_weight.shape[1]
    cut = (in_cols + out_cols) // 2
    ways = width // rows
    half = ways // 2
    columns = lax.axis_size("dp")
    place = lax.axis_index("dp")
    low = lax.rem(lax.axis_index("fsdp"), 2)
    high = lax.axis_index("fsdp") // 2
    scalars = jnp.stack([low, place, high]).astype(jnp.int32)
    strides = [[2 * h + bit for h in range(half)] for bit in range(2)]

    def swap_row(v):
        return lax.ppermute(v, "fsdp", [(i, i ^ 1) for i in range(ways)])

    def swap_far(v):
        return lax.ppermute(v, "dp", [(i, i ^ 2) for i in range(columns)])

    def swap_core(v):
        return lax.ppermute(v, "dp", [(i, i ^ 1) for i in range(columns)])

    def shift_high(v, s):
        return lax.ppermute(v, "fsdp", [(i, (i + 2 * s) % ways) for i in range(ways)])

    def gather_high(v):
        return lax.all_gather(v, "fsdp", axis=0, tiled=True, axis_index_groups=strides)

    def scatter_high(v):
        return lax.psum_scatter(
            v, "fsdp", scatter_dimension=0, tiled=True, axis_index_groups=strides
        )

    (packed,) = call(
        pack_kernel,
        scalars,
        [in_weight, out_weight, mixer_gain[None, :], ffn_gain[None, :], conv_kernel],
        [shape((rows, 2 * cut + PAD), LINK)],
    )
    shifts = [packed] + [shift_high(packed, s) for s in range(1, half)]
    tall = half * rows
    down_other = swap_row(after(down_weight, packed))
    down_pair = jnp.where(
        low == 0,
        jnp.concatenate([down_weight, down_other], axis=0),
        jnp.concatenate([down_other, down_weight], axis=0),
    )
    shifts[0] = after(shifts[0], down_pair)
    first, second, small_near = call(
        merge_kernel,
        scalars,
        shifts,
        [shape((tall, cut), LINK), shape((tall, cut), LINK), shape((tall, PAD), LINK)],
    )
    gate_near = gather_high(after(gate_weight, first))
    up_near = gather_high(after(up_weight, first))
    down_all = gather_high(after(down_pair, first))
    first_row = swap_row(first)
    second_far = swap_far(second)
    small_away = swap_row(small_near)
    second_row = swap_row(second)
    first_far = swap_far(first)
    second_far_row = swap_row(second_far)
    first_row_far = swap_far(first_row)
    cot_far = swap_far(after(cotangent, first_row_far))
    chip = [[[first, first_row], [first_far, first_row_far]], [[second, second_row], [second_far, second_far_row]]]
    pieces = []
    for k in range(2):
        other = [[swap_core(v) for v in pair] for pair in chip[k]]
        for pair in (chip[k][0], other[0], chip[k][1], other[1]):
            pieces += pair
    pieces[0] = after(pieces[0], gate_near, small_away)
    gate_row = swap_row(gate_near)
    up_row = swap_row(up_near)

    def gather_tokens(v, far):
        return [v, swap_core(v), far, swap_core(far)]

    cots = gather_tokens(cotangent, cot_far)

    seg_ids = segments[0]
    zero = jnp.zeros((2,), F32)
    same = jnp.stack(
        [
            jnp.concatenate([zero[:1], (seg_ids[1:] == seg_ids[:-1]).astype(F32)]),
            jnp.concatenate([zero, (seg_ids[2:] == seg_ids[:-2]).astype(F32)]),
        ],
        axis=1,
    )
    normed, parts, scaled, hidden, normed_two, gains, in_all, outw_all = call(
        functools.partial(mixer_kernel, rows),
        scalars,
        [tokens, same, small_near, small_away, *pieces],
        [
            shape((count, width), LINK),
            shape((3, count, width), F32),
            shape((count, width), LINK),
            shape((count, width), F32),
            shape((count, width), LINK),
            shape((8, width), F32),
            shape((width, columns * in_cols), LINK),
            shape((width, columns * out_cols), LINK),
        ],
        apart=2,
        flops=8 * count * width * width,
        scratch=[
            pltpu.VMEM((width, PAD), F32),
            pltpu.VMEM((width, columns * in_cols), LINK),
            pltpu.VMEM((width, columns * out_cols), LINK),
            pltpu.SemaphoreType.DMA,
            pltpu.SemaphoreType.DMA,
        ],
        limit=56,
    )

    normed_two = after(normed_two, up_near, cot_far, gate_row)
    normeds = gather_tokens(normed_two, swap_far(normed_two))
    act, silu, slope, gate_all, up_all = act_call(
        rows, scalars, normeds, [gate_near, gate_row, up_near, up_row]
    )

    def add(*pairs):
        return call(
            add_kernel,
            scalars,
            [p[0] for p in pairs] + [p[1] for p in pairs],
            [shape(p[0].shape, LINK) for p in pairs],
        )

    def join(near, away_got):
        return call(add_kernel, scalars, [near, away_got], [shape(near.shape, LINK)])[0]

    weights = (silu, slope, gate_all, up_all, down_all)
    gate_xc, up_xc, back_xc = back_call(3, [cots[3]], *weights)
    down_near, down_away = weight_grad(
        rows,
        scalars,
        [after(cots[0], back_xc), *cots[1:]],
        [act],
        [(0, 0), (0, 1), (0, 2), (0, 3)],
    )
    gate_x, up_x, back_far = back_call(
        2, [after(cots[2], down_away)], *weights, got=swap_core(back_xc)
    )
    gate_o, up_o, back_own, back_c = back_call(
        0, [after(cots[0], back_far), cots[1]], *weights
    )
    down_got = swap_row(down_away)
    back_one = swap_far(back_far[: 3 * count // 4])
    back_two = swap_far(back_far[3 * count // 4 :])
    spots = [(0, 0), (0, 1), (1, 0), (2, 0)]
    down_sum = join(down_near, down_got)
    gate_near_grad, gate_away, up_whole = pair_grad(
        rows,
        scalars,
        [after(normeds[0], down_sum, back_one), *normeds[1:]],
        [gate_o, gate_x, gate_xc],
        [up_o, up_x, up_xc],
        spots,
    )
    up_pair = scatter_high(up_whole).reshape(2, rows, -1)
    up_mine = jnp.where(low == 0, up_pair[0], up_pair[1])
    up_other = jnp.where(low == 0, up_pair[1], up_pair[0])
    grad_down = scatter_high(down_sum).astype(F32)
    gate_one = swap_row(gate_away[: tall // 2])
    gate_two = swap_row(gate_away[tall // 2 :])

    hidden_grad, branch, proj, sums = call(
        mixer_back_kernel,
        scalars,
        [after(back_own, gate_away), swap_core(back_c), back_one, back_two, hidden, cotangent, same, gains, parts, outw_all],
        [
            shape((count, width), F32),
            shape((count, width), LINK),
            shape((count, 3 * width), LINK),
            shape((8, width), F32),
        ],
        flops=2 * count * width * width,
        limit=48,
    )

    def mixer_grads(order, first_arg):
        return call(
            functools.partial(mixer_grads_kernel, rows, order),
            scalars,
            [first_arg, proj, branch, scaled],
            [shape((tall, cut), LINK)] * 8,
            flops=4 * count * width * width,
            scratch=[
                pltpu.VMEM((width, cut), F32),
                pltpu.VMEM((8, tall, cut), LINK),
                pltpu.SemaphoreType.DMA((8,)),
            ],
            apart=8,
        )

    input_grad, sums = call(
        functools.partial(mixer_input_kernel, rows),
        scalars,
        [tokens, hidden_grad, gains, sums, proj, in_all],
        [shape((count, width), F32), shape((8, width), F32)],
        flops=6 * count * width * width,
        scratch=[pltpu.VMEM((count, width), F32)],
    )
    sums_core = sums + swap_core(sums)
    sums_far = sums_core + swap_far(sums_core)
    send = mixer_grads((1, 3), after(normed, gate_one, input_grad))
    got = [swap_core(v) for v in send]
    mine = mixer_grads((0, 2), after(normed, send[0], sums_core))
    mine = [*mine[:5], after(mine[5], sums_far), *mine[6:]]
    a_away_far, b_away_far, a_near_far, b_away_own = add(
        *((after(mine[k], gate_two), got[k]) for k in (5, 7, 4, 3))
    )
    a_away_got = swap_far(a_away_far)
    b_away_got = swap_row(b_away_far)
    a_near_got = swap_far(a_near_far)
    b_own_got = swap_row(b_away_own)

    out_own, out_c, out_x, out_xc = out_call(after(act, a_near_far), down_all, count, [up_pair])
    (a_away,), (b_far,) = (
        call(join_kernel, scalars, parts, [shape((tall, cut), LINK)], deps=[out_own])
        for parts in ([mine[1], got[1], a_away_got], [mine[6], got[6], b_away_got])
    )
    gate_got = jnp.concatenate([gate_one, gate_two], axis=0)
    (gate_sum,) = call(
        add_kernel,
        scalars,
        [gate_near_grad, gate_got],
        [shape(gate_near_grad.shape, LINK)],
        deps=[a_near_got, b_own_got, a_away, b_far],
    )
    grad_gate = scatter_high(gate_sum).astype(F32)
    own, *sends = call(
        functools.partial(last_kernel, rows),
        scalars,
        [
            mine[0],
            got[0],
            a_near_got,
            swap_row(a_away),
            mine[2],
            got[2],
            b_own_got,
            swap_far(b_far),
            sums_far + swap_row(sums_far),
        ],
        [shape((rows, 2 * cut + PAD), F32)] + [shape((rows, 2 * cut + PAD), LINK)] * (half - 1),
        scratch=[pltpu.VMEM((width, PAD), F32)],
        deps=[gate_sum],
    )
    gots = [shift_high(sends[s - 1], s) for s in range(1, half)]
    (out_far,) = add((after(out_x, own), swap_core(out_xc)))
    out_got, out_got_far = swap_core(out_c), swap_far(out_far)
    up_row = swap_row(after(up_other, own))
    grad_up = up_mine.astype(F32) + up_row.astype(F32)
    grad_in, grad_outw, one_grad, two_grad, taps_grad = call(
        final_kernel,
        scalars,
        [own, *gots],
        [
            shape((rows, in_cols), F32),
            shape((rows, out_cols), F32),
            shape((1, rows), F32),
            shape((1, rows), F32),
            shape((rows, 3), F32),
        ],
        deps=[grad_up, grad_gate, grad_down],
    )
    result = (
        hidden + (out_own.astype(F32) + out_got.astype(F32) + out_got_far.astype(F32))
    ).astype(LINK)
    return (
        result,
        input_grad,
        one_grad[0],
        grad_in,
        taps_grad,
        grad_outw,
        two_grad[0],
        grad_gate,
        grad_up,
        grad_down,
    )


def solution(mesh):
    rows_spec, cols_spec = P(("dp", "fsdp"), None), P("fsdp", "dp")
    gain_spec, taps_spec = P("fsdp"), P("fsdp", None)
    return jax.shard_map(
        body,
        mesh=mesh,
        in_specs=(
            rows_spec,
            rows_spec,
            gain_spec,
            cols_spec,
            taps_spec,
            cols_spec,
            gain_spec,
            cols_spec,
            cols_spec,
            cols_spec,
            rows_spec,
        ),
        out_specs=(
            rows_spec,
            rows_spec,
            gain_spec,
            cols_spec,
            taps_spec,
            cols_spec,
            gain_spec,
            cols_spec,
            cols_spec,
            cols_spec,
        ),
        check_vma=False,
    )
```

```python
import functools

import jax
import jax.numpy as jnp
from jax import lax
from jax.experimental import pallas as pl
from jax.experimental.pallas import tpu as pltpu
from jax.sharding import PartitionSpec as P

EPSILON = 1e-05
LINK = jnp.bfloat16
F32 = jnp.float32
PAD = 128
MIB = 1 << 20


def dot_plain(left, right):
    return jnp.dot(left, right, preferred_element_type=F32)


def dot_rows(left, right):
    return lax.dot_general(left, right, (((0,), (0,)), ((), ())), preferred_element_type=F32)


def dot_last(left, right):
    return lax.dot_general(left, right, (((1,), (1,)), ((), ())), preferred_element_type=F32)


def after(v, *others):
    return lax.optimization_barrier((v, *others))[0]


def shape(dims, dtype):
    return jax.ShapeDtypeStruct(dims, dtype)


SCALARS = pl.BlockSpec(memory_space=pltpu.SMEM)
WHOLE = pl.BlockSpec(memory_space=pltpu.VMEM)
APART = pl.BlockSpec(memory_space=pl.ANY)


def call(kernel, scalars, args, outs, flops=0, limit=40, scratch=(), apart=0, deps=()):
    moved = sum(a.size * a.dtype.itemsize for a in args) + sum(
        o.size * jnp.dtype(o.dtype).itemsize for o in outs
    )
    first, last = 1 + len(args), 1 + len(args) + len(deps)

    def run(*refs):
        kernel(*refs[:first], *refs[last:])

    return pl.pallas_call(
        run,
        out_shape=outs,
        in_specs=[SCALARS] + [WHOLE] * len(args) + [APART] * len(deps),
        out_specs=[WHOLE] * (len(outs) - apart) + [APART] * apart,
        scratch_shapes=list(scratch),
        compiler_params=pltpu.CompilerParams(vmem_limit_bytes=limit * MIB),
        cost_estimate=pl.CostEstimate(flops=flops, bytes_accessed=moved, transcendentals=0),
    )(scalars, *args, *deps)


def pack_kernel(where_ref, in_ref, out_ref, one_ref, two_ref, taps_ref, packed_ref):
    rows = in_ref.shape[0]
    in_half, out_half = in_ref.shape[1] // 2, out_ref.shape[1] // 2
    cut = in_half + out_half
    packed_ref[:, :in_half] = in_ref[:, :in_half]
    packed_ref[:, in_half:cut] = out_ref[:, :out_half]
    packed_ref[:, cut : cut + in_half] = in_ref[:, in_half:]
    packed_ref[:, cut + in_half : 2 * cut] = out_ref[:, out_half:]
    eye = lax.broadcasted_iota(jnp.int32, (rows, rows), 0) == lax.broadcasted_iota(
        jnp.int32, (rows, rows), 1
    )
    lane = lax.broadcasted_iota(jnp.int32, (rows, PAD), 1)
    small = jnp.zeros((rows, PAD), F32)
    for k, ref in enumerate((one_ref, two_ref)):
        column = jnp.sum(jnp.where(eye, ref[...].astype(F32), 0.0), axis=1, keepdims=True)
        small = jnp.where(lane == k, column, small)
    for k in range(3):
        small = jnp.where(lane == 2 + k, taps_ref[:, k : k + 1].astype(F32), small)
    packed_ref[:, 2 * cut :] = small.astype(LINK)


def merge_kernel(where_ref, *refs):
    pieces, (first_ref, second_ref, small_ref) = refs[:-3], refs[-3:]
    rows = pieces[0].shape[0]
    high = where_ref[2]
    cut = first_ref.shape[1]
    for s, piece in enumerate(pieces):
        spot = high - s
        spot = jnp.where(spot < 0, spot + len(pieces), spot)
        at = pl.ds(pl.multiple_of(spot * rows, rows), rows)
        first_ref[at, :] = piece[:, :cut]
        second_ref[at, :] = piece[:, cut : 2 * cut]
        small_ref[at, :] = piece[:, 2 * cut :]


def natural(low, near, away, put, rows, blocks):
    def one(h, carry):
        at = pl.ds(pl.multiple_of(h * rows, rows), rows)
        put(pl.ds(pl.multiple_of((2 * h + low) * rows, rows), rows), at, near)
        put(pl.ds(pl.multiple_of((2 * h + 1 - low) * rows, rows), rows), at, away)
        return carry

    lax.fori_loop(0, blocks, one, 0)


def mixer_weights_kernel(rows, where_ref, *refs):
    pieces, (in_ref, out_ref) = refs[:16], refs[16:18]
    low, place = where_ref[0], where_ref[1]
    in_half, out_half = in_ref.shape[1] // 8, out_ref.shape[1] // 8
    for k in range(8):
        half, r = k // 4, k % 4
        block = lax.bitwise_xor(place, r)
        in_at = pl.ds(pl.multiple_of((2 * block + half) * in_half, PAD), in_half)
        out_at = pl.ds(pl.multiple_of((2 * block + half) * out_half, PAD), out_half)

        def put(to, at, ref):
            in_ref[to, in_at] = ref[at, :in_half]
            out_ref[to, out_at] = ref[at, in_half:]

        natural(low, pieces[2 * k], pieces[2 * k + 1], put, rows, pieces[0].shape[0] // rows)


def back_rows(v, steps):
    return pltpu.roll(v, steps, 0)


def ahead_rows(v, steps):
    return pltpu.roll(v, v.shape[0] - steps, 0)


def small_rows(rows, low, near_ref, away_ref, small_ref):
    def put(to, at, ref):
        small_ref[to, :] = ref[at, :].astype(F32)

    natural(low, near_ref, away_ref, put, rows, near_ref.shape[0] // rows)
    return small_ref[...].T[:8]


def mixer_kernel(
    rows,
    where_ref,
    tokens_ref,
    same_ref,
    near_ref,
    away_ref,
    *refs,
):
    pieces = refs[:16]
    normed_ref, parts_ref, scaled_ref, hidden_ref, next_ref, gains_ref = refs[16:22]
    small_ref, in_ref, outw_ref, in_sem, outw_sem = refs[24:]
    mixer_weights_kernel(rows, where_ref, *pieces, in_ref, outw_ref)
    in_copy = pltpu.make_async_copy(in_ref, refs[22], in_sem)
    outw_copy = pltpu.make_async_copy(outw_ref, refs[23], outw_sem)
    in_copy.start()
    outw_copy.start()
    width = tokens_ref.shape[1]
    step = 256
    gains_ref[...] = small_rows(rows, where_ref[0], near_ref, away_ref, small_ref)
    inputs = tokens_ref[...].astype(F32)
    inverse = lax.rsqrt(jnp.mean(inputs * inputs, axis=1, keepdims=True) + EPSILON)
    normed_ref[...] = (inputs * inverse * gains_ref[0:1, :]).astype(LINK)

    def chunk(q, carry):
        at = pl.ds(q * step, step)

        def part(k):
            w = in_ref[:, pl.ds(k * width + q * step, step)]
            v = dot_plain(normed_ref[...], w)
            parts_ref[k, :, at] = v
            return v

        b_part = part(0)
        x_part = part(2)
        gated = b_part * x_part
        mixed = (
            gains_ref[2:3, at] * gated
            + gains_ref[3:4, at] * (back_rows(gated, 1) * same_ref[:, 0:1])
            + gains_ref[4:5, at] * (back_rows(gated, 2) * same_ref[:, 1:2])
        )
        scaled_ref[:, at] = (part(1) * mixed).astype(LINK)
        return carry

    for q in range(width // step):
        chunk(q, 0)

    def final(q, total):
        at = pl.ds(q * step, step)
        v = tokens_ref[:, at].astype(F32) + dot_last(scaled_ref[...], outw_ref[at, :])
        hidden_ref[:, at] = v
        return total + jnp.sum(v * v, axis=1, keepdims=True)

    total = jnp.zeros((tokens_ref.shape[0], 1), F32)
    for q in range(width // step):
        total = final(q, total)
    inverse_two = lax.rsqrt(total / width + EPSILON)
    next_ref[...] = (hidden_ref[...] * inverse_two * gains_ref[1:2, :]).astype(LINK)
    in_copy.wait()
    outw_copy.wait()


def mixer_back_kernel(
    where_ref,
    own_ref,
    got_ref,
    far_one_ref,
    far_two_ref,
    hidden_ref,
    cot_ref,
    same_ref,
    gains_ref,
    parts_ref,
    outw_ref,
    hidden_grad_ref,
    branch_ref,
    proj_ref,
    sums_ref,
):
    width = hidden_ref.shape[1]
    step = 256
    hidden = hidden_ref[...]
    inverse = lax.rsqrt(jnp.mean(hidden * hidden, axis=1, keepdims=True) + EPSILON)
    far = jnp.concatenate([far_one_ref[...], far_two_ref[...]], axis=0)
    grad = own_ref[...].astype(F32) + got_ref[...].astype(F32) + far.astype(F32)
    sums_ref[0:1, :] = jnp.zeros((1, width), F32)
    sums_ref[1:2, :] = jnp.sum(grad * (hidden * inverse), axis=0, keepdims=True)
    weighted = grad * gains_ref[1:2, :]
    mean = jnp.mean(weighted * hidden, axis=1, keepdims=True)
    total = cot_ref[...].astype(F32) + inverse * (weighted - hidden * (inverse * inverse * mean))
    hidden_grad_ref[...] = total
    branch_ref[...] = total.astype(LINK)

    def chunk(q, carry):
        at = pl.ds(q * step, step)
        grad_scaled = dot_plain(branch_ref[...], outw_ref[:, at])
        b_part, c_part, x_part = (parts_ref[k, :, at] for k in range(3))
        same_one, same_two = same_ref[:, 0:1], same_ref[:, 1:2]
        gated = b_part * x_part
        back_one = back_rows(gated, 1) * same_one
        back_two = back_rows(gated, 2) * same_two
        taps = [gains_ref[2 + k : 3 + k, at] for k in range(3)]
        mixed = taps[0] * gated + taps[1] * back_one + taps[2] * back_two
        grad_mixed = grad_scaled * c_part
        sums_ref[2:3, at] = jnp.sum(grad_mixed * gated, axis=0, keepdims=True)
        sums_ref[3:4, at] = jnp.sum(grad_mixed * back_one, axis=0, keepdims=True)
        sums_ref[4:5, at] = jnp.sum(grad_mixed * back_two, axis=0, keepdims=True)
        grad_gated = (
            taps[0] * grad_mixed
            + taps[1] * ahead_rows(grad_mixed * same_one, 1)
            + taps[2] * ahead_rows(grad_mixed * same_two, 2)
        )
        for k, v in enumerate((grad_gated * x_part, grad_scaled * mixed, grad_gated * b_part)):
            proj_ref[:, pl.ds(k * width + q * step, step)] = v.astype(LINK)
        return carry

    for q in range(width // step):
        chunk(q, 0)
    sums_ref[5:8, :] = jnp.zeros((3, width), F32)


def mixer_grads_kernel(
    rows, order, where_ref, normed_ref, proj_ref, branch_ref, scaled_ref, *refs
):
    low, place = where_ref[0], where_ref[1]
    outs, (total_ref, held_ref, sems) = refs[:8], refs[8:]
    in_half = proj_ref.shape[1] // 8
    out_half = scaled_ref.shape[1] // 8
    for n in range(4):
        i, half = n // 2, n % 2
        block = 2 * lax.bitwise_xor(place, order[i]) + half
        in_at = pl.ds(pl.multiple_of(block * in_half, PAD), in_half)
        out_at = pl.ds(pl.multiple_of(block * out_half, PAD), out_half)
        total_ref[:, :in_half] = dot_rows(normed_ref[...], proj_ref[:, in_at])
        total_ref[:, in_half:] = dot_rows(branch_ref[...], scaled_ref[:, out_at])

        def copy(h, carry, n=n):
            to = pl.ds(pl.multiple_of(h * rows, rows), rows)
            for k, bit in enumerate((low, 1 - low)):
                at = pl.ds(pl.multiple_of((2 * h + bit) * rows, rows), rows)
                held_ref[2 * n + k, to, :] = total_ref[at, :].astype(LINK)
            return carry

        lax.fori_loop(0, held_ref.shape[1] // rows, copy, 0)
        for k in (2 * n, 2 * n + 1):
            pltpu.make_async_copy(held_ref.at[k], outs[k], sems.at[k]).start()
    for k in range(8):
        pltpu.make_async_copy(held_ref.at[k], outs[k], sems.at[k]).wait()


def final_kernel(where_ref, own_ref, *refs):
    gots, (in_ref, outw_ref, one_ref, two_ref, taps_ref) = refs[:-5], refs[-5:]
    in_half, out_half = in_ref.shape[1] // 2, outw_ref.shape[1] // 2
    cut = in_half + out_half

    def total(start, size):
        v = own_ref[:, start : start + size]
        for ref in gots:
            v = v + ref[:, start : start + size].astype(F32)
        return v

    for k in range(2):
        in_ref[:, k * in_half : (k + 1) * in_half] = total(k * cut, in_half)
        outw_ref[:, k * out_half : (k + 1) * out_half] = total(k * cut + in_half, out_half)
    small = total(2 * cut, PAD)
    turned = small.T
    one_ref[...] = turned[0:1]
    two_ref[...] = turned[1:2]
    taps_ref[...] = small[:, 2:5]


def join_kernel(where_ref, *refs):
    a, b, c = (r[...].astype(F32) for r in refs[:3])
    refs[3][...] = (a + b + c).astype(LINK)


def add_kernel(where_ref, *refs):
    n = len(refs) // 3
    for a, b, c in zip(refs[:n], refs[n : 2 * n], refs[2 * n :]):
        c[...] = (a[...].astype(F32) + b[...].astype(F32)).astype(c.dtype)


def last_kernel(
    rows, where_ref, a_ref, a_got_ref, a_far_ref, a_row_ref, b_ref, b_got_ref, b_row_ref, b_far_ref, small_ref, *refs
):
    low, high = where_ref[0], where_ref[2]
    cut = a_ref.shape[1]
    own_ref, sends, turned_ref = refs[0], refs[1:-1], refs[-1]
    width = turned_ref.shape[0]
    turned_ref[...] = jnp.concatenate(
        [small_ref[...], jnp.zeros((PAD - 8, width), F32)], axis=0
    ).T

    def total(at, *parts):
        v = parts[0][at, :].astype(F32)
        for p in parts[1:]:
            v = v + p[at, :].astype(F32)
        return v

    for s, ref in enumerate((own_ref, *sends)):
        spot = high + s
        spot = jnp.where(spot >= len(sends) + 1, spot - len(sends) - 1, spot)
        at = pl.ds(pl.multiple_of(spot * rows, rows), rows)
        ref[:, :cut] = total(at, a_ref, a_got_ref, a_far_ref, a_row_ref).astype(ref.dtype)
        ref[:, cut : 2 * cut] = total(at, b_ref, b_got_ref, b_row_ref, b_far_ref).astype(ref.dtype)
        at = pl.ds(pl.multiple_of((2 * spot + low) * rows, rows), rows)
        ref[:, 2 * cut :] = turned_ref[at, :].astype(ref.dtype)


def mixer_input_kernel(
    rows,
    where_ref,
    tokens_ref,
    hidden_grad_ref,
    gains_ref,
    sums_ref,
    proj_ref,
    in_ref,
    input_ref,
    small_ref,
    grad_ref,
):
    width = tokens_ref.shape[1]
    step = 256
    inputs = tokens_ref[...].astype(F32)
    inverse = lax.rsqrt(jnp.mean(inputs * inputs, axis=1, keepdims=True) + EPSILON)

    def chunk(q, carry):
        at = pl.ds(q * step, step)
        grad_ref[:, at] = dot_last(proj_ref[...], in_ref[at, :])
        return carry

    for q in range(width // step):
        chunk(q, 0)
    grad = grad_ref[...]
    row = lax.broadcasted_iota(jnp.int32, (8, width), 0)
    gain_grad = jnp.sum(grad * (inputs * inverse), axis=0, keepdims=True)
    small_ref[...] = jnp.where(row == 0, gain_grad, sums_ref[...])
    weighted = grad * gains_ref[0:1, :]
    mean = jnp.mean(weighted * inputs, axis=1, keepdims=True)
    input_ref[...] = hidden_grad_ref[...] + inverse * (
        weighted - inputs * (inverse * inverse * mean)
    )


TILE = 256


def piece_specs(pieces, count, width, tile=TILE):
    tiles = count // tile
    return [
        pl.BlockSpec(
            (tile, width), lambda t, k=k: (jnp.clip(t - k * tiles, 0, tiles - 1), 0)
        )
        for k in range(pieces)
    ]


def pick(refs, tiles):
    v = refs[0][...]
    for k in range(1, len(refs)):
        v = jnp.where(pl.program_id(0) >= k * tiles, refs[k][...], v)
    return v


def put_piece(refs, tiles, v):
    for k, ref in enumerate(refs):

        @pl.when((pl.program_id(0) >= k * tiles) & (pl.program_id(0) < (k + 1) * tiles))
        def _(ref=ref):
            ref[...] = v.astype(ref.dtype)


def whole_spec(v):
    return pl.BlockSpec(v.shape, lambda t: (0, 0))


def tiled(kernel, grid, in_specs, args, out_specs, outs, flops, limit=56, scratch=()):
    moved = sum(a.size * a.dtype.itemsize for a in args) + sum(
        o.size * jnp.dtype(o.dtype).itemsize for o in outs
    )
    return pl.pallas_call(
        kernel,
        grid=(grid,),
        in_specs=in_specs,
        out_specs=out_specs,
        out_shape=outs,
        scratch_shapes=list(scratch),
        compiler_params=pltpu.CompilerParams(vmem_limit_bytes=limit * MIB),
        cost_estimate=pl.CostEstimate(flops=flops, bytes_accessed=moved, transcendentals=0),
    )(*args)


def act_kernel(tiles, rows, where_ref, *refs):
    pieces, woven, (act_ref, silu_ref, slope_ref, gate_ref, up_ref) = refs[:4], refs[4:8], refs[8:]

    @pl.when(pl.program_id(0) == 0)
    def _():
        for k, whole_ref in enumerate((gate_ref, up_ref)):

            def put(to, at, ref, whole_ref=whole_ref):
                whole_ref[to, :] = ref[at, :]

            natural(where_ref[0], *woven[2 * k : 2 * k + 2], put, rows, woven[0].shape[0] // rows)

    normed = pick(pieces, tiles)
    gate = dot_plain(normed, gate_ref[...])
    up = dot_plain(normed, up_ref[...])
    sigmoid = 1.0 / (1.0 + jnp.exp(-gate))
    silu = gate * sigmoid
    act_ref[...] = (silu * up).astype(LINK)
    silu_ref[...] = silu.astype(LINK)
    slope_ref[...] = (up * (sigmoid + silu * (1.0 - sigmoid))).astype(LINK)


def act_call(rows, scalars, pieces, woven):
    count, width = pieces[0].shape
    inner = woven[0].shape[1]
    tile = count
    tiles = count // tile
    wide = pl.BlockSpec((tile, inner), lambda t: (t, 0))
    weight = shape((width, inner), LINK)
    return tiled(
        functools.partial(act_kernel, tiles, rows),
        4 * tiles,
        [SCALARS] + piece_specs(4, count, width, tile) + [whole_spec(v) for v in woven],
        [scalars, *pieces, *woven],
        [wide] * 3 + [whole_spec(weight)] * 2,
        [shape((4 * count, inner), LINK)] * 3 + [weight] * 2,
        16 * count * width * inner,
    )


def back_kernel(pieces, tiles, with_got, *refs):
    cots, refs = refs[:pieces], refs[pieces:]
    silu_ref, slope_ref, gate_ref, up_ref, down_ref = refs[:5]
    refs = refs[5:]
    if with_got:
        got_ref, refs = refs[0], refs[1:]
    grad_gate_ref, grad_up_ref = refs[:2]
    grad_act = dot_plain(pick(cots, tiles), down_ref[...])
    grad_up_ref[...] = (grad_act * silu_ref[...].astype(F32)).astype(LINK)
    grad_gate_ref[...] = (grad_act * slope_ref[...].astype(F32)).astype(LINK)
    back = dot_last(grad_gate_ref[...], gate_ref[...]) + dot_last(grad_up_ref[...], up_ref[...])
    if with_got:
        back = back + got_ref[...].astype(F32)
    put_piece(refs[2:], tiles, back)


def back_call(start, cots, silu, slope, gate, up, down, got=None):
    count, width = cots[0].shape
    inner = gate.shape[1]
    tiles, pieces = count // TILE, len(cots)
    wide_in = pl.BlockSpec((TILE, inner), lambda t: (t + start * tiles, 0))
    wide = pl.BlockSpec((TILE, inner), lambda t: (t, 0))
    thin = piece_specs(pieces, count, width)
    extra = [] if got is None else [got]
    return tiled(
        functools.partial(back_kernel, pieces, tiles, got is not None),
        pieces * tiles,
        thin + [wide_in] * 2 + [whole_spec(gate)] * 3 + thin[: len(extra)],
        [*cots, silu, slope, gate, up, down, *extra],
        [wide] * 2 + thin,
        [shape((pieces * count, inner), LINK)] * 2 + [shape((count, width), LINK)] * pieces,
        6 * pieces * count * width * inner,
    )


def out_kernel(tiles, skip, act_ref, down_ref, *refs):
    put_piece(refs[skip:], tiles, dot_last(act_ref[...], down_ref[...]))


def out_call(act, down, count, deps):
    width, inner = down.shape
    tiles = count // TILE
    return tiled(
        functools.partial(out_kernel, tiles, len(deps)),
        4 * tiles,
        [pl.BlockSpec((TILE, inner), lambda t: (t, 0)), whole_spec(down)] + [APART] * len(deps),
        [act, down, *deps],
        piece_specs(4, count, width),
        [shape((count, width), LINK)] * 4,
        8 * count * width * inner,
    )


def weight_grad_kernel(rows, spots, whole, where_ref, *refs):
    lefts, refs = refs[:4], refs[4:]
    low = where_ref[0]
    count = lefts[0].shape[0]
    at = pl.ds(pl.multiple_of(pl.program_id(0) * TILE, TILE), TILE)
    total = None
    for left, (k, start) in zip(lefts, spots):
        v = dot_rows(left[:, at], refs[k][start * count : (start + 1) * count, :])
        total = v if total is None else total + v
    if whole:
        refs[-1][...] = total.astype(LINK)
        return
    near_ref, away_ref, total_ref = refs[-3:]
    total_ref[...] = total
    for h in range(near_ref.shape[0] // rows):
        to = pl.ds(h * rows, rows)
        for ref, bit in ((near_ref, low), (away_ref, 1 - low)):
            at = pl.ds(pl.multiple_of((2 * h + bit) * rows, rows), rows)
            ref[to, :] = total_ref[at, :].astype(ref.dtype)


def pair_grad_kernel(rows, spots, where_ref, *refs):
    lefts, gates, ups = refs[:4], refs[4:7], refs[7:10]
    near_ref, away_ref, up_ref, total_ref = refs[10:]
    low = where_ref[0]
    count = lefts[0].shape[0]
    at = pl.ds(pl.multiple_of(pl.program_id(0) * TILE, TILE), TILE)

    def total(rights):
        v = None
        for left, (k, start) in zip(lefts, spots):
            part = dot_rows(left[:, at], rights[k][start * count : (start + 1) * count, :])
            v = part if v is None else v + part
        return v

    up_ref[...] = total(ups).astype(LINK)
    total_ref[...] = total(gates)
    for h in range(near_ref.shape[0] // rows):
        to = pl.ds(h * rows, rows)
        for ref, bit in ((near_ref, low), (away_ref, 1 - low)):
            at_rows = pl.ds(pl.multiple_of((2 * h + bit) * rows, rows), rows)
            ref[to, :] = total_ref[at_rows, :].astype(ref.dtype)


def pair_grad(rows, scalars, lefts, gates, ups, spots):
    count, width = lefts[0].shape
    inner = gates[0].shape[1]
    half = pl.BlockSpec((TILE // 2, inner), lambda t: (t, 0))
    args = [*lefts, *gates, *ups]
    return tiled(
        functools.partial(pair_grad_kernel, rows, spots),
        width // TILE,
        [SCALARS] + [whole_spec(v) for v in args],
        [scalars, *args],
        [half, half, pl.BlockSpec((TILE, inner), lambda t: (t, 0))],
        [
            shape((width // 2, inner), F32),
            shape((width // 2, inner), LINK),
            shape((width, inner), LINK),
        ],
        16 * count * width * inner,
        scratch=[pltpu.VMEM((TILE, inner), F32)],
    )


def weight_grad(rows, scalars, lefts, rights, spots, whole=False):
    count, width = lefts[0].shape
    inner = rights[0].shape[1]
    half = pl.BlockSpec((TILE // 2, inner), lambda t: (t, 0))
    return tiled(
        functools.partial(weight_grad_kernel, rows, spots, whole),
        width // TILE,
        [SCALARS] + [whole_spec(v) for v in (*lefts, *rights)],
        [scalars, *lefts, *rights],
        [pl.BlockSpec((TILE, inner), lambda t: (t, 0))] if whole else [half, half],
        [shape((width, inner), LINK)]
        if whole
        else [shape((width // 2, inner), F32), shape((width // 2, inner), LINK)],
        8 * count * width * inner,
        scratch=[] if whole else [pltpu.VMEM((TILE, inner), F32)],
    )


def body(
    tokens,
    segments,
    mixer_gain,
    in_weight,
    conv_kernel,
    out_weight,
    ffn_gain,
    gate_weight,
    up_weight,
    down_weight,
    cotangent,
):
    count, width = tokens.shape
    rows = in_weight.shape[0]
    in_cols, out_cols = in_weight.shape[1], out_weight.shape[1]
    cut = (in_cols + out_cols) // 2
    ways = width // rows
    half = ways // 2
    columns = lax.axis_size("dp")
    place = lax.axis_index("dp")
    low = lax.rem(lax.axis_index("fsdp"), 2)
    high = lax.axis_index("fsdp") // 2
    scalars = jnp.stack([low, place, high]).astype(jnp.int32)
    strides = [[2 * h + bit for h in range(half)] for bit in range(2)]

    def swap_row(v):
        return lax.ppermute(v, "fsdp", [(i, i ^ 1) for i in range(ways)])

    def swap_far(v):
        return lax.ppermute(v, "dp", [(i, i ^ 2) for i in range(columns)])

    def swap_core(v):
        return lax.ppermute(v, "dp", [(i, i ^ 1) for i in range(columns)])

    def shift_high(v, s):
        return lax.ppermute(v, "fsdp", [(i, (i + 2 * s) % ways) for i in range(ways)])

    def gather_high(v):
        return lax.all_gather(v, "fsdp", axis=0, tiled=True, axis_index_groups=strides)

    def scatter_high(v):
        return lax.psum_scatter(
            v, "fsdp", scatter_dimension=0, tiled=True, axis_index_groups=strides
        )

    (packed,) = call(
        pack_kernel,
        scalars,
        [in_weight, out_weight, mixer_gain[None, :], ffn_gain[None, :], conv_kernel],
        [shape((rows, 2 * cut + PAD), LINK)],
    )
    shifts = [packed] + [shift_high(packed, s) for s in range(1, half)]
    tall = half * rows
    down_other = swap_row(after(down_weight, packed))
    down_pair = jnp.where(
        low == 0,
        jnp.concatenate([down_weight, down_other], axis=0),
        jnp.concatenate([down_other, down_weight], axis=0),
    )
    shifts[0] = after(shifts[0], down_pair)
    first, second, small_near = call(
        merge_kernel,
        scalars,
        shifts,
        [shape((tall, cut), LINK), shape((tall, cut), LINK), shape((tall, PAD), LINK)],
    )
    gate_near = gather_high(after(gate_weight, first))
    up_near = gather_high(after(up_weight, first))
    down_all = gather_high(after(down_pair, first))
    first_row = swap_row(first)
    second_far = swap_far(second)
    small_away = swap_row(small_near)
    second_row = swap_row(second)
    first_far = swap_far(first)
    second_far_row = swap_row(second_far)
    first_row_far = swap_far(first_row)
    cot_far = swap_far(after(cotangent, first_row_far))
    chip = [[[first, first_row], [first_far, first_row_far]], [[second, second_row], [second_far, second_far_row]]]
    pieces = []
    for k in range(2):
        other = [[swap_core(v) for v in pair] for pair in chip[k]]
        for pair in (chip[k][0], other[0], chip[k][1], other[1]):
            pieces += pair
    pieces[0] = after(pieces[0], gate_near, small_away)
    gate_row = swap_row(gate_near)
    up_row = swap_row(up_near)

    def gather_tokens(v, far):
        return [v, swap_core(v), far, swap_core(far)]

    cots = gather_tokens(cotangent, cot_far)

    seg_ids = segments[0]
    zero = jnp.zeros((2,), F32)
    same = jnp.stack(
        [
            jnp.concatenate([zero[:1], (seg_ids[1:] == seg_ids[:-1]).astype(F32)]),
            jnp.concatenate([zero, (seg_ids[2:] == seg_ids[:-2]).astype(F32)]),
        ],
        axis=1,
    )
    normed, parts, scaled, hidden, normed_two, gains, in_all, outw_all = call(
        functools.partial(mixer_kernel, rows),
        scalars,
        [tokens, same, small_near, small_away, *pieces],
        [
            shape((count, width), LINK),
            shape((3, count, width), F32),
            shape((count, width), LINK),
            shape((count, width), F32),
            shape((count, width), LINK),
            shape((8, width), F32),
            shape((width, columns * in_cols), LINK),
            shape((width, columns * out_cols), LINK),
        ],
        apart=2,
        flops=8 * count * width * width,
        scratch=[
            pltpu.VMEM((width, PAD), F32),
            pltpu.VMEM((width, columns * in_cols), LINK),
            pltpu.VMEM((width, columns * out_cols), LINK),
            pltpu.SemaphoreType.DMA,
            pltpu.SemaphoreType.DMA,
        ],
        limit=56,
    )

    normed_two = after(normed_two, up_near, cot_far, gate_row)
    normeds = gather_tokens(normed_two, swap_far(normed_two))
    act, silu, slope, gate_all, up_all = act_call(
        rows, scalars, normeds, [gate_near, gate_row, up_near, up_row]
    )

    def add(*pairs):
        return call(
            add_kernel,
            scalars,
            [p[0] for p in pairs] + [p[1] for p in pairs],
            [shape(p[0].shape, LINK) for p in pairs],
        )

    def join(near, away_got):
        return call(add_kernel, scalars, [near, away_got], [shape(near.shape, LINK)])[0]

    weights = (silu, slope, gate_all, up_all, down_all)
    gate_xc, up_xc, back_xc = back_call(3, [cots[3]], *weights)
    down_near, down_away = weight_grad(
        rows,
        scalars,
        [after(cots[0], back_xc), *cots[1:]],
        [act],
        [(0, 0), (0, 1), (0, 2), (0, 3)],
    )
    gate_x, up_x, back_far = back_call(
        2, [after(cots[2], down_away)], *weights, got=swap_core(back_xc)
    )
    gate_o, up_o, back_own, back_c = back_call(
        0, [after(cots[0], back_far), cots[1]], *weights
    )
    down_got = swap_row(down_away)
    back_one = swap_far(back_far[: 3 * count // 4])
    back_two = swap_far(back_far[3 * count // 4 :])
    spots = [(0, 0), (0, 1), (1, 0), (2, 0)]
    down_sum = join(down_near, down_got)
    gate_near_grad, gate_away, up_whole = pair_grad(
        rows,
        scalars,
        [after(normeds[0], down_sum, back_one), *normeds[1:]],
        [gate_o, gate_x, gate_xc],
        [up_o, up_x, up_xc],
        spots,
    )
    up_pair = scatter_high(up_whole).reshape(2, rows, -1)
    up_mine = jnp.where(low == 0, up_pair[0], up_pair[1])
    up_other = jnp.where(low == 0, up_pair[1], up_pair[0])
    grad_down = scatter_high(down_sum).astype(F32)
    gate_one = swap_row(gate_away[: tall // 2])
    gate_two = swap_row(gate_away[tall // 2 :])

    hidden_grad, branch, proj, sums = call(
        mixer_back_kernel,
        scalars,
        [after(back_own, gate_away), swap_core(back_c), back_one, back_two, hidden, cotangent, same, gains, parts, outw_all],
        [
            shape((count, width), F32),
            shape((count, width), LINK),
            shape((count, 3 * width), LINK),
            shape((8, width), F32),
        ],
        flops=2 * count * width * width,
        limit=48,
    )

    def mixer_grads(order, first_arg):
        return call(
            functools.partial(mixer_grads_kernel, rows, order),
            scalars,
            [first_arg, proj, branch, scaled],
            [shape((tall, cut), LINK)] * 8,
            flops=4 * count * width * width,
            scratch=[
                pltpu.VMEM((width, cut), F32),
                pltpu.VMEM((8, tall, cut), LINK),
                pltpu.SemaphoreType.DMA((8,)),
            ],
            apart=8,
        )

    input_grad, sums = call(
        functools.partial(mixer_input_kernel, rows),
        scalars,
        [tokens, hidden_grad, gains, sums, proj, in_all],
        [shape((count, width), F32), shape((8, width), F32)],
        flops=6 * count * width * width,
        scratch=[pltpu.VMEM((count, width), F32)],
    )
    sums_core = sums + swap_core(sums)
    sums_far = sums_core + swap_far(sums_core)
    send = mixer_grads((1, 3), after(normed, gate_one, input_grad))
    got = [swap_core(v) for v in send]
    mine = mixer_grads((0, 2), after(normed, send[0], sums_core))
    mine = [*mine[:5], after(mine[5], sums_far), *mine[6:]]
    a_away_far, b_away_far, a_near_far, b_away_own = add(
        *((after(mine[k], gate_two), got[k]) for k in (5, 7, 4, 3))
    )
    a_away_got = swap_far(a_away_far)
    b_away_got = swap_row(b_away_far)
    a_near_got = swap_far(a_near_far)
    b_own_got = swap_row(b_away_own)

    out_own, out_c, out_x, out_xc = out_call(after(act, a_near_far), down_all, count, [up_pair])
    (a_away,), (b_far,) = (
        call(join_kernel, scalars, parts, [shape((tall, cut), LINK)], deps=[out_own])
        for parts in ([mine[1], got[1], a_away_got], [mine[6], got[6], b_away_got])
    )
    gate_got = jnp.concatenate([gate_one, gate_two], axis=0)
    (gate_sum,) = call(
        add_kernel,
        scalars,
        [gate_near_grad, gate_got],
        [shape(gate_near_grad.shape, LINK)],
        deps=[a_near_got, b_own_got, a_away, b_far],
    )
    grad_gate = scatter_high(gate_sum).astype(F32)
    own, *sends = call(
        functools.partial(last_kernel, rows),
        scalars,
        [
            mine[0],
            got[0],
            a_near_got,
            swap_row(a_away),
            mine[2],
            got[2],
            b_own_got,
            swap_far(b_far),
            sums_far + swap_row(sums_far),
        ],
        [shape((rows, 2 * cut + PAD), F32)] + [shape((rows, 2 * cut + PAD), LINK)] * (half - 1),
        scratch=[pltpu.VMEM((width, PAD), F32)],
        deps=[gate_sum],
    )
    gots = [shift_high(sends[s - 1], s) for s in range(1, half)]
    (out_far,) = add((after(out_x, own), swap_core(out_xc)))
    out_got, out_got_far = swap_core(out_c), swap_far(out_far)
    up_row = swap_row(after(up_other, own))
    grad_up = up_mine.astype(F32) + up_row.astype(F32)
    grad_in, grad_outw, one_grad, two_grad, taps_grad = call(
        final_kernel,
        scalars,
        [own, *gots],
        [
            shape((rows, in_cols), F32),
            shape((rows, out_cols), F32),
            shape((1, rows), F32),
            shape((1, rows), F32),
            shape((rows, 3), F32),
        ],
        deps=[grad_up, grad_gate, grad_down],
    )
    result = (
        hidden + (out_own.astype(F32) + out_got.astype(F32) + out_got_far.astype(F32))
    ).astype(LINK)
    return (
        result,
        input_grad,
        one_grad[0],
        grad_in,
        taps_grad,
        grad_outw,
        two_grad[0],
        grad_gate,
        grad_up,
        grad_down,
    )


def solution(mesh):
    rows_spec, cols_spec = P(("dp", "fsdp"), None), P("fsdp", "dp")
    gain_spec, taps_spec = P("fsdp"), P("fsdp", None)
    return jax.shard_map(
        body,
        mesh=mesh,
        in_specs=(
            rows_spec,
            rows_spec,
            gain_spec,
            cols_spec,
            taps_spec,
            cols_spec,
            gain_spec,
            cols_spec,
            cols_spec,
            cols_spec,
            rows_spec,
        ),
        out_specs=(
            rows_spec,
            rows_spec,
            gain_spec,
            cols_spec,
            taps_spec,
            cols_spec,
            gain_spec,
            cols_spec,
            cols_spec,
            cols_spec,
        ),
        check_vma=False,
    )
```
